32 devices in a mesh: seq: 8 (over z, x), head: 4 (over y, core).
Axes of the slice: x: 2, y: 2, z: 4, core: 2. Of those that a mesh axis runs over, the one named last changes fastest.
Arguments:
- history: bfloat16 [6144, 1024], P('seq'), may hold values from -6 to 6
- ln_gain: bfloat16 [1024], replicated, may hold values from 0.5 to 1.5
- w_in: bfloat16 [4, 1024, 1024], P(None, None, 'head'), may hold values from -0.1875 to 0.1875
- out_gain: bfloat16 [1024], P('head'), may hold values from 0.5 to 1.5
- w_out: bfloat16 [1024, 1024], P('head'), may hold values from -0.25 to 0.25
- block_lists: int32 [48, 16], P('seq'), may hold values from 0 to 47, as said below
- counts: int32 [48], P('seq'), may hold values from 1 to 16, as said below
Outputs:
- mixed: bfloat16 [6144, 1024], P('seq', 'head')
The draws below stay inside these ranges and needn't reach their ends.
Inputs may be any that keep to these rules, and one draw needn't show every extreme that they name: For query block b, entries 0 to counts[b] - 1 of block_lists[b] are distinct blocks from max(0, b - 31) to b, and entry 0 is b itself; later entries equal b and are not live. counts[b] is at most min(16, b + 1); the last block has min(16, 32, 48) live entries.
All inputs are finite; a program needn't handle non-finite values.
Results may differ from the reference program's by a relative error of at most 0.008.
Values may be sent and summed in bfloat16 or wider, within the bound.
No kernel may reach another device: no remote copies, remote signals or barrier semaphores. Data moves between devices by JAX's collectives and lax.ppermute only.
A program may use at most 64 MiB of HBM per device.

```python
import jax
import jax.numpy as jnp
from jax import lax

D = 1024
H = 8
DH = 128
BLK = 128
WIN = 32
MAXK = 16
TOK_DEV = 768
NBLK = 48
L = 6144


def pattern(key):
    base = jax.random.fold_in(key, 11)
    key_level, key_count, key_order = jax.random.split(base, 3)
    blocks_dev = TOK_DEV // BLK
    devices_seq = NBLK // blocks_dev
    block_ids = jnp.arange(NBLK, dtype=jnp.int32)
    window_avail = jnp.minimum(WIN, block_ids + 1)
    levels = jax.random.randint(key_level, (devices_seq,), MAXK // 2, MAXK + 1)
    level_rows = levels[block_ids // blocks_dev]
    counted = jax.random.randint(key_count, (NBLK,), (level_rows + 1) // 2, level_rows + 1)
    counted = jnp.minimum(counted, window_avail)
    counted = jnp.where(block_ids == NBLK - 1, jnp.minimum(MAXK, window_avail), counted)
    offsets = jnp.arange(1, WIN, dtype=jnp.int32)
    scores = jax.random.randint(key_order, (NBLK, WIN - 1), 0, 1 << 20) * WIN + offsets[None, :]
    scores = jnp.where(offsets[None, :] < window_avail[:, None], scores, scores + (1 << 26))
    order = jnp.argsort(scores, axis=1, stable=True)[:, :MAXK - 1].astype(jnp.int32) + 1
    picked = block_ids[:, None] - order
    slot_ids = jnp.arange(1, MAXK, dtype=jnp.int32)
    picked = jnp.where(slot_ids[None, :] < counted[:, None], picked, block_ids[:, None])
    listed = jnp.concatenate([block_ids[:, None], picked], axis=1)
    return (listed.astype(jnp.int32), counted.astype(jnp.int32))


def draw_block_lists(key, part):
    return pattern(key)[0]


def draw_counts(key, part):
    return pattern(key)[1]


def spiked(result, own_key, source, target, blocks, factor):
    owner, partner = [(jnp.arange(result.shape[axis_at]) // (result.shape[axis_at] // blocks)).reshape([-1 if axis == axis_at else 1 for axis in range(result.ndim)]) for axis_at in (source, target)]
    chosen = jax.random.permutation(own_key, blocks)[partner]
    strong = (owner == chosen) | (owner == (partner + blocks // 2) % blocks)
    return jnp.where(strong, factor * result, result)


def shard_levels(stream_key, dims, cuts, least, largest):
    factor_of, own = 1.0, jax.random.fold_in(stream_key, 6)
    for dim, blocks in cuts:
        draws = jnp.exp(jax.random.uniform(jax.random.fold_in(own, dim), (blocks,), jnp.float32, least / len(cuts), largest / len(cuts)))
        factor_of = factor_of * jnp.repeat(draws, dims[dim] // blocks).reshape([-1 if axis == dim else 1 for axis in range(len(dims))])
    return factor_of


def bell_draw(own_key, shape, scale, most, shards=(), held_as=jnp.bfloat16):
    drawn = jax.random.normal(own_key, shape, jnp.float32) * scale
    if len(shards) > 0:
        drawn = shard_levels(own_key, shape, shards, -0.22, 0.18) * drawn
    return jnp.clip(drawn, min=-most, max=most).astype(held_as)


def gaussian_with(rng, dims, spread, reach, cuts, heavy, kind=jnp.bfloat16):
    entries = spread * jax.random.normal(rng, dims, jnp.float32)
    if cuts:
        entries = entries * shard_levels(rng, dims, cuts, -0.22, 0.18)
    return jnp.clip(spiked(entries, jax.random.fold_in(rng, 3), *heavy), -reach, reach).astype(kind)


def setup_inputs(seed: int = 0) -> dict:
    key_of = jax.random.split(jax.random.key(seed), 8)
    history = bell_draw(key_of[0], (L, D), 1.0, 6.0, ((0, 8),))
    ln_gain = jnp.clip(jax.random.uniform(key_of[1], (D,), jnp.float32, 0.5, 1.5), 0.5, 1.5).astype(jnp.bfloat16)
    w_in = bell_draw(key_of[2], (4, D, H * DH), D ** -0.5, 0.1875, ((2, 4),))
    out_gain = jnp.clip(0.5 + 1.0 * jax.random.uniform(key_of[3], (H * DH,), jnp.float32) ** shard_levels(key_of[3], (H * DH,), ((0, 4),), -0.2, 0.2), 0.5, 1.5).astype(jnp.bfloat16)
    w_out = gaussian_with(key_of[4], (H * DH, D), (H * DH) ** -0.5, 0.25, ((0, 4),), (0, 1, 4, 2.0))
    block_lists = draw_block_lists(jax.random.fold_in(key_of[7], 71), 0)
    counts = draw_counts(jax.random.fold_in(key_of[7], 71), 0)
    return dict(history=history, ln_gain=ln_gain, w_in=w_in, out_gain=out_gain, w_out=w_out, block_lists=block_lists, counts=counts)


EPS = 1e-05

def reference(history, ln_gain, w_in, out_gain, w_out, block_lists, counts):
    floats = history.astype(jnp.float32)
    centre = lax.optimization_barrier(jnp.mean(floats, axis=-1, keepdims=True))
    spread_sq = lax.optimization_barrier(jnp.mean(jnp.square(floats - centre), axis=-1, keepdims=True))
    normed_x = ((floats - centre) * lax.rsqrt(spread_sq + EPS) * ln_gain.astype(jnp.float32)).astype(jnp.bfloat16)
    parts = [jax.nn.silu(jnp.dot(normed_x, w_in[which], preferred_element_type=jnp.float32)).astype(jnp.bfloat16) for which in range(4)]
    gating, values, queries, keys = parts
    key_blocks = keys.reshape(NBLK, BLK, H, DH)
    value_blocks = values.reshape(NBLK, BLK, H, DH)
    query_blocks = queries.reshape(NBLK, BLK, H, DH)
    positions = jnp.arange(BLK, dtype=jnp.int32)
    causal = positions[None, :] <= positions[:, None]
    scale = DH ** (-0.5)

    def one_block(block):
        listed = block_lists[block]
        in_list = jnp.arange(MAXK, dtype=jnp.int32) < counts[block]
        picked_keys = key_blocks[listed].astype(jnp.float32)
        picked_values = value_blocks[listed].astype(jnp.float32)
        query_here = query_blocks[block].astype(jnp.float32)
        scores = jnp.einsum('qhe,tkhe->hqtk', query_here, picked_keys) * scale
        allowed = in_list[None, :, None] & ((listed != block)[None, :, None] | causal[:, None, :])
        weights = jnp.where(allowed[None], jax.nn.silu(scores), 0.0).astype(jnp.bfloat16)
        weights = lax.optimization_barrier(weights).astype(jnp.float32)
        return jnp.einsum('hqtk,tkhe->qhe', weights, picked_values)
    attended = lax.map(one_block, jnp.arange(NBLK, dtype=jnp.int32)).reshape(NBLK * BLK, H, DH)
    centre_h = lax.optimization_barrier(jnp.mean(attended, axis=-1, keepdims=True))
    spread_h = lax.optimization_barrier(jnp.mean(jnp.square(attended - centre_h), axis=-1, keepdims=True))
    normed_h = (attended - centre_h) * lax.rsqrt(spread_h + EPS)
    gated = normed_h * out_gain.astype(jnp.float32).reshape(H, DH) * gating.astype(jnp.float32).reshape(NBLK * BLK, H, DH)
    gated = gated.astype(jnp.bfloat16).reshape(NBLK * BLK, H * DH)
    mixed = jnp.dot(gated, w_out, preferred_element_type=jnp.float32) + floats
    return mixed.astype(jnp.bfloat16)
```

```python
import functools

import jax
import jax.numpy as jnp
from jax import lax
from jax.experimental import pallas as pl
from jax.experimental.pallas import tpu as pltpu
from jax.sharding import PartitionSpec as P

DH = 128
BLK = 128
WIN = 32
MAXK = 16
EPS = 1e-05
GROUP = 4

NT = (((1,), (1,)), ((), ()))


def silu(v):
    half = 0.5 * v
    return half * jnp.tanh(half) + half


def normed(rows, gain):
    floats = rows.astype(jnp.float32)
    centre = jnp.mean(floats, axis=-1, keepdims=True)
    off = floats - centre
    spread = jnp.mean(jnp.square(off), axis=-1, keepdims=True)
    return (off * lax.rsqrt(spread + EPS) * gain.astype(jnp.float32)).astype(jnp.bfloat16)


def norm_kernel(history_ref, gain_ref, out_ref):
    out_ref[...] = normed(history_ref[...], gain_ref[...])


def own_kernel(history_ref, gain_ref, w_ref, gate_ref, query_ref):
    here = normed(history_ref[...], gain_ref[...])
    gate_ref[...] = silu(jnp.dot(here, w_ref[0], preferred_element_type=jnp.float32)).astype(
        jnp.bfloat16
    )
    query_ref[...] = silu(jnp.dot(here, w_ref[2], preferred_element_type=jnp.float32)).astype(
        jnp.bfloat16
    )


def attend_kernel(
    slots_ref,
    live_ref,
    lists_ref,
    counts_ref,
    base_ref,
    normed_ref,
    w_ref,
    query_ref,
    gate_ref,
    gain_ref,
    out_ref,
    keys_ref,
    values_ref,
):
    step = pl.program_id(0)
    chunk = normed_ref.shape[0]
    sub = 2 * BLK
    cols = query_ref.shape[1]
    heads = cols // DH
    blocks_dev = counts_ref.shape[0]

    @pl.when(live_ref[step] > 0)
    def _():
        for part in range(chunk // sub):
            rows = normed_ref[pl.ds(part * sub, sub), :]
            at = pl.ds(step * chunk + part * sub, sub)
            keys_ref[at, :] = silu(
                jnp.dot(rows, w_ref[3], preferred_element_type=jnp.float32)
            ).astype(jnp.bfloat16)
            values_ref[at, :] = silu(
                jnp.dot(rows, w_ref[1], preferred_element_type=jnp.float32)
            ).astype(jnp.bfloat16)

    @pl.when(step == pl.num_programs(0) - 1)
    def _():
        base = base_ref[0]
        scale = 0.5 * DH ** (-0.5)
        causal = lax.broadcasted_iota(jnp.int32, (BLK, BLK), 1) <= lax.broadcasted_iota(
            jnp.int32, (BLK, BLK), 0
        )

        def one_block(i, unused):
            count = counts_ref[i]
            here = pl.ds(pl.multiple_of(i * BLK, BLK), BLK)
            query = query_ref[here, :]

            def group(j, sums):
                starts, scales = [], []
                for t in range(GROUP):
                    entry = j * GROUP + t
                    starts.append(pl.multiple_of((lists_ref[i, entry] - base) * BLK, BLK))
                    scales.append(jnp.where(entry < count, scale, 0.0))
                done = []
                for h in range(heads):
                    at = pl.ds(h * DH, DH)
                    keys = jnp.concatenate([keys_ref[pl.ds(s, BLK), at] for s in starts], axis=0)
                    values = jnp.concatenate(
                        [values_ref[pl.ds(s, BLK), at] for s in starts], axis=0
                    )
                    scores = lax.dot_general(
                        query[:, h * DH : (h + 1) * DH],
                        keys,
                        NT,
                        preferred_element_type=jnp.float32,
                    )
                    weights = []
                    for t in range(GROUP):
                        half = scores[:, t * BLK : (t + 1) * BLK] * scales[t]
                        weight = half * jnp.tanh(half) + half
                        if t == 0:
                            weight = jnp.where(causal | (j > 0), weight, 0.0)
                        weights.append(weight.astype(jnp.bfloat16))
                    done.append(
                        sums[h]
                        + jnp.dot(
                            jnp.concatenate(weights, axis=1),
                            values,
                            preferred_element_type=jnp.float32,
                        )
                    )
                return tuple(done)

            zero = tuple(jnp.zeros((BLK, DH), jnp.float32) for h in range(heads))
            sums = lax.fori_loop(0, (count + GROUP - 1) // GROUP, group, zero)
            for h in range(heads):
                at = pl.ds(h * DH, DH)
                centre = jnp.mean(sums[h], axis=-1, keepdims=True)
                off = sums[h] - centre
                spread = jnp.mean(jnp.square(off), axis=-1, keepdims=True)
                gated = (
                    off
                    * lax.rsqrt(spread + EPS)
                    * gain_ref[:, at].astype(jnp.float32)
                    * gate_ref[here, at].astype(jnp.float32)
                )
                out_ref[here, at] = gated.astype(jnp.bfloat16)
            return unused

        lax.fori_loop(0, blocks_dev, one_block, 0)


def out_kernel(gated_ref, w_ref, history_ref, out_ref):
    mixed = jnp.dot(gated_ref[...], w_ref[...], preferred_element_type=jnp.float32)
    out_ref[...] = (mixed + history_ref[...].astype(jnp.float32)).astype(jnp.bfloat16)


def shifted(shard, by):
    length = lax.axis_size("seq")
    return lax.ppermute(shard, "seq", [(i, i + by) for i in range(length - by)])


def body(history, ln_gain, w_in, out_gain, w_out, block_lists, counts):
    tok_rows, width = history.shape
    blocks_dev = counts.shape[0]
    cols = w_in.shape[2]
    n_seq, n_head = lax.axis_size("seq"), lax.axis_size("head")
    seq_index, head_index = lax.axis_index("seq"), lax.axis_index("head")
    reach = (WIN - 1 + blocks_dev - 1) // blocks_dev
    depth = reach + 1
    gain = ln_gain.reshape(1, width)

    share_rows = tok_rows // n_head
    share = pl.pallas_call(
        norm_kernel,
        grid=(1,),
        out_shape=jax.ShapeDtypeStruct((share_rows, width), jnp.bfloat16),
    )(lax.dynamic_slice_in_dim(history, head_index * share_rows, share_rows, 0), gain)
    steps = jnp.arange(depth, dtype=jnp.int32)
    sources = seq_index - reach + steps
    if n_seq <= depth + 1:
        window = lax.all_gather(share, ("seq", "head"), axis=0, tiled=True)
        slots = jnp.maximum(sources, 0)
    else:
        shares = jnp.stack([shifted(share, reach - d) for d in range(reach)] + [share])
        window = lax.all_gather(shares, "head", axis=1).reshape(depth * tok_rows, width)
        slots = steps
    live = (sources >= 0).astype(jnp.int32)

    gate, query = pl.pallas_call(
        own_kernel,
        grid=(3,),
        in_specs=[
            pl.BlockSpec((tok_rows // 3, width), lambda i: (i, 0)),
            pl.BlockSpec((1, width), lambda i: (0, 0)),
            pl.BlockSpec((4, width, cols), lambda i: (0, 0, 0)),
        ],
        out_specs=[pl.BlockSpec((tok_rows // 3, cols), lambda i: (i, 0))] * 2,
        out_shape=[jax.ShapeDtypeStruct((tok_rows, cols), jnp.bfloat16)] * 2,
        compiler_params=pltpu.CompilerParams(vmem_limit_bytes=48 << 20),
    )(history, gain, w_in)

    whole = lambda shape: pl.BlockSpec(shape, lambda i, *refs: (0,) * len(shape))
    gated = pl.pallas_call(
        attend_kernel,
        grid_spec=pltpu.PrefetchScalarGridSpec(
            num_scalar_prefetch=5,
            grid=(depth,),
            in_specs=[
                pl.BlockSpec((tok_rows, width), lambda i, slots, *refs: (slots[i], 0)),
                whole((4, width, cols)),
                whole((tok_rows, cols)),
                whole((tok_rows, cols)),
                whole((1, cols)),
            ],
            out_specs=whole((tok_rows, cols)),
            scratch_shapes=[pltpu.VMEM((depth * tok_rows, cols), jnp.bfloat16)] * 2,
        ),
        out_shape=jax.ShapeDtypeStruct((tok_rows, cols), jnp.bfloat16),
        compiler_params=pltpu.CompilerParams(vmem_limit_bytes=48 << 20),
    )(
        slots,
        live,
        block_lists,
        counts,
        ((seq_index - reach) * blocks_dev).reshape(1).astype(jnp.int32),
        window,
        w_in,
        query,
        gate,
        out_gain.reshape(1, cols),
    )

    w_mine = lax.all_to_all(w_out, "head", split_axis=1, concat_axis=0, tiled=True)
    all_gated = lax.all_gather(gated, "head", axis=1, tiled=True)
    out_cols = width // n_head
    residual = lax.dynamic_slice_in_dim(history, head_index * out_cols, out_cols, 1)
    return pl.pallas_call(
        out_kernel,
        grid=(3,),
        in_specs=[
            pl.BlockSpec((tok_rows // 3, all_gated.shape[1]), lambda i: (i, 0)),
            pl.BlockSpec(w_mine.shape, lambda i: (0, 0)),
            pl.BlockSpec((tok_rows // 3, out_cols), lambda i: (i, 0)),
        ],
        out_specs=pl.BlockSpec((tok_rows // 3, out_cols), lambda i: (i, 0)),
        out_shape=jax.ShapeDtypeStruct((tok_rows, out_cols), jnp.bfloat16),
        compiler_params=pltpu.CompilerParams(vmem_limit_bytes=48 << 20),
    )(all_gated, w_mine, residual)


def solution(mesh):
    placed = (
        P("seq", None),
        P(),
        P(None, None, "head"),
        P("head"),
        P("head", None),
        P("seq", None),
        P("seq"),
    )
    return jax.shard_map(
        body, mesh=mesh, in_specs=placed, out_specs=P("seq", "head"), check_vma=False
    )
```

```python
import jax
import jax.numpy as jnp
from jax import lax
from jax.experimental import pallas as pl
from jax.experimental.pallas import tpu as pltpu
from jax.sharding import PartitionSpec as P

DH = 128
BLK = 128
WIN = 32
MAXK = 16
EPS = 1e-05
GROUP = 4

NT = (((1,), (1,)), ((), ()))
PARAMS = pltpu.CompilerParams(vmem_limit_bytes=48 << 20)


def silu(v):
    half = 0.5 * v
    return half * jnp.tanh(half) + half


def project(rows, w):
    return silu(jnp.dot(rows, w, preferred_element_type=jnp.float32)).astype(jnp.bfloat16)


def normed(rows, gain):
    floats = rows.astype(jnp.float32)
    centre = jnp.mean(floats, axis=-1, keepdims=True)
    off = floats - centre
    spread = jnp.mean(jnp.square(off), axis=-1, keepdims=True)
    return (off * lax.rsqrt(spread + EPS) * gain.astype(jnp.float32)).astype(jnp.bfloat16)


def norm_kernel(head_ref, history_ref, gain_ref, out_ref):
    out_ref[...] = normed(history_ref[...], gain_ref[...])


def own_kernel(history_ref, gain_ref, w_ref, gate_ref, values_ref, query_ref, keys_ref):
    here = normed(history_ref[...], gain_ref[...])
    query_ref[...] = project(here, w_ref[2])
    keys_ref[...] = project(here, w_ref[3])
    values_ref[...] = project(here, w_ref[1])
    gate_ref[...] = project(here, w_ref[0])


def list_pairs(base, lists_ref, counts_ref, first, blocks, pairs_ref, n):
    for b in range(blocks):

        def entry(t, n):
            g = lists_ref[b, t] - base
            pairs_ref[n] = (first + b) * 16 + g
            return n + jnp.where((g >= 0) & (g < blocks), 1, 0)

        n = lax.fori_loop(0, counts_ref[b], entry, n)
    return n


def attend(own, base, lists, counts, lists_x, counts_x, query_ref, keys_ref, values_ref, sums_ref, pairs_ref):
    blocks = counts.shape[0]
    heads = query_ref.shape[1] // DH
    scale = 0.5 * DH ** (-0.5)
    n = list_pairs(base, lists, counts, 0, blocks, pairs_ref, 0)
    n = list_pairs(base, lists_x, counts_x, blocks, blocks, pairs_ref, n)
    for t in range(GROUP):
        pairs_ref[n + t] = 0
    behind = lax.broadcasted_iota(jnp.int32, (BLK, BLK), 1) - lax.broadcasted_iota(
        jnp.int32, (BLK, BLK), 0
    )

    def group(j, unused):
        done = []
        for t in range(GROUP):
            code = pairs_ref[j * GROUP + t]
            b, g = code // 16, code % 16
            factor = jnp.where(j * GROUP + t < n, scale, 0.0)
            rows = pl.ds(pl.multiple_of(b * BLK, BLK), BLK)
            at = pl.ds(pl.multiple_of(g * BLK, BLK), BLK)
            for h in range(heads):
                cols = pl.ds(h * DH, DH)
                scores = lax.dot_general(
                    query_ref[rows, cols], keys_ref[at, cols], NT, preferred_element_type=jnp.float32
                )
                half = scores * factor
                weights = half * jnp.tanh(half) + half
                if own:
                    weights = jnp.where(behind <= jnp.where(b == g, 0, BLK), weights, 0.0)
                update = jnp.dot(
                    weights.astype(jnp.bfloat16),
                    values_ref[at, cols],
                    preferred_element_type=jnp.float32,
                )
                done.append((rows, cols, update))
        for rows, cols, update in done:
            sums_ref[rows, cols] += update
        return unused

    lax.fori_loop(0, (n + GROUP - 1) // GROUP, group, 0)


def own_attend_kernel(
    place, lists, counts, lists_x, counts_x, query_ref, query_x_ref, keys_ref, values_ref, sums_ref, both_ref, pairs_ref
):
    rows = query_ref.shape[0]
    both_ref[0:rows, :] = query_ref[...]
    both_ref[rows : 2 * rows, :] = query_x_ref[...]
    sums_ref[...] = jnp.zeros_like(sums_ref)
    attend(
        True, place[0] * counts.shape[0], lists, counts, lists_x, counts_x, both_ref, keys_ref, values_ref, sums_ref, pairs_ref
    )


def make_chunk_kernel(back, n_head, last):
    def kernel(place, lists, counts, lists_x, counts_x, *refs):
        pieces = refs[:n_head]
        w_keys_ref, w_values_ref, query_ref, query_x_ref, before_ref = refs[n_head : n_head + 5]
        if last:
            sums_ref, send_ref, total_ref, both_ref, keys_ref, values_ref, pairs_ref = refs[n_head + 5 :]
        else:
            total_ref, both_ref, keys_ref, values_ref, pairs_ref = refs[n_head + 5 :]
        rows, cols = query_ref.shape
        share = pieces[0].shape[0]
        source = place[0] - 2 * back
        total_ref[...] = before_ref[...]

        @pl.when(source >= 0)
        def _():
            both_ref[0:rows, :] = query_ref[...]
            both_ref[rows : 2 * rows, :] = query_x_ref[...]
            for m, piece in enumerate(pieces):
                at = pl.ds(pl.multiple_of((place[1] ^ m) * share, share), share)
                keys_ref[at, :] = project(piece[...], w_keys_ref[0])
                values_ref[at, :] = project(piece[...], w_values_ref[0])
            attend(
                False, source * counts.shape[0], lists, counts, lists_x, counts_x,
                both_ref, keys_ref, values_ref, total_ref, pairs_ref,
            )

        if last:
            sums_ref[...] = total_ref[0:rows, :]
            for h in range(cols // DH):
                at = pl.ds(h * DH, DH)
                part = total_ref[rows : 2 * rows, at]
                send_ref[:, at] = (part - jnp.mean(part, axis=-1, keepdims=True)).astype(jnp.bfloat16)

    return kernel


def finish_kernel(sums_ref, arrived_ref, gate_ref, gain_ref, out_ref):
    for h in range(sums_ref.shape[1] // DH):
        at = pl.ds(h * DH, DH)
        part = sums_ref[:, at]
        part = part - jnp.mean(part, axis=-1, keepdims=True) + arrived_ref[:, at].astype(jnp.float32)
        off = part - jnp.mean(part, axis=-1, keepdims=True)
        spread = jnp.mean(jnp.square(off), axis=-1, keepdims=True)
        out_ref[:, at] = (
            off
            * lax.rsqrt(spread + EPS)
            * gain_ref[:, at].astype(jnp.float32)
            * gate_ref[:, at].astype(jnp.float32)
        ).astype(jnp.bfloat16)


def out_kernel(place, *refs):
    *pieces, w_ref, history_ref, out_ref = refs
    cols = pieces[0].shape[1]
    mixed = history_ref[...].astype(jnp.float32)
    for m, piece in enumerate(pieces):
        at = pl.ds(pl.multiple_of((place[1] ^ m) * cols, cols), cols)
        mixed = mixed + jnp.dot(piece[...], w_ref[at, :], preferred_element_type=jnp.float32)
    out_ref[...] = mixed.astype(jnp.bfloat16)


def crossed(array, axis, bit):
    return lax.ppermute(array, axis, [(i, i ^ bit) for i in range(lax.axis_size(axis))])


def spread(piece):
    n = lax.axis_size("head")
    pieces = {0: piece}
    bit = n // 2
    while bit:
        pieces.update({m + bit: crossed(p, "head", bit) for m, p in list(pieces.items())})
        bit //= 2
    return [pieces[m] for m in range(n)]


def whole(shape):
    return pl.BlockSpec(shape, lambda *at: (0,) * len(shape))


def body(history, ln_gain, w_in, out_gain, w_out, block_lists, counts):
    tok_rows, width = history.shape
    blocks = counts.shape[0]
    cols = w_in.shape[2]
    n_seq, n_head = lax.axis_size("seq"), lax.axis_size("head")
    seq_index, head_index = lax.axis_index("seq"), lax.axis_index("head")
    planes = (WIN - 1 + 2 * blocks - 1) // (2 * blocks)
    gain = ln_gain.reshape(1, width)
    place = jnp.stack([seq_index, head_index]).astype(jnp.int32)
    rows_of = lambda n: jax.ShapeDtypeStruct((n, cols), jnp.bfloat16)
    n_pairs = 2 * blocks * MAXK + GROUP

    share_rows = tok_rows // n_head
    share = pl.pallas_call(
        norm_kernel,
        grid_spec=pltpu.PrefetchScalarGridSpec(
            num_scalar_prefetch=1,
            grid=(1,),
            in_specs=[pl.BlockSpec((share_rows, width), lambda i, place: (place[1], 0)), whole((1, width))],
            out_specs=whole((share_rows, width)),
        ),
        out_shape=jax.ShapeDtypeStruct((share_rows, width), jnp.bfloat16),
    )(place, history, gain)
    upward = [(i, i + 2) for i in range(n_seq - 2)]
    chunks = []
    for back in range(planes):
        share = lax.ppermute(share, "seq", upward)
        chunks.append(spread(share))
    w_mine = lax.all_to_all(w_out, "head", split_axis=1, concat_axis=0, tiled=True)

    part = tok_rows // 3
    gate, values, query, keys = pl.pallas_call(
        own_kernel,
        grid=(3,),
        in_specs=[
            pl.BlockSpec((part, width), lambda i: (i, 0)),
            pl.BlockSpec((1, width), lambda i: (0, 0)),
            whole((4, width, cols)),
        ],
        out_specs=[pl.BlockSpec((part, cols), lambda i: (i, 0))] * 4,
        out_shape=[rows_of(tok_rows)] * 4,
        compiler_params=PARAMS,
    )(history, gain, w_in)
    query_x = crossed(query, "seq", 1)
    told = crossed(jnp.concatenate([block_lists, counts[:, None]], axis=1), "seq", 1)
    scalars = (place, block_lists, counts, told[:, :MAXK], told[:, MAXK])

    sums_shape = jax.ShapeDtypeStruct((2 * tok_rows, cols), jnp.float32)
    sums = pl.pallas_call(
        own_attend_kernel,
        grid_spec=pltpu.PrefetchScalarGridSpec(
            num_scalar_prefetch=5,
            grid=(1,),
            in_specs=[whole((tok_rows, cols))] * 4,
            out_specs=whole(sums_shape.shape),
            scratch_shapes=[
                pltpu.VMEM((2 * tok_rows, cols), jnp.bfloat16),
                pltpu.SMEM((n_pairs,), jnp.int32),
            ],
        ),
        out_shape=sums_shape,
        compiler_params=PARAMS,
    )(*scalars, query, query_x, keys, values)

    for back, pieces in enumerate(chunks, start=1):
        last = back == planes
        if last:
            out_shape = [jax.ShapeDtypeStruct((tok_rows, cols), jnp.float32), rows_of(tok_rows)]
        else:
            out_shape = sums_shape
        sums = pl.pallas_call(
            make_chunk_kernel(back, n_head, last),
            grid_spec=pltpu.PrefetchScalarGridSpec(
                num_scalar_prefetch=5,
                grid=(1,),
                in_specs=[whole((share_rows, width))] * n_head
                + [
                    pl.BlockSpec((1, width, cols), lambda *at: (3, 0, 0)),
                    pl.BlockSpec((1, width, cols), lambda *at: (1, 0, 0)),
                    whole((tok_rows, cols)),
                    whole((tok_rows, cols)),
                    whole(sums_shape.shape),
                ],
                out_specs=[whole((tok_rows, cols))] * 2 if last else whole(sums_shape.shape),
                scratch_shapes=([pltpu.VMEM(sums_shape.shape, jnp.float32)] if last else [])
                + [
                    pltpu.VMEM((2 * tok_rows, cols), jnp.bfloat16),
                    pltpu.VMEM((tok_rows, cols), jnp.bfloat16),
                    pltpu.VMEM((tok_rows, cols), jnp.bfloat16),
                    pltpu.SMEM((n_pairs,), jnp.int32),
                ],
            ),
            out_shape=out_shape,
            compiler_params=PARAMS,
        )(*scalars, *pieces, w_in, w_in, query, query_x, sums)
    mine, send = sums
    arrived = crossed(send, "seq", 1)
    gated = pl.pallas_call(
        finish_kernel,
        grid=(1,),
        in_specs=[whole((tok_rows, cols))] * 3 + [whole((1, cols))],
        out_specs=whole((tok_rows, cols)),
        out_shape=rows_of(tok_rows),
        compiler_params=PARAMS,
    )(mine, arrived, gate, out_gain.reshape(1, cols))

    gated_pieces = spread(gated)
    out_cols = width // n_head
    return pl.pallas_call(
        out_kernel,
        grid_spec=pltpu.PrefetchScalarGridSpec(
            num_scalar_prefetch=1,
            grid=(3,),
            in_specs=[pl.BlockSpec((part, cols), lambda i, place: (i, 0))] * n_head
            + [
                whole(w_mine.shape),
                pl.BlockSpec((part, out_cols), lambda i, place: (i, place[1])),
            ],
            out_specs=pl.BlockSpec((part, out_cols), lambda i, place: (i, 0)),
        ),
        out_shape=jax.ShapeDtypeStruct((tok_rows, out_cols), jnp.bfloat16),
        compiler_params=PARAMS,
    )(place, *gated_pieces, w_mine, history)


def solution(mesh):
    placed = (
        P("seq", None),
        P(),
        P(None, None, "head"),
        P("head"),
        P("head", None),
        P("seq", None),
        P("seq"),
    )
    return jax.shard_map(
        body, mesh=mesh, in_specs=placed, out_specs=P("seq", "head"), check_vma=False
    )
```

```python
import jax
import jax.numpy as jnp
from jax import lax
from jax.experimental import pallas as pl
from jax.experimental.pallas import tpu as pltpu
from jax.sharding import PartitionSpec as P

DH = 128
BLK = 128
WIN = 32
MAXK = 16
EPS = 1e-05
PLANES = 2
FAR = 2 * PLANES + 1
SCALE = 0.5 * DH ** (-0.5)

NT = (((1,), (1,)), ((), ()))


def params():
    return pltpu.CompilerParams(vmem_limit_bytes=48 << 20)


def cost(us):
    return pl.CostEstimate(flops=int(us * 1e9 * 0.3), bytes_accessed=int(us * 3e6 * 0.3), transcendentals=0)


def silu(v):
    half = 0.5 * v
    return half * jnp.tanh(half) + half


def project(rows, w):
    return silu(jnp.dot(rows, w, preferred_element_type=jnp.float32))


def normed(rows, gain):
    floats = rows.astype(jnp.float32)
    centre = jnp.mean(floats, axis=-1, keepdims=True)
    off = floats - centre
    spread_sq = jnp.mean(jnp.square(off), axis=-1, keepdims=True)
    return (off * lax.rsqrt(spread_sq + EPS) * gain.astype(jnp.float32)).astype(jnp.bfloat16)


def norm_kernel(history_ref, gain_ref, out_ref, rows_ref, sem):
    share = out_ref.shape[0]
    at = pl.ds(pl.multiple_of(lax.axis_index("head") * share, share), share)
    copy = pltpu.make_async_copy(history_ref.at[at], rows_ref, sem)
    copy.start()
    copy.wait()
    out_ref[...] = normed(rows_ref[...], gain_ref[...].reshape(1, -1))


def own_kernel(history_ref, gain_ref, w_ref, gate_ref, values_ref, query_ref, keys_t_ref, tail_ref):
    here = normed(history_ref[...], gain_ref[...].reshape(1, -1))
    query_ref[...] = project(here, w_ref[2]).astype(jnp.bfloat16)
    keys = project(here, w_ref[3])
    keys_t_ref[...] = keys.T.astype(jnp.bfloat16)
    values = project(here, w_ref[1]).astype(jnp.bfloat16)
    values_ref[...] = values
    tail_ref[0] = keys[-BLK:].astype(jnp.bfloat16)
    tail_ref[1] = values[-BLK:]
    gate_ref[...] = project(here, w_ref[0]).astype(jnp.bfloat16)


def mark(live_ref, told_ref, source, blocks, first):
    base = source * blocks
    for b in range(blocks):
        for g in range(blocks):
            live_ref[(first + b) * 8 + g] = 0.0

        def entry(t, unused):
            g = told_ref[b, t] - base
            live_ref[(first + b) * 8 + jnp.where((g >= 0) & (g < blocks), g, 7)] = SCALE
            return unused

        lax.fori_loop(0, told_ref[b, MAXK], entry, 0)


def tile(scores, factor):
    half = scores * factor
    return half * jnp.tanh(half) + half


def attend_dense(query_ref, q_rows, sums_ref, sum_rows, keys_t_ref, values_ref, factors):
    blocks = len(factors[0])
    for h in range(query_ref.shape[1] // DH):
        cols = pl.ds(h * DH, DH)
        scores = jnp.dot(
            query_ref[q_rows, cols], keys_t_ref[cols, :], preferred_element_type=jnp.float32
        )
        weights = [
            jnp.concatenate(
                [
                    tile(scores[i * BLK : (i + 1) * BLK, g * BLK : (g + 1) * BLK], factors[i][g])
                    for i in range(2)
                ],
                axis=0,
            ).astype(jnp.bfloat16)
            for g in range(blocks)
        ]
        sums_ref[sum_rows, cols] += jnp.dot(
            jnp.concatenate(weights, axis=1), values_ref[:, cols], preferred_element_type=jnp.float32
        )


def attend_all(query_ref, sums_ref, sum_first, keys_t_ref, values_ref, live_ref, live_first, blocks):
    def two(p, unused):
        factors = [
            [live_ref[(live_first + 2 * p + i) * 8 + g] for g in range(blocks)] for i in range(2)
        ]

        @pl.when(sum(factors[0]) + sum(factors[1]) > 0.0)
        def _():
            q_rows = pl.ds(pl.multiple_of(p * 2 * BLK, 2 * BLK), 2 * BLK)
            sum_rows = pl.ds(pl.multiple_of(sum_first + p * 2 * BLK, 2 * BLK), 2 * BLK)
            attend_dense(query_ref, q_rows, sums_ref, sum_rows, keys_t_ref, values_ref, factors)

        return unused

    lax.fori_loop(0, blocks // 2, two, 0)


def own_attend_kernel(told_ref, told_x_ref, query_ref, query_x_ref, keys_t_ref, values_ref, sums_ref, live_ref):
    rows = query_ref.shape[0]
    blocks = rows // BLK
    here = lax.axis_index("seq")
    mark(live_ref, told_ref, here, blocks, 0)
    mark(live_ref, told_x_ref, here, blocks, blocks)
    sums_ref[rows:, :] = jnp.zeros((rows, sums_ref.shape[1]), jnp.float32)
    behind = lax.broadcasted_iota(jnp.int32, (BLK, BLK), 1) <= lax.broadcasted_iota(
        jnp.int32, (BLK, BLK), 0
    )
    for p in range(blocks // 2):
        q_rows = pl.ds(p * 2 * BLK, 2 * BLK)
        seen = pl.ds(0, (2 * p + 2) * BLK)
        for h in range(query_ref.shape[1] // DH):
            cols = pl.ds(h * DH, DH)
            scores = jnp.dot(
                query_ref[q_rows, cols], keys_t_ref[cols, seen], preferred_element_type=jnp.float32
            )
            weights = []
            for g in range(2 * p + 2):
                column = []
                for i in range(2):
                    b = 2 * p + i
                    if g > b:
                        column.append(jnp.zeros((BLK, BLK), jnp.float32))
                        continue
                    part = tile(
                        scores[i * BLK : (i + 1) * BLK, g * BLK : (g + 1) * BLK], live_ref[b * 8 + g]
                    )
                    column.append(jnp.where(behind, part, 0.0) if g == b else part)
                weights.append(jnp.concatenate(column, axis=0).astype(jnp.bfloat16))
            sums_ref[q_rows, cols] = jnp.dot(
                jnp.concatenate(weights, axis=1),
                values_ref[seen, cols],
                preferred_element_type=jnp.float32,
            )
    attend_all(query_x_ref, sums_ref, rows, keys_t_ref, values_ref, live_ref, blocks, blocks)


def centred(part):
    return part - jnp.mean(part, axis=-1, keepdims=True)


def send_off(sums_ref, first, send_ref):
    rows, cols = send_ref.shape
    for h in range(cols // DH):
        at = pl.ds(h * DH, DH)
        send_ref[:, at] = centred(sums_ref[pl.ds(first, rows), at]).astype(jnp.bfloat16)


def far_kernel(told_ref, query_ref, keys_t_ref, values_ref, send_ref, sums_ref, live_ref):
    blocks = query_ref.shape[0] // BLK
    here = lax.axis_index("seq")

    @pl.when((here % 2 == 1) & (here + FAR < lax.axis_size("seq")))
    def _():
        mark(live_ref, told_ref, here, blocks, 0)
        sums_ref[...] = jnp.zeros_like(sums_ref)
        attend_all(query_ref, sums_ref, 0, keys_t_ref, values_ref, live_ref, 0, blocks)
        send_off(sums_ref, 0, send_ref)


def make_chunk_kernel(back, n_head, last):
    def kernel(told_ref, told_x_ref, *refs):
        pieces = refs[:n_head]
        w_keys_ref, w_values_ref, query_ref, query_x_ref, before_ref = refs[n_head : n_head + 5]
        refs = refs[n_head + 5 :]
        if last:
            tail_ref, sums_ref, send_ref, total_ref, keys_ref, keys_t_ref, values_ref, live_ref = refs
        else:
            total_ref, keys_ref, keys_t_ref, values_ref, live_ref = refs
        rows, cols = query_ref.shape
        blocks = rows // BLK
        share = pieces[0].shape[0]
        here = lax.axis_index("seq")
        source = here - 2 * back
        total_ref[...] = before_ref[...]

        @pl.when(source >= 0)
        def _():
            for m, piece in enumerate(pieces):
                at = pl.ds(pl.multiple_of((lax.axis_index("head") ^ m) * share, share), share)
                keys_ref[at, :] = project(piece[...], w_keys_ref[0])
                values_ref[at, :] = project(piece[...], w_values_ref[0]).astype(jnp.bfloat16)
            keys_t_ref[...] = keys_ref[...].T.astype(jnp.bfloat16)
            mark(live_ref, told_ref, source, blocks, 0)
            mark(live_ref, told_x_ref, source, blocks, blocks)
            attend_all(query_ref, total_ref, 0, keys_t_ref, values_ref, live_ref, 0, blocks)
            attend_all(query_x_ref, total_ref, rows, keys_t_ref, values_ref, live_ref, blocks, blocks)

        if last:
            farthest = here - FAR - 1

            @pl.when(farthest >= 0)
            def _():
                mark(live_ref, told_ref, farthest, blocks, 0)
                for h in range(cols // DH):
                    at = pl.ds(h * DH, DH)
                    scores = lax.dot_general(
                        query_ref[0:BLK, at], tail_ref[0, :, at], NT, preferred_element_type=jnp.float32
                    )
                    weights = tile(scores, live_ref[blocks - 1]).astype(jnp.bfloat16)
                    total_ref[0:BLK, at] += jnp.dot(
                        weights, tail_ref[1, :, at], preferred_element_type=jnp.float32
                    )

            sums_ref[...] = total_ref[0:rows, :]
            send_off(total_ref, rows, send_ref)

    return kernel


def finish_kernel(sums_ref, near_ref, far_ref, gate_ref, gain_ref, out_ref):
    for h in range(sums_ref.shape[1] // DH):
        at = pl.ds(h * DH, DH)
        part = centred(sums_ref[:, at])
        part = part + near_ref[:, at].astype(jnp.float32) + far_ref[:, at].astype(jnp.float32)
        off = centred(part)
        spread_sq = jnp.mean(jnp.square(off), axis=-1, keepdims=True)
        out_ref[:, at] = (
            off
            * lax.rsqrt(spread_sq + EPS)
            * gain_ref[at].reshape(1, -1).astype(jnp.float32)
            * gate_ref[:, at].astype(jnp.float32)
        ).astype(jnp.bfloat16)


def out_kernel(head_ref, *refs):
    *pieces, w_ref, history_ref, out_ref = refs
    cols = pieces[0].shape[1]
    mixed = history_ref[...].astype(jnp.float32)
    for m, piece in enumerate(pieces):
        at = pl.ds(pl.multiple_of((head_ref[0] ^ m) * cols, cols), cols)
        mixed = mixed + jnp.dot(piece[...], w_ref[at, :], preferred_element_type=jnp.float32)
    out_ref[...] = mixed.astype(jnp.bfloat16)


def crossed(array, axis, bit):
    return lax.ppermute(array, axis, [(i, i ^ bit) for i in range(lax.axis_size(axis))])


def spread(piece):
    n = lax.axis_size("head")
    pieces = {0: piece}
    bit = n // 2
    while bit:
        pieces.update({m + bit: crossed(p, "head", bit) for m, p in list(pieces.items())})
        bit //= 2
    return [pieces[m] for m in range(n)]


def whole(shape):
    return pl.BlockSpec(shape, lambda *at: (0,) * len(shape))


def body(history, ln_gain, w_in, out_gain, w_out, block_lists, counts):
    tok_rows, width = history.shape
    blocks = counts.shape[0]
    cols = w_in.shape[2]
    n_seq, n_head = lax.axis_size("seq"), lax.axis_size("head")
    assert 2 * (PLANES + 1) * blocks - (WIN - 1) == blocks - 1
    rows_of = lambda n: jax.ShapeDtypeStruct((n, cols), jnp.bfloat16)
    barrier = lax.optimization_barrier

    told = jnp.concatenate([block_lists, counts[:, None]], axis=1)

    share_rows = tok_rows // n_head
    share = pl.pallas_call(
        norm_kernel,
        in_specs=[pl.BlockSpec(memory_space=pl.ANY), pl.BlockSpec(memory_space=pltpu.VMEM)],
        out_specs=pl.BlockSpec(memory_space=pltpu.VMEM),
        out_shape=jax.ShapeDtypeStruct((share_rows, width), jnp.bfloat16),
        scratch_shapes=[pltpu.VMEM((share_rows, width), jnp.bfloat16), pltpu.SemaphoreType.DMA],
        cost_estimate=cost(2),
    )(history, ln_gain)
    gain, share = barrier((ln_gain, share))
    upward = [(i, i + 2) for i in range(n_seq - 2)]
    share_1 = lax.ppermute(share, "seq", upward)

    part = tok_rows // 3
    gate, values, query, keys_t, tail = pl.pallas_call(
        own_kernel,
        grid=(3,),
        in_specs=[
            pl.BlockSpec((part, width), lambda i: (i, 0)),
            whole((width,)),
            whole((4, width, cols)),
        ],
        out_specs=[pl.BlockSpec((part, cols), lambda i: (i, 0))] * 3
        + [pl.BlockSpec((cols, part), lambda i: (0, i)), whole((2, BLK, cols))],
        out_shape=[rows_of(tok_rows)] * 3
        + [
            jax.ShapeDtypeStruct((cols, tok_rows), jnp.bfloat16),
            jax.ShapeDtypeStruct((2, BLK, cols), jnp.bfloat16),
        ],
        compiler_params=params(),
        cost_estimate=cost(4),
    )(history, gain, w_in)
    downward = [(i, i - FAR) for i in range(FAR + 1, n_seq, 2)]
    query_x, told_x = crossed(query, "seq", 1), crossed(told, "seq", 1)
    query_far, told_far = (lax.ppermute(a, "seq", downward) for a in (query, told))
    tail = lax.ppermute(tail, "seq", [(i, i + FAR + 1) for i in range(n_seq - FAR - 1)])
    w_mine = lax.all_to_all(w_out, "head", split_axis=1, concat_axis=0, tiled=True)

    share_1, query = barrier((share_1, query))
    share_2 = lax.ppermute(share_1, "seq", upward)
    chunk_1 = spread(share_1)

    sums_shape = jax.ShapeDtypeStruct((2 * tok_rows, cols), jnp.float32)
    n_live = 2 * blocks * 8
    sums = pl.pallas_call(
        own_attend_kernel,
        grid_spec=pltpu.PrefetchScalarGridSpec(
            num_scalar_prefetch=2,
            grid=(1,),
            in_specs=[whole((tok_rows, cols))] * 2
            + [whole((cols, tok_rows)), whole((tok_rows, cols))],
            out_specs=whole(sums_shape.shape),
            scratch_shapes=[pltpu.SMEM((n_live,), jnp.float32)],
        ),
        out_shape=sums_shape,
        compiler_params=params(),
        cost_estimate=cost(6),
    )(told, told_x, query, query_x, keys_t, values)

    far = pl.pallas_call(
        far_kernel,
        grid_spec=pltpu.PrefetchScalarGridSpec(
            num_scalar_prefetch=1,
            grid=(1,),
            in_specs=[
                whole((tok_rows, cols)),
                whole((cols, tok_rows)),
                whole((tok_rows, cols)),
            ],
            out_specs=whole((tok_rows, cols)),
            scratch_shapes=[
                pltpu.VMEM((tok_rows, cols), jnp.float32),
                pltpu.SMEM((n_live,), jnp.float32),
            ],
        ),
        out_shape=rows_of(tok_rows),
        compiler_params=params(),
        cost_estimate=cost(3),
    )(told_far, query_far, keys_t, values)
    far = lax.ppermute(far, "seq", [(i, i + FAR) for i in range(1, n_seq - FAR, 2)])

    share_2, sums, w_mine = barrier((share_2, sums, w_mine))
    chunk_2 = spread(share_2)

    for back, pieces in ((1, chunk_1), (2, chunk_2)):
        last = back == PLANES
        extra = [tail] if last else []
        sums = pl.pallas_call(
            make_chunk_kernel(back, n_head, last),
            grid_spec=pltpu.PrefetchScalarGridSpec(
                num_scalar_prefetch=2,
                grid=(1,),
                in_specs=[whole((share_rows, width))] * n_head
                + [
                    pl.BlockSpec((1, width, cols), lambda *at: (3, 0, 0)),
                    pl.BlockSpec((1, width, cols), lambda *at: (1, 0, 0)),
                    whole((tok_rows, cols)),
                    whole((tok_rows, cols)),
                    whole(sums_shape.shape),
                ]
                + [whole(e.shape) for e in extra],
                out_specs=[whole((tok_rows, cols))] * 2 if last else whole(sums_shape.shape),
                scratch_shapes=([pltpu.VMEM(sums_shape.shape, jnp.float32)] if last else [])
                + [
                    pltpu.VMEM((tok_rows, cols), jnp.float32),
                    pltpu.VMEM((cols, tok_rows), jnp.bfloat16),
                    pltpu.VMEM((tok_rows, cols), jnp.bfloat16),
                    pltpu.SMEM((n_live,), jnp.float32),
                ],
            ),
            out_shape=[jax.ShapeDtypeStruct((tok_rows, cols), jnp.float32), rows_of(tok_rows)]
            if last
            else sums_shape,
            compiler_params=params(),
            cost_estimate=cost(6),
        )(told, told_x, *pieces, w_in, w_in, query, query_x, sums, *extra)
    mine, send = sums
    near = crossed(send, "seq", 1)
    gated = pl.pallas_call(
        finish_kernel,
        grid=(1,),
        in_specs=[whole((tok_rows, cols))] * 4 + [whole((cols,))],
        out_specs=whole((tok_rows, cols)),
        out_shape=rows_of(tok_rows),
        compiler_params=params(),
        cost_estimate=cost(1),
    )(mine, near, far, gate, out_gain)

    gated_pieces = spread(gated)
    out_cols = width // n_head
    return pl.pallas_call(
        out_kernel,
        grid_spec=pltpu.PrefetchScalarGridSpec(
            num_scalar_prefetch=1,
            grid=(3,),
            in_specs=[pl.BlockSpec((part, cols), lambda i, head: (i, 0))] * n_head
            + [
                whole(w_mine.shape),
                pl.BlockSpec((part, out_cols), lambda i, head: (i, head[0])),
            ],
            out_specs=pl.BlockSpec((part, out_cols), lambda i, head: (i, 0)),
        ),
        out_shape=jax.ShapeDtypeStruct((tok_rows, out_cols), jnp.bfloat16),
        compiler_params=params(),
        cost_estimate=cost(3),
    )(lax.axis_index("head").reshape(1).astype(jnp.int32), *gated_pieces, w_mine, history)


def solution(mesh):
    placed = (
        P("seq", None),
        P(),
        P(None, None, "head"),
        P("head"),
        P("head", None),
        P("seq", None),
        P("seq"),
    )
    return jax.shard_map(
        body, mesh=mesh, in_specs=placed, out_specs=P("seq", "head"), check_vma=False
    )
```

```python
import jax
import jax.numpy as jnp
from jax import lax
from jax.experimental import pallas as pl
from jax.experimental.pallas import tpu as pltpu
from jax.sharding import PartitionSpec as P

DH = 128
BLK = 128
WIN = 32
MAXK = 16
EPS = 1e-05
PLANES = 2
FAR = 2 * PLANES + 1
SCALE = 0.5 * DH ** (-0.5)

NT = (((1,), (1,)), ((), ()))


def params(mib=24):
    return pltpu.CompilerParams(vmem_limit_bytes=mib << 20)


def cost(us):
    return pl.CostEstimate(flops=int(us * 1e9 * 0.3), bytes_accessed=int(us * 3e6 * 0.3), transcendentals=0)


def silu(v):
    half = 0.5 * v
    return half * jnp.tanh(half) + half


def project(rows, w):
    return silu(jnp.dot(rows, w, preferred_element_type=jnp.float32))


def normed(rows, gain):
    floats = rows.astype(jnp.float32)
    centre = jnp.mean(floats, axis=-1, keepdims=True)
    off = floats - centre
    spread_sq = jnp.mean(jnp.square(off), axis=-1, keepdims=True)
    return (off * lax.rsqrt(spread_sq + EPS) * gain.astype(jnp.float32)).astype(jnp.bfloat16)


def norm_kernel(history_ref, gain_ref, out_ref, rows_ref, sems):
    share = out_ref.shape[0]
    steps = sems.shape[0]
    step = share // steps
    first = lax.axis_index("head") * share
    copies = []
    for i in range(steps):
        at = pl.ds(pl.multiple_of(first + i * step, step), step)
        copies.append(
            pltpu.make_async_copy(history_ref.at[at], rows_ref.at[pl.ds(i * step, step)], sems.at[i])
        )
        copies[i].start()
    gain = gain_ref[...].reshape(1, -1)
    for i in range(steps):
        copies[i].wait()
        at = pl.ds(i * step, step)
        out_ref[at, :] = normed(rows_ref[at, :], gain)


def own_kernel(history_ref, gain_ref, w_ref, gate_ref, values_ref, query_ref, keys_t_ref, tail_ref):
    here = normed(history_ref[...], gain_ref[...].reshape(1, -1))
    query_ref[...] = project(here, w_ref[2]).astype(jnp.bfloat16)
    keys = project(here, w_ref[3])
    keys_t_ref[...] = keys.T.astype(jnp.bfloat16)
    values = project(here, w_ref[1]).astype(jnp.bfloat16)
    values_ref[...] = values
    tail_ref[0] = keys[-BLK:].astype(jnp.bfloat16)
    tail_ref[1] = values[-BLK:]
    gate_ref[...] = project(here, w_ref[0]).astype(jnp.bfloat16)


def mark(live_ref, told_ref, base, key_blocks, first):
    for b in range(told_ref.shape[0]):
        for g in range(key_blocks):
            live_ref[(first + b) * 8 + g] = 0.0

        def entry(t, unused):
            g = told_ref[b, t] - base
            live_ref[(first + b) * 8 + jnp.where((g >= 0) & (g < key_blocks), g, 7)] = SCALE
            return unused

        lax.fori_loop(0, told_ref[b, MAXK], entry, 0)


def tile(scores, factor):
    half = scores * factor
    return half * jnp.tanh(half) + half


def attend_dense(query_ref, rows, sums_ref, keys_t_ref, values_ref, factors):
    n, blocks = len(factors), len(factors[0])
    for h in range(query_ref.shape[1] // DH):
        cols = pl.ds(h * DH, DH)
        scores = jnp.dot(
            query_ref[rows, cols], keys_t_ref[cols, :], preferred_element_type=jnp.float32
        )
        weights = [
            jnp.concatenate(
                [
                    tile(scores[i * BLK : (i + 1) * BLK, g * BLK : (g + 1) * BLK], factors[i][g])
                    for i in range(n)
                ],
                axis=0,
            ).astype(jnp.bfloat16)
            for g in range(blocks)
        ]
        sums_ref[rows, cols] += jnp.dot(
            jnp.concatenate(weights, axis=1), values_ref[:, cols], preferred_element_type=jnp.float32
        )


def attend_all(query_ref, sums_ref, keys_t_ref, values_ref, live_ref, live_first, key_blocks):
    n = 3

    def some(p, unused):
        factors = [
            [live_ref[(live_first + n * p + i) * 8 + g] for g in range(key_blocks)] for i in range(n)
        ]

        @pl.when(sum(sum(f) for f in factors) > 0.0)
        def _():
            rows = pl.ds(pl.multiple_of(p * n * BLK, n * BLK), n * BLK)
            attend_dense(query_ref, rows, sums_ref, keys_t_ref, values_ref, factors)

        return unused

    lax.fori_loop(0, query_ref.shape[0] // (n * BLK), some, 0)


def own_attend_kernel(
    told_ref, told_x_ref, query_ref, query_x_ref, keys_t_ref, values_ref, sums_ref, sums_x_ref, live_ref
):
    rows, cols = query_ref.shape
    blocks = rows // BLK
    here = lax.axis_index("seq")
    mark(live_ref, told_ref, here * blocks, blocks, 0)
    mark(live_ref, told_x_ref, here * blocks, blocks, blocks)
    sums_x_ref[...] = jnp.zeros((rows, cols), jnp.float32)
    behind = lax.broadcasted_iota(jnp.int32, (BLK, BLK), 1) <= lax.broadcasted_iota(
        jnp.int32, (BLK, BLK), 0
    )
    for p in range(blocks // 2):
        q_rows = pl.ds(p * 2 * BLK, 2 * BLK)
        seen = pl.ds(0, (2 * p + 2) * BLK)
        for h in range(cols // DH):
            at = pl.ds(h * DH, DH)
            scores = jnp.dot(
                query_ref[q_rows, at], keys_t_ref[at, seen], preferred_element_type=jnp.float32
            )
            weights = []
            for g in range(2 * p + 2):
                column = []
                for i in range(2):
                    b = 2 * p + i
                    if g > b:
                        column.append(jnp.zeros((BLK, BLK), jnp.float32))
                        continue
                    part = tile(
                        scores[i * BLK : (i + 1) * BLK, g * BLK : (g + 1) * BLK], live_ref[b * 8 + g]
                    )
                    column.append(jnp.where(behind, part, 0.0) if g == b else part)
                weights.append(jnp.concatenate(column, axis=0).astype(jnp.bfloat16))
            sums_ref[q_rows, at] = jnp.dot(
                jnp.concatenate(weights, axis=1),
                values_ref[seen, at],
                preferred_element_type=jnp.float32,
            )
    attend_all(query_x_ref, sums_x_ref, keys_t_ref, values_ref, live_ref, blocks, blocks)


def centred(part):
    return part - jnp.mean(part, axis=-1, keepdims=True)


def send_off(sums_ref, send_ref):
    for h in range(send_ref.shape[1] // DH):
        at = pl.ds(h * DH, DH)
        send_ref[:, at] = centred(sums_ref[:, at]).astype(jnp.bfloat16)


def far_kernel(told_ref, query_ref, keys_t_ref, values_ref, send_ref, sums_ref, live_ref):
    blocks = query_ref.shape[0] // BLK
    here = lax.axis_index("seq")

    @pl.when((here % 2 == 1) & (here + FAR < lax.axis_size("seq")))
    def _():
        mark(live_ref, told_ref, here * blocks, blocks, 0)
        sums_ref[...] = jnp.zeros_like(sums_ref)
        attend_all(query_ref, sums_ref, keys_t_ref, values_ref, live_ref, 0, blocks)
        send_off(sums_ref, send_ref)


def half_base(source, blocks, n_head, crossed_half):
    half = lax.axis_index("head") // (n_head // 2)
    return source * blocks + (half ^ crossed_half) * (blocks // 2)


def half_keys(pieces, w_ref, keys_ref, keys_t_ref, values_ref):
    share = pieces[0].shape[0]
    for m, piece in enumerate(pieces):
        at = ((lax.axis_index("head") % len(pieces)) ^ m) * share
        at = pl.ds(pl.multiple_of(at, share), share)
        keys_ref[at, :] = project(piece[...], w_ref[3])
        values_ref[at, :] = project(piece[...], w_ref[1]).astype(jnp.bfloat16)
    keys_t_ref[...] = keys_ref[...].T.astype(jnp.bfloat16)


def make_half_kernel(back, n_head, crossed_half):
    def kernel(told_ref, told_x_ref, *refs):
        pieces, refs = refs[: n_head // 2], refs[n_head // 2 :]
        w_ref, query_ref, query_x_ref, unused, unused_x, sums_ref, sums_x_ref, keys_ref, keys_t_ref, values_ref, live_ref = refs
        blocks = query_ref.shape[0] // BLK
        source = lax.axis_index("seq") - 2 * back

        @pl.when(source >= 0)
        def _():
            half_keys(pieces, w_ref, keys_ref, keys_t_ref, values_ref)
            base = half_base(source, blocks, n_head, crossed_half)
            mark(live_ref, told_ref, base, blocks // 2, 0)
            mark(live_ref, told_x_ref, base, blocks // 2, blocks)
            attend_all(query_ref, sums_ref, keys_t_ref, values_ref, live_ref, 0, blocks // 2)
            attend_all(query_x_ref, sums_x_ref, keys_t_ref, values_ref, live_ref, blocks, blocks // 2)

    return kernel


def make_last_kernel(back, n_head):
    def kernel(told_x_ref, *refs):
        pieces, refs = refs[: n_head // 2], refs[n_head // 2 :]
        w_ref, query_x_ref, before_ref, send_ref, keys_t_ref, values_ref, sums_ref, keys_ref, live_ref = refs
        blocks = query_x_ref.shape[0] // BLK
        source = lax.axis_index("seq") - 2 * back
        sums_ref[...] = before_ref[...]

        @pl.when(source >= 0)
        def _():
            half_keys(pieces, w_ref, keys_ref, keys_t_ref, values_ref)
            mark(live_ref, told_x_ref, half_base(source, blocks, n_head, 1), blocks // 2, 0)
            attend_all(query_x_ref, sums_ref, keys_t_ref, values_ref, live_ref, 0, blocks // 2)

        send_off(sums_ref, send_ref)

    return kernel


def make_own_last_kernel(back, n_head):
    def kernel(told_ref, query_ref, keys_t_ref, values_ref, tail_ref, unused, sums_ref, live_ref):
        rows, cols = query_ref.shape
        blocks = rows // BLK
        here = lax.axis_index("seq")
        source = here - 2 * back

        @pl.when(source >= 0)
        def _():
            mark(live_ref, told_ref, half_base(source, blocks, n_head, 1), blocks // 2, 0)
            attend_all(query_ref, sums_ref, keys_t_ref, values_ref, live_ref, 0, blocks // 2)

        farthest = here - FAR - 1

        @pl.when(farthest >= 0)
        def _():
            mark(live_ref, told_ref, farthest * blocks + blocks - 1, 1, 0)
            for h in range(cols // DH):
                at = pl.ds(h * DH, DH)
                scores = lax.dot_general(
                    query_ref[0:BLK, at], tail_ref[0, :, at], NT, preferred_element_type=jnp.float32
                )
                weights = tile(scores, live_ref[0]).astype(jnp.bfloat16)
                sums_ref[0:BLK, at] += jnp.dot(
                    weights, tail_ref[1, :, at], preferred_element_type=jnp.float32
                )

    return kernel


def finish_kernel(sums_ref, near_ref, far_ref, gate_ref, gain_ref, out_ref):
    for h in range(sums_ref.shape[1] // DH):
        at = pl.ds(h * DH, DH)
        part = centred(sums_ref[:, at])
        part = part + near_ref[:, at].astype(jnp.float32) + far_ref[:, at].astype(jnp.float32)
        off = centred(part)
        spread_sq = jnp.mean(jnp.square(off), axis=-1, keepdims=True)
        out_ref[:, at] = (
            off
            * lax.rsqrt(spread_sq + EPS)
            * gain_ref[at].reshape(1, -1).astype(jnp.float32)
            * gate_ref[:, at].astype(jnp.float32)
        ).astype(jnp.bfloat16)


def mix(total, pieces, first, w_ref):
    cols = pieces[0].shape[1]
    for m, piece in enumerate(pieces, start=first):
        at = pl.ds(pl.multiple_of((lax.axis_index("head") ^ m) * cols, cols), cols)
        total = total + jnp.dot(piece[...], w_ref[at, :], preferred_element_type=jnp.float32)
    return total


def near_out_kernel(*refs):
    *pieces, w_ref, history_ref, out_ref = refs
    cols = out_ref.shape[1]
    at = pl.ds(pl.multiple_of(lax.axis_index("head") * cols, cols), cols)
    out_ref[...] = mix(history_ref[:, at].astype(jnp.float32), pieces, 0, w_ref)


def far_out_kernel(*refs):
    *pieces, w_ref, near_ref, out_ref = refs
    out_ref[...] = mix(near_ref[...], pieces, len(pieces), w_ref).astype(jnp.bfloat16)


def crossed(array, axis, bit):
    return lax.ppermute(array, axis, [(i, i ^ bit) for i in range(lax.axis_size(axis))])


def spread(piece, bit):
    pieces = {0: piece}
    while bit:
        pieces.update({m + bit: crossed(p, "head", bit) for m, p in list(pieces.items())})
        bit //= 2
    return [pieces[m] for m in sorted(pieces)]


def whole(shape):
    return pl.BlockSpec(shape, lambda *at: (0,) * len(shape))


def body(history, ln_gain, w_in, out_gain, w_out, block_lists, counts):
    tok_rows, width = history.shape
    blocks = counts.shape[0]
    cols = w_in.shape[2]
    n_seq, n_head = lax.axis_size("seq"), lax.axis_size("head")
    assert 2 * (PLANES + 1) * blocks - (WIN - 1) == blocks - 1
    barrier = lax.optimization_barrier

    told = jnp.concatenate([block_lists, counts[:, None]], axis=1)

    shape = lambda like, n, m: jax.ShapeDtypeStruct((n, m), like)
    bf16, f32 = jnp.bfloat16, jnp.float32
    wide = pl.BlockSpec(memory_space=pltpu.VMEM)
    flat = pl.BlockSpec(memory_space=pltpu.SMEM)
    n_live = 2 * blocks * 8

    share_rows = tok_rows // n_head
    half_rows = tok_rows // 2
    steps = share_rows // 48
    share = pl.pallas_call(
        norm_kernel,
        in_specs=[pl.BlockSpec(memory_space=pl.ANY), wide],
        out_specs=wide,
        out_shape=shape(bf16, share_rows, width),
        scratch_shapes=[pltpu.VMEM((share_rows, width), bf16), pltpu.SemaphoreType.DMA((steps,))],
        cost_estimate=cost(2),
        compiler_params=params(),
    )(history, ln_gain)
    gain, share = barrier((ln_gain, share))
    upward = [(i, i + 2) for i in range(n_seq - 2)]
    share_1 = lax.ppermute(share, "seq", upward)

    part = tok_rows // 3
    gate, values, query, keys_t, tail = pl.pallas_call(
        own_kernel,
        grid=(3,),
        in_specs=[pl.BlockSpec((part, width), lambda i: (i, 0)), wide, wide],
        out_specs=[pl.BlockSpec((part, cols), lambda i: (i, 0))] * 3
        + [pl.BlockSpec((cols, part), lambda i: (0, i)), whole((2, BLK, cols))],
        out_shape=[shape(bf16, tok_rows, cols)] * 3
        + [shape(bf16, cols, tok_rows), jax.ShapeDtypeStruct((2, BLK, cols), bf16)],
        compiler_params=params(),
        cost_estimate=cost(4),
    )(history, gain, w_in)
    downward = [(i, i - FAR) for i in range(FAR + 1, n_seq, 2)]
    query_x, told_x = crossed(query, "seq", 1), crossed(told, "seq", 1)
    query_far, told_far = (lax.ppermute(a, "seq", downward) for a in (query, told))
    tail = lax.ppermute(tail, "seq", [(i, i + FAR + 1) for i in range(n_seq - FAR - 1)])
    w_mine = lax.all_to_all(w_out, "head", split_axis=1, concat_axis=0, tiled=True)

    share_1, query = barrier((share_1, query))
    share_2 = lax.ppermute(share_1, "seq", upward)
    near_1 = spread(share_1, n_head // 4)
    cross_1 = crossed(share_1, "head", n_head // 2)

    sums = pl.pallas_call(
        own_attend_kernel,
        in_specs=[flat] * 2 + [wide] * 4,
        out_specs=[wide] * 2,
        out_shape=[shape(f32, tok_rows, cols)] * 2,
        scratch_shapes=[pltpu.SMEM((n_live,), f32)],
        compiler_params=params(),
        cost_estimate=cost(4),
    )(told, told_x, query, query_x, keys_t, values)

    half_scratch = [
        pltpu.VMEM((half_rows, cols), f32),
        pltpu.VMEM((cols, half_rows), bf16),
        pltpu.VMEM((half_rows, cols), bf16),
        pltpu.SMEM((n_live,), f32),
    ]

    def half_chunk(back, crossed_half, pieces, sums):
        n = len(pieces)
        return pl.pallas_call(
            make_half_kernel(back, n_head, crossed_half),
            in_specs=[flat] * 2 + [wide] * (n + 5),
            out_specs=[wide] * 2,
            out_shape=[shape(f32, tok_rows, cols)] * 2,
            input_output_aliases={n + 5: 0, n + 6: 1},
            scratch_shapes=half_scratch,
            compiler_params=params(),
            cost_estimate=cost(4),
        )(told, told_x, *pieces, w_in, query, query_x, *sums)

    sums = half_chunk(1, 0, near_1, sums)
    share_2, sums, w_mine = barrier((share_2, tuple(sums), w_mine))
    near_2 = spread(share_2, n_head // 4)
    cross_2 = crossed(share_2, "head", n_head // 2)

    far = pl.pallas_call(
        far_kernel,
        in_specs=[flat] + [wide] * 3,
        out_specs=wide,
        out_shape=shape(bf16, tok_rows, cols),
        scratch_shapes=[pltpu.VMEM((tok_rows, cols), f32), pltpu.SMEM((n_live,), f32)],
        compiler_params=params(),
        cost_estimate=cost(2),
    )(told_far, query_far, keys_t, values)

    sums = half_chunk(1, 1, spread(cross_1, n_head // 4), sums)
    sums = half_chunk(2, 0, near_2, sums)
    cross_2, sums, far, tail = barrier((cross_2, tuple(sums), far, tail))
    far = lax.ppermute(far, "seq", [(i, i + FAR) for i in range(1, n_seq - FAR, 2)])
    pieces = spread(cross_2, n_head // 4)
    send, keys_t, values = pl.pallas_call(
        make_last_kernel(PLANES, n_head),
        in_specs=[flat] + [wide] * (len(pieces) + 3),
        out_specs=[wide] * 3,
        out_shape=[
            shape(bf16, tok_rows, cols),
            shape(bf16, cols, half_rows),
            shape(bf16, half_rows, cols),
        ],
        scratch_shapes=[
            pltpu.VMEM((tok_rows, cols), f32),
            pltpu.VMEM((half_rows, cols), f32),
            pltpu.SMEM((n_live,), f32),
        ],
        compiler_params=params(),
        cost_estimate=cost(4),
    )(told_x, *pieces, w_in, query_x, sums[1])
    near = crossed(send, "seq", 1)
    mine = pl.pallas_call(
        make_own_last_kernel(PLANES, n_head),
        in_specs=[flat] + [wide] * 5,
        out_specs=wide,
        out_shape=shape(f32, tok_rows, cols),
        input_output_aliases={5: 0},
        scratch_shapes=[pltpu.SMEM((n_live,), f32)],
        compiler_params=params(),
        cost_estimate=cost(3),
    )(told, query, keys_t, values, tail, sums[0])
    near, mine = barrier((near, mine))
    gated = pl.pallas_call(
        finish_kernel,
        in_specs=[wide] * 5,
        out_specs=wide,
        out_shape=shape(bf16, tok_rows, cols),
        compiler_params=params(),
        cost_estimate=cost(1),
    )(mine, near, far, gate, out_gain)

    out_cols = width // n_head
    cross_gated = crossed(gated, "head", n_head // 2)
    near_gated = spread(gated, n_head // 4)
    mixed = pl.pallas_call(
        near_out_kernel,
        in_specs=[wide] * (n_head // 2 + 2),
        out_specs=wide,
        out_shape=shape(f32, tok_rows, out_cols),
        compiler_params=params(),
        cost_estimate=cost(2),
    )(*near_gated, w_mine, history)
    cross_gated, mixed = barrier((cross_gated, mixed))
    return pl.pallas_call(
        far_out_kernel,
        in_specs=[wide] * (n_head // 2 + 2),
        out_specs=wide,
        out_shape=shape(bf16, tok_rows, out_cols),
        compiler_params=params(),
        cost_estimate=cost(2),
    )(*spread(cross_gated, n_head // 4), w_mine, mixed)


def solution(mesh):
    placed = (
        P("seq", None),
        P(),
        P(None, None, "head"),
        P("head"),
        P("head", None),
        P("seq", None),
        P("seq"),
    )
    return jax.shard_map(
        body, mesh=mesh, in_specs=placed, out_specs=P("seq", "head"), check_vma=False
    )
```

```python
import jax
import jax.numpy as jnp
from jax import lax
from jax.experimental import pallas as pl
from jax.experimental.pallas import tpu as pltpu
from jax.sharding import PartitionSpec as P

DH = 128
BLK = 128
WIN = 32
MAXK = 16
EPS = 1e-05
PLANES = 2
FAR = 2 * PLANES + 1
SCALE = 0.5 * DH ** (-0.5)

NT = (((1,), (1,)), ((), ()))


def params(mib=12):
    return pltpu.CompilerParams(vmem_limit_bytes=mib << 20)


def cost(us):
    return pl.CostEstimate(flops=int(us * 1e9 * 0.3), bytes_accessed=int(us * 3e6 * 0.3), transcendentals=0)


def silu(v):
    half = 0.5 * v
    return half * jnp.tanh(half) + half


def project(rows, w):
    return silu(jnp.dot(rows, w, preferred_element_type=jnp.float32))


def normed(rows, gain):
    floats = rows.astype(jnp.float32)
    centre = jnp.mean(floats, axis=-1, keepdims=True)
    off = floats - centre
    spread_sq = jnp.mean(jnp.square(off), axis=-1, keepdims=True)
    return (off * lax.rsqrt(spread_sq + EPS) * gain.astype(jnp.float32)).astype(jnp.bfloat16)


def norm_kernel(history_ref, gain_ref, out_ref, rows_ref, gain_rows_ref, sems):
    share = out_ref.shape[0]
    steps = sems.shape[0] - 1
    step = share // steps
    first = lax.axis_index("head") * share
    gain_copy = pltpu.make_async_copy(gain_ref, gain_rows_ref, sems.at[steps])
    gain_copy.start()
    copies = []
    for i in range(steps):
        at = pl.ds(pl.multiple_of(first + i * step, step), step)
        copies.append(
            pltpu.make_async_copy(history_ref.at[at], rows_ref.at[pl.ds(i * step, step)], sems.at[i])
        )
        copies[i].start()
    gain_copy.wait()
    gain = gain_rows_ref[...].reshape(1, -1)
    for i in range(steps):
        copies[i].wait()
        at = pl.ds(i * step, step)
        out_ref[at, :] = normed(rows_ref[at, :], gain)


def own_kernel(history_ref, gain_ref, w_ref, gate_ref, values_ref, query_ref, keys_t_ref, tail_ref):
    here = normed(history_ref[...], gain_ref[...].reshape(1, -1))
    query_ref[...] = project(here, w_ref[2]).astype(jnp.bfloat16)
    keys = project(here, w_ref[3])
    keys_t_ref[...] = keys.T.astype(jnp.bfloat16)
    values = project(here, w_ref[1]).astype(jnp.bfloat16)
    values_ref[...] = values
    tail_ref[0] = keys[-BLK:].astype(jnp.bfloat16)
    tail_ref[1] = values[-BLK:]
    gate_ref[...] = project(here, w_ref[0]).astype(jnp.bfloat16)


def mark(live_ref, told_ref, base, key_blocks, first):
    for b in range(told_ref.shape[0]):
        for g in range(key_blocks):
            live_ref[(first + b) * 8 + g] = 0.0

        def entry(t, unused):
            g = told_ref[b, t] - base
            live_ref[(first + b) * 8 + jnp.where((g >= 0) & (g < key_blocks), g, 7)] = SCALE
            return unused

        lax.fori_loop(0, told_ref[b, MAXK], entry, 0)


def tile(scores, factor):
    half = scores * factor
    return half * jnp.tanh(half) + half


def attend_dense(query_ref, rows, sums_ref, keys_t_ref, values_ref, factors):
    n, blocks = len(factors), len(factors[0])
    for h in range(query_ref.shape[1] // DH):
        cols = pl.ds(h * DH, DH)
        scores = jnp.dot(
            query_ref[rows, cols], keys_t_ref[cols, :], preferred_element_type=jnp.float32
        )
        weights = [
            jnp.concatenate(
                [
                    tile(scores[i * BLK : (i + 1) * BLK, g * BLK : (g + 1) * BLK], factors[i][g])
                    for i in range(n)
                ],
                axis=0,
            ).astype(jnp.bfloat16)
            for g in range(blocks)
        ]
        sums_ref[rows, cols] += jnp.dot(
            jnp.concatenate(weights, axis=1), values_ref[:, cols], preferred_element_type=jnp.float32
        )


def attend_all(query_ref, sums_ref, keys_t_ref, values_ref, live_ref, live_first, key_blocks):
    n = 2

    def some(p, unused):
        factors = [
            [live_ref[(live_first + n * p + i) * 8 + g] for g in range(key_blocks)] for i in range(n)
        ]

        @pl.when(sum(sum(f) for f in factors) > 0.0)
        def _():
            rows = pl.ds(pl.multiple_of(p * n * BLK, n * BLK), n * BLK)
            attend_dense(query_ref, rows, sums_ref, keys_t_ref, values_ref, factors)

        return unused

    lax.fori_loop(0, query_ref.shape[0] // (n * BLK), some, 0)


def own_attend_kernel(
    told_ref, told_x_ref, query_ref, query_x_ref, keys_t_ref, values_ref, sums_ref, sums_x_ref, live_ref
):
    rows, cols = query_ref.shape
    blocks = rows // BLK
    here = lax.axis_index("seq")
    mark(live_ref, told_ref, here * blocks, blocks, 0)
    mark(live_ref, told_x_ref, here * blocks, blocks, blocks)
    sums_x_ref[...] = jnp.zeros((rows, cols), jnp.float32)
    behind = lax.broadcasted_iota(jnp.int32, (BLK, BLK), 1) <= lax.broadcasted_iota(
        jnp.int32, (BLK, BLK), 0
    )
    for p in range(blocks // 2):
        q_rows = pl.ds(p * 2 * BLK, 2 * BLK)
        seen = pl.ds(0, (2 * p + 2) * BLK)
        for h in range(cols // DH):
            at = pl.ds(h * DH, DH)
            scores = jnp.dot(
                query_ref[q_rows, at], keys_t_ref[at, seen], preferred_element_type=jnp.float32
            )
            weights = []
            for g in range(2 * p + 2):
                column = []
                for i in range(2):
                    b = 2 * p + i
                    if g > b:
                        column.append(jnp.zeros((BLK, BLK), jnp.float32))
                        continue
                    part = tile(
                        scores[i * BLK : (i + 1) * BLK, g * BLK : (g + 1) * BLK], live_ref[b * 8 + g]
                    )
                    column.append(jnp.where(behind, part, 0.0) if g == b else part)
                weights.append(jnp.concatenate(column, axis=0).astype(jnp.bfloat16))
            sums_ref[q_rows, at] = jnp.dot(
                jnp.concatenate(weights, axis=1),
                values_ref[seen, at],
                preferred_element_type=jnp.float32,
            )
    attend_all(query_x_ref, sums_x_ref, keys_t_ref, values_ref, live_ref, blocks, blocks)


def centred(part):
    return part - jnp.mean(part, axis=-1, keepdims=True)


def send_off(sums_ref, send_ref):
    for h in range(send_ref.shape[1] // DH):
        at = pl.ds(h * DH, DH)
        send_ref[:, at] = centred(sums_ref[:, at]).astype(jnp.bfloat16)


def far_kernel(told_ref, query_ref, keys_t_ref, values_ref, send_ref, sums_ref, live_ref):
    blocks = query_ref.shape[0] // BLK
    here = lax.axis_index("seq")

    @pl.when((here % 2 == 1) & (here + FAR < lax.axis_size("seq")))
    def _():
        mark(live_ref, told_ref, here * blocks, blocks, 0)
        sums_ref[...] = jnp.zeros_like(sums_ref)
        attend_all(query_ref, sums_ref, keys_t_ref, values_ref, live_ref, 0, blocks)
        send_off(sums_ref, send_ref)


def chunk_keys(pieces, w_ref, keys_ref, keys_t_ref, values_ref):
    share = pieces[0].shape[0]
    for m, piece in enumerate(pieces):
        at = pl.ds(pl.multiple_of((lax.axis_index("head") ^ m) * share, share), share)
        keys_ref[at, :] = project(piece[...], w_ref[3])
        values_ref[at, :] = project(piece[...], w_ref[1]).astype(jnp.bfloat16)
    keys_t_ref[...] = keys_ref[...].T.astype(jnp.bfloat16)


def make_chunk_kernel(back, n_head):
    def kernel(told_ref, told_x_ref, *refs):
        pieces, refs = refs[:n_head], refs[n_head:]
        w_ref, query_ref, query_x_ref, unused, unused_x = refs[:5]
        sums_ref, sums_x_ref, keys_ref, keys_t_ref, values_ref, live_ref = refs[5:]
        blocks = query_ref.shape[0] // BLK
        source = lax.axis_index("seq") - 2 * back

        @pl.when(source >= 0)
        def _():
            chunk_keys(pieces, w_ref, keys_ref, keys_t_ref, values_ref)
            mark(live_ref, told_ref, source * blocks, blocks, 0)
            mark(live_ref, told_x_ref, source * blocks, blocks, blocks)
            attend_all(query_ref, sums_ref, keys_t_ref, values_ref, live_ref, 0, blocks)
            attend_all(query_x_ref, sums_x_ref, keys_t_ref, values_ref, live_ref, blocks, blocks)

    return kernel


def make_last_kernel(back, n_head):
    def kernel(told_x_ref, *refs):
        pieces, refs = refs[:n_head], refs[n_head:]
        w_ref, query_x_ref, before_ref, send_ref, keys_t_ref, values_ref, sums_ref, keys_ref, live_ref = refs
        blocks = query_x_ref.shape[0] // BLK
        source = lax.axis_index("seq") - 2 * back
        sums_ref[...] = before_ref[...]

        @pl.when(source >= 0)
        def _():
            chunk_keys(pieces, w_ref, keys_ref, keys_t_ref, values_ref)
            mark(live_ref, told_x_ref, source * blocks, blocks, 0)
            attend_all(query_x_ref, sums_ref, keys_t_ref, values_ref, live_ref, 0, blocks)

        send_off(sums_ref, send_ref)

    return kernel


def make_own_last_kernel(back):
    def kernel(told_ref, query_ref, keys_t_ref, values_ref, tail_ref, unused, sums_ref, live_ref):
        rows, cols = query_ref.shape
        blocks = rows // BLK
        here = lax.axis_index("seq")
        source = here - 2 * back

        @pl.when(source >= 0)
        def _():
            mark(live_ref, told_ref, source * blocks, blocks, 0)
            attend_all(query_ref, sums_ref, keys_t_ref, values_ref, live_ref, 0, blocks)

        farthest = here - FAR - 1

        @pl.when(farthest >= 0)
        def _():
            mark(live_ref, told_ref, farthest * blocks + blocks - 1, 1, 0)
            for h in range(cols // DH):
                at = pl.ds(h * DH, DH)
                scores = lax.dot_general(
                    query_ref[0:BLK, at], tail_ref[0, :, at], NT, preferred_element_type=jnp.float32
                )
                weights = tile(scores, live_ref[0]).astype(jnp.bfloat16)
                sums_ref[0:BLK, at] += jnp.dot(
                    weights, tail_ref[1, :, at], preferred_element_type=jnp.float32
                )

    return kernel


def finish_kernel(sums_ref, near_ref, far_ref, gate_ref, gain_ref, out_ref):
    for h in range(sums_ref.shape[1] // DH):
        at = pl.ds(h * DH, DH)
        part = centred(sums_ref[:, at])
        part = part + near_ref[:, at].astype(jnp.float32) + far_ref[:, at].astype(jnp.float32)
        off = centred(part)
        spread_sq = jnp.mean(jnp.square(off), axis=-1, keepdims=True)
        out_ref[:, at] = (
            off
            * lax.rsqrt(spread_sq + EPS)
            * gain_ref[at].reshape(1, -1).astype(jnp.float32)
            * gate_ref[:, at].astype(jnp.float32)
        ).astype(jnp.bfloat16)


def mix(total, pieces, first, w_ref):
    cols = pieces[0].shape[1]
    for m, piece in enumerate(pieces, start=first):
        at = pl.ds(pl.multiple_of((lax.axis_index("head") ^ m) * cols, cols), cols)
        total = total + jnp.dot(piece[...], w_ref[at, :], preferred_element_type=jnp.float32)
    return total


def near_out_kernel(*refs):
    *pieces, w_ref, history_ref, out_ref = refs
    cols = out_ref.shape[1]
    at = pl.ds(pl.multiple_of(lax.axis_index("head") * cols, cols), cols)
    out_ref[...] = mix(history_ref[:, at].astype(jnp.float32), pieces, 0, w_ref)


def far_out_kernel(*refs):
    *pieces, w_ref, near_ref, out_ref = refs
    out_ref[...] = mix(near_ref[...], pieces, len(pieces), w_ref).astype(jnp.bfloat16)


def crossed(array, axis, bit):
    return lax.ppermute(array, axis, [(i, i ^ bit) for i in range(lax.axis_size(axis))])


def spread(piece, bit):
    pieces = {0: piece}
    while bit:
        pieces.update({m + bit: crossed(p, "head", bit) for m, p in list(pieces.items())})
        bit //= 2
    return [pieces[m] for m in sorted(pieces)]


def whole(shape):
    return pl.BlockSpec(shape, lambda *at: (0,) * len(shape))


def body(history, ln_gain, w_in, out_gain, w_out, block_lists, counts):
    tok_rows, width = history.shape
    blocks = counts.shape[0]
    cols = w_in.shape[2]
    n_seq, n_head = lax.axis_size("seq"), lax.axis_size("head")
    assert 2 * (PLANES + 1) * blocks - (WIN - 1) == blocks - 1
    barrier = lax.optimization_barrier

    told = jnp.concatenate([block_lists, counts[:, None]], axis=1)

    shape = lambda like, n, m: jax.ShapeDtypeStruct((n, m), like)
    bf16, f32 = jnp.bfloat16, jnp.float32
    wide = pl.BlockSpec(memory_space=pltpu.VMEM)
    flat = pl.BlockSpec(memory_space=pltpu.SMEM)
    n_live = 2 * blocks * 8

    share_rows = tok_rows // n_head
    steps = share_rows // 48
    share = pl.pallas_call(
        norm_kernel,
        in_specs=[pl.BlockSpec(memory_space=pltpu.HBM)] * 2,
        out_specs=wide,
        out_shape=shape(bf16, share_rows, width),
        scratch_shapes=[
            pltpu.VMEM((share_rows, width), bf16),
            pltpu.VMEM((width,), bf16),
            pltpu.SemaphoreType.DMA((steps + 1,)),
        ],
        cost_estimate=cost(2),
        compiler_params=params(),
    )(history, ln_gain)
    gain, share = barrier((ln_gain, share))
    upward = [(i, i + 2) for i in range(n_seq - 2)]
    share_1 = lax.ppermute(share, "seq", upward)

    part = tok_rows // 3
    gate, values, query, keys_t, tail = pl.pallas_call(
        own_kernel,
        grid=(3,),
        in_specs=[pl.BlockSpec((part, width), lambda i: (i, 0)), wide, wide],
        out_specs=[pl.BlockSpec((part, cols), lambda i: (i, 0))] * 3
        + [pl.BlockSpec((cols, part), lambda i: (0, i)), whole((2, BLK, cols))],
        out_shape=[shape(bf16, tok_rows, cols)] * 3
        + [shape(bf16, cols, tok_rows), jax.ShapeDtypeStruct((2, BLK, cols), bf16)],
        compiler_params=params(),
        cost_estimate=cost(4),
    )(history, gain, w_in)
    downward = [(i, i - FAR) for i in range(FAR + 1, n_seq, 2)]
    query_x, told_x = crossed(query, "seq", 1), crossed(told, "seq", 1)
    query_far, told_far = (lax.ppermute(a, "seq", downward) for a in (query, told))
    tail = lax.ppermute(tail, "seq", [(i, i + FAR + 1) for i in range(n_seq - FAR - 1)])
    w_mine = lax.all_to_all(w_out, "head", split_axis=1, concat_axis=0, tiled=True)

    share_1, query, w_mine = barrier((share_1, query, w_mine))
    share_2 = lax.ppermute(share_1, "seq", upward)
    chunk_1 = spread(share_1, n_head // 2)

    sums = pl.pallas_call(
        own_attend_kernel,
        in_specs=[flat] * 2 + [wide] * 4,
        out_specs=[wide] * 2,
        out_shape=[shape(f32, tok_rows, cols)] * 2,
        scratch_shapes=[pltpu.SMEM((n_live,), f32)],
        compiler_params=params(),
        cost_estimate=cost(4),
    )(told, told_x, query, query_x, keys_t, values)

    share_2, sums = barrier((share_2, tuple(sums)))
    cross_2 = crossed(share_2, "head", n_head // 2)
    near_2 = spread(share_2, n_head // 4)

    keys_shapes = [(tok_rows, cols), (cols, tok_rows), (tok_rows, cols)]
    sums = pl.pallas_call(
        make_chunk_kernel(1, n_head),
        in_specs=[flat] * 2 + [wide] * (n_head + 5),
        out_specs=[wide] * 2,
        out_shape=[shape(f32, tok_rows, cols)] * 2,
        input_output_aliases={n_head + 5: 0, n_head + 6: 1},
        scratch_shapes=[
            pltpu.VMEM(dims, kind) for dims, kind in zip(keys_shapes, (f32, bf16, bf16))
        ]
        + [pltpu.SMEM((n_live,), f32)],
        compiler_params=params(),
        cost_estimate=cost(4),
    )(told, told_x, *chunk_1, w_in, query, query_x, *sums)

    far = pl.pallas_call(
        far_kernel,
        in_specs=[flat] + [wide] * 3,
        out_specs=wide,
        out_shape=shape(bf16, tok_rows, cols),
        scratch_shapes=[pltpu.VMEM((tok_rows, cols), f32), pltpu.SMEM((n_live,), f32)],
        compiler_params=params(),
        cost_estimate=cost(2),
    )(told_far, query_far, keys_t, values)

    cross_2, sums, far, tail = barrier((cross_2, tuple(sums), far, tail))
    far = lax.ppermute(far, "seq", [(i, i + FAR) for i in range(1, n_seq - FAR, 2)])
    send, keys_t, values = pl.pallas_call(
        make_last_kernel(PLANES, n_head),
        in_specs=[flat] + [wide] * (n_head + 3),
        out_specs=[wide] * 3,
        out_shape=[shape(bf16, *dims) for dims in (keys_shapes[0], *keys_shapes[1:])],
        scratch_shapes=[
            pltpu.VMEM((tok_rows, cols), f32),
            pltpu.VMEM((tok_rows, cols), f32),
            pltpu.SMEM((n_live,), f32),
        ],
        compiler_params=params(),
        cost_estimate=cost(4),
    )(told_x, *near_2, *spread(cross_2, n_head // 4), w_in, query_x, sums[1])
    near = crossed(send, "seq", 1)
    mine = pl.pallas_call(
        make_own_last_kernel(PLANES),
        in_specs=[flat] + [wide] * 5,
        out_specs=wide,
        out_shape=shape(f32, tok_rows, cols),
        input_output_aliases={5: 0},
        scratch_shapes=[pltpu.SMEM((n_live,), f32)],
        compiler_params=params(),
        cost_estimate=cost(3),
    )(told, query, keys_t, values, tail, sums[0])
    near, mine = barrier((near, mine))
    gated = pl.pallas_call(
        finish_kernel,
        in_specs=[wide] * 5,
        out_specs=wide,
        out_shape=shape(bf16, tok_rows, cols),
        compiler_params=params(),
        cost_estimate=cost(1),
    )(mine, near, far, gate, out_gain)

    out_cols = width // n_head
    cross_gated = crossed(gated, "head", n_head // 2)
    near_gated = spread(gated, n_head // 4)
    mixed = pl.pallas_call(
        near_out_kernel,
        in_specs=[wide] * (n_head // 2 + 2),
        out_specs=wide,
        out_shape=shape(f32, tok_rows, out_cols),
        compiler_params=params(),
        cost_estimate=cost(2),
    )(*near_gated, w_mine, history)
    cross_gated, mixed = barrier((cross_gated, mixed))
    return pl.pallas_call(
        far_out_kernel,
        in_specs=[wide] * (n_head // 2 + 2),
        out_specs=wide,
        out_shape=shape(bf16, tok_rows, out_cols),
        compiler_params=params(),
        cost_estimate=cost(2),
    )(*spread(cross_gated, n_head // 4), w_mine, mixed)


def solution(mesh):
    placed = (
        P("seq", None),
        P(),
        P(None, None, "head"),
        P("head"),
        P("head", None),
        P("seq", None),
        P("seq"),
    )
    return jax.shard_map(
        body, mesh=mesh, in_specs=placed, out_specs=P("seq", "head"), check_vma=False
    )
```

```python
import jax
import jax.numpy as jnp
from jax import lax
from jax.experimental import pallas as pl
from jax.experimental.pallas import tpu as pltpu
from jax.sharding import PartitionSpec as P

DH = 128
BLK = 128
WIN = 32
MAXK = 16
EPS = 1e-05
PLANES = 2
FAR = 2 * PLANES + 1
SCALE = 0.5 * DH ** (-0.5)

NT = (((1,), (1,)), ((), ()))


def params(mib=12):
    return pltpu.CompilerParams(vmem_limit_bytes=mib << 20)


def cost(us):
    return pl.CostEstimate(flops=int(us * 1e9 * 0.3), bytes_accessed=int(us * 3e6 * 0.3), transcendentals=0)


def silu(v):
    half = 0.5 * v
    return half * jnp.tanh(half) + half


def project(rows, w):
    return silu(jnp.dot(rows, w, preferred_element_type=jnp.float32))


def normed(rows, gain):
    floats = rows.astype(jnp.float32)
    centre = jnp.mean(floats, axis=-1, keepdims=True)
    off = floats - centre
    spread_sq = jnp.mean(jnp.square(off), axis=-1, keepdims=True)
    return (off * lax.rsqrt(spread_sq + EPS) * gain.astype(jnp.float32)).astype(jnp.bfloat16)


def norm_kernel(history_ref, gain_ref, out_ref, rows_ref, gain_rows_ref, sems):
    share = out_ref.shape[0]
    steps = sems.shape[0] - 1
    step = share // steps
    first = lax.axis_index("head") * share
    gain_copy = pltpu.make_async_copy(gain_ref, gain_rows_ref, sems.at[steps])
    gain_copy.start()
    copies = []
    for i in range(steps):
        at = pl.ds(pl.multiple_of(first + i * step, step), step)
        copies.append(
            pltpu.make_async_copy(history_ref.at[at], rows_ref.at[pl.ds(i * step, step)], sems.at[i])
        )
        copies[i].start()
    gain_copy.wait()
    gain = gain_rows_ref[...].reshape(1, -1)
    for i in range(steps):
        copies[i].wait()
        at = pl.ds(i * step, step)
        out_ref[at, :] = normed(rows_ref[at, :], gain)


def mark(live_ref, told_ref, base, key_blocks, first):
    for b in range(told_ref.shape[0]):
        for g in range(key_blocks):
            live_ref[(first + b) * 8 + g] = 0.0

        def entry(t, unused):
            g = told_ref[b, t] - base
            live_ref[(first + b) * 8 + jnp.where((g >= 0) & (g < key_blocks), g, 7)] = SCALE
            return unused

        lax.fori_loop(0, told_ref[b, MAXK], entry, 0)


def tile(scores, factor):
    half = scores * factor
    return half * jnp.tanh(half) + half


def attend_dense(query_ref, rows, sums_ref, keys_t_ref, values_ref, factors):
    n, blocks = len(factors), len(factors[0])
    for h in range(query_ref.shape[1] // DH):
        cols = pl.ds(h * DH, DH)
        scores = jnp.dot(
            query_ref[rows, cols], keys_t_ref[cols, :], preferred_element_type=jnp.float32
        )
        weights = [
            jnp.concatenate(
                [
                    tile(scores[i * BLK : (i + 1) * BLK, g * BLK : (g + 1) * BLK], factors[i][g])
                    for i in range(n)
                ],
                axis=0,
            ).astype(jnp.bfloat16)
            for g in range(blocks)
        ]
        sums_ref[rows, cols] += jnp.dot(
            jnp.concatenate(weights, axis=1), values_ref[:, cols], preferred_element_type=jnp.float32
        )


def attend_all(query_ref, sums_ref, keys_t_ref, values_ref, live_ref, live_first, key_blocks):
    n = 2

    def some(p, unused):
        factors = [
            [live_ref[(live_first + n * p + i) * 8 + g] for g in range(key_blocks)] for i in range(n)
        ]

        @pl.when(sum(sum(f) for f in factors) > 0.0)
        def _():
            rows = pl.ds(pl.multiple_of(p * n * BLK, n * BLK), n * BLK)
            attend_dense(query_ref, rows, sums_ref, keys_t_ref, values_ref, factors)

        return unused

    lax.fori_loop(0, query_ref.shape[0] // (n * BLK), some, 0)


def fetch(pairs, sems):
    copies = [pltpu.make_async_copy(a, b, sems.at[i]) for i, (a, b) in enumerate(pairs)]
    for copy in copies:
        copy.start()
    return copies


def wait(copies):
    for copy in copies:
        copy.wait()


def own_kernel(
    told_ref, history_hbm, gain_hbm, w_ref,
    gate_hbm, values_hbm, query_hbm, keys_t_hbm, tail_hbm, sums_hbm,
    history_ref, gain_ref, gate_ref, values_ref, query_ref, keys_t_ref, tail_ref, sums_ref, live_ref, sems, out_sems,
):
    rows, cols = query_ref.shape
    blocks = rows // BLK
    part = 2 * BLK
    parts = [pl.ds(p * part, part) for p in range(rows // part)]
    gain_copy, *copies = fetch(
        [(gain_hbm, gain_ref)] + [(history_hbm.at[at], history_ref.at[at]) for at in parts], sems
    )
    mark(live_ref, told_ref, lax.axis_index("seq") * blocks, blocks, 0)
    gain_copy.wait()
    gain = gain_ref[...].reshape(1, -1)
    for at, copy in zip(parts, copies):
        copy.wait()
        here = normed(history_ref[at, :], gain)
        query_ref[at, :] = project(here, w_ref[2]).astype(jnp.bfloat16)
        keys = project(here, w_ref[3])
        keys_t_ref[:, at] = keys.T.astype(jnp.bfloat16)
        values = project(here, w_ref[1]).astype(jnp.bfloat16)
        values_ref[at, :] = values
        gate_ref[at, :] = project(here, w_ref[0]).astype(jnp.bfloat16)
    tail_ref[0] = keys[-BLK:].astype(jnp.bfloat16)
    tail_ref[1] = values[-BLK:]
    done = [
        (query_ref, query_hbm), (values_ref, values_hbm), (keys_t_ref, keys_t_hbm),
        (gate_ref, gate_hbm), (tail_ref, tail_hbm), (sums_ref, sums_hbm),
    ]
    out = fetch(done[:-1], out_sems)
    behind = lax.broadcasted_iota(jnp.int32, (BLK, BLK), 1) <= lax.broadcasted_iota(
        jnp.int32, (BLK, BLK), 0
    )
    for p in range(blocks // 2):
        q_rows = pl.ds(p * 2 * BLK, 2 * BLK)
        seen = pl.ds(0, (2 * p + 2) * BLK)
        for h in range(cols // DH):
            at = pl.ds(h * DH, DH)
            scores = jnp.dot(
                query_ref[q_rows, at], keys_t_ref[at, seen], preferred_element_type=jnp.float32
            )
            weights = []
            for g in range(2 * p + 2):
                column = []
                for i in range(2):
                    b = 2 * p + i
                    if g > b:
                        column.append(jnp.zeros((BLK, BLK), jnp.float32))
                        continue
                    some = tile(
                        scores[i * BLK : (i + 1) * BLK, g * BLK : (g + 1) * BLK], live_ref[b * 8 + g]
                    )
                    column.append(jnp.where(behind, some, 0.0) if g == b else some)
                weights.append(jnp.concatenate(column, axis=0).astype(jnp.bfloat16))
            sums_ref[q_rows, at] = jnp.dot(
                jnp.concatenate(weights, axis=1),
                values_ref[seen, at],
                preferred_element_type=jnp.float32,
            )
    last = pltpu.make_async_copy(sums_ref, sums_hbm, out_sems.at[len(done) - 1])
    last.start()
    wait(out + [last])


def centred(part):
    return part - jnp.mean(part, axis=-1, keepdims=True)


def send_off(sums_ref, send_ref):
    for h in range(send_ref.shape[1] // DH):
        at = pl.ds(h * DH, DH)
        send_ref[:, at] = centred(sums_ref[:, at]).astype(jnp.bfloat16)


def far_kernel(
    told_ref, query_ref, keys_t_hbm, values_hbm, send_ref, keys_t_ref, values_ref, sums_ref, live_ref, sems
):
    blocks = query_ref.shape[0] // BLK
    here = lax.axis_index("seq")

    @pl.when((here % 2 == 1) & (here + FAR < lax.axis_size("seq")))
    def _():
        copies = fetch([(keys_t_hbm, keys_t_ref), (values_hbm, values_ref)], sems)
        mark(live_ref, told_ref, here * blocks, blocks, 0)
        sums_ref[...] = jnp.zeros_like(sums_ref)
        wait(copies)
        attend_all(query_ref, sums_ref, keys_t_ref, values_ref, live_ref, 0, blocks)
        send_off(sums_ref, send_ref)


def chunk_keys(pieces, w_ref, keys_ref, keys_t_ref, values_ref):
    share = pieces[0].shape[0]
    for m, piece in enumerate(pieces):
        at = pl.ds(pl.multiple_of((lax.axis_index("head") ^ m) * share, share), share)
        keys_ref[at, :] = project(piece[...], w_ref[3])
        values_ref[at, :] = project(piece[...], w_ref[1]).astype(jnp.bfloat16)
    keys_t_ref[...] = keys_ref[...].T.astype(jnp.bfloat16)


def make_chunk_kernel(back, n_head):
    def kernel(told_ref, told_x_ref, *refs):
        pieces, refs = refs[:n_head], refs[n_head:]
        w_ref, query_hbm, query_x_hbm, own_t_hbm, own_values_hbm, before_hbm, sums_hbm, sums_x_hbm = refs[:8]
        query_ref, query_x_ref, own_t_ref, own_values_ref, sums_ref, sums_x_ref = refs[8:14]
        keys_ref, keys_t_ref, values_ref, live_ref, sems, out_sems = refs[14:]
        blocks = query_ref.shape[0] // BLK
        here = lax.axis_index("seq")
        source = here - 2 * back
        copies = fetch(
            [
                (query_x_hbm, query_x_ref), (own_t_hbm, own_t_ref), (own_values_hbm, own_values_ref),
                (before_hbm, sums_ref), (query_hbm, query_ref),
            ],
            sems,
        )
        sums_x_ref[...] = jnp.zeros_like(sums_x_ref)
        mark(live_ref, told_x_ref, here * blocks, blocks, 0)

        @pl.when(source >= 0)
        def _():
            chunk_keys(pieces, w_ref, keys_ref, keys_t_ref, values_ref)

        wait(copies)
        attend_all(query_x_ref, sums_x_ref, own_t_ref, own_values_ref, live_ref, 0, blocks)

        @pl.when(source >= 0)
        def _():
            mark(live_ref, told_ref, source * blocks, blocks, 0)
            mark(live_ref, told_x_ref, source * blocks, blocks, blocks)
            attend_all(query_ref, sums_ref, keys_t_ref, values_ref, live_ref, 0, blocks)
            attend_all(query_x_ref, sums_x_ref, keys_t_ref, values_ref, live_ref, blocks, blocks)

        wait(fetch([(sums_ref, sums_hbm), (sums_x_ref, sums_x_hbm)], out_sems))

    return kernel


def make_last_kernel(back, n_head):
    def kernel(told_x_ref, *refs):
        pieces, refs = refs[:n_head], refs[n_head:]
        w_ref, query_x_hbm, before_hbm, send_ref, keys_t_ref, values_ref = refs[:6]
        query_x_ref, sums_ref, keys_ref, live_ref, sems = refs[6:]
        blocks = query_x_ref.shape[0] // BLK
        source = lax.axis_index("seq") - 2 * back
        copies = fetch([(query_x_hbm, query_x_ref), (before_hbm, sums_ref)], sems)

        @pl.when(source >= 0)
        def _():
            chunk_keys(pieces, w_ref, keys_ref, keys_t_ref, values_ref)
            mark(live_ref, told_x_ref, source * blocks, blocks, 0)

        wait(copies)

        @pl.when(source >= 0)
        def _():
            attend_all(query_x_ref, sums_ref, keys_t_ref, values_ref, live_ref, 0, blocks)

        send_off(sums_ref, send_ref)

    return kernel


def make_own_last_kernel(back):
    def kernel(
        told_ref, query_hbm, keys_t_ref, values_ref, tail_ref, before_hbm, sums_ref, query_ref, live_ref, sems
    ):
        rows, cols = query_ref.shape
        blocks = rows // BLK
        here = lax.axis_index("seq")
        source = here - 2 * back
        copies = fetch([(query_hbm, query_ref), (before_hbm, sums_ref)], sems)
        mark(live_ref, told_ref, source * blocks, blocks, 0)
        wait(copies)

        @pl.when(source >= 0)
        def _():
            attend_all(query_ref, sums_ref, keys_t_ref, values_ref, live_ref, 0, blocks)

        farthest = here - FAR - 1

        @pl.when(farthest >= 0)
        def _():
            mark(live_ref, told_ref, farthest * blocks + blocks - 1, 1, 0)
            for h in range(cols // DH):
                at = pl.ds(h * DH, DH)
                scores = lax.dot_general(
                    query_ref[0:BLK, at], tail_ref[0, :, at], NT, preferred_element_type=jnp.float32
                )
                weights = tile(scores, live_ref[0]).astype(jnp.bfloat16)
                sums_ref[0:BLK, at] += jnp.dot(
                    weights, tail_ref[1, :, at], preferred_element_type=jnp.float32
                )

    return kernel


def finish_kernel(sums_ref, near_ref, far_ref, gate_ref, gain_ref, out_ref):
    for h in range(sums_ref.shape[1] // DH):
        at = pl.ds(h * DH, DH)
        part = centred(sums_ref[:, at])
        part = part + near_ref[:, at].astype(jnp.float32) + far_ref[:, at].astype(jnp.float32)
        off = centred(part)
        spread_sq = jnp.mean(jnp.square(off), axis=-1, keepdims=True)
        out_ref[:, at] = (
            off
            * lax.rsqrt(spread_sq + EPS)
            * gain_ref[at].reshape(1, -1).astype(jnp.float32)
            * gate_ref[:, at].astype(jnp.float32)
        ).astype(jnp.bfloat16)


def mix(total, pieces, first, w_ref):
    cols = pieces[0].shape[1]
    for m, piece in enumerate(pieces, start=first):
        at = pl.ds(pl.multiple_of((lax.axis_index("head") ^ m) * cols, cols), cols)
        total = total + jnp.dot(piece[...], w_ref[at, :], preferred_element_type=jnp.float32)
    return total


def near_out_kernel(*refs):
    *pieces, w_ref, history_hbm, out_ref, history_ref, sem = refs
    cols = out_ref.shape[1]
    at = pl.ds(pl.multiple_of(lax.axis_index("head") * cols, cols), cols)
    copy = pltpu.make_async_copy(history_hbm.at[:, at], history_ref, sem)
    copy.start()
    total = mix(jnp.zeros(out_ref.shape, jnp.float32), pieces, 0, w_ref)
    copy.wait()
    out_ref[...] = total + history_ref[...].astype(jnp.float32)


def far_out_kernel(*refs):
    *pieces, w_ref, near_ref, out_ref = refs
    out_ref[...] = mix(near_ref[...], pieces, len(pieces), w_ref).astype(jnp.bfloat16)


def crossed(array, axis, bit):
    return lax.ppermute(array, axis, [(i, i ^ bit) for i in range(lax.axis_size(axis))])


def spread(piece, bit):
    pieces = {0: piece}
    while bit:
        pieces.update({m + bit: crossed(p, "head", bit) for m, p in list(pieces.items())})
        bit //= 2
    return [pieces[m] for m in sorted(pieces)]


def body(history, ln_gain, w_in, out_gain, w_out, block_lists, counts):
    tok_rows, width = history.shape
    blocks = counts.shape[0]
    cols = w_in.shape[2]
    n_seq, n_head = lax.axis_size("seq"), lax.axis_size("head")
    assert 2 * (PLANES + 1) * blocks - (WIN - 1) == blocks - 1
    barrier = lax.optimization_barrier

    shape = lambda like, *dims: jax.ShapeDtypeStruct(dims, like)
    bf16, f32 = jnp.bfloat16, jnp.float32
    wide = pl.BlockSpec(memory_space=pltpu.VMEM)
    flat = pl.BlockSpec(memory_space=pltpu.SMEM)
    far_off = pl.BlockSpec(memory_space=pltpu.HBM)
    n_live = 2 * blocks * 8
    upright, lying = (tok_rows, cols), (cols, tok_rows)
    sems = lambda n: pltpu.SemaphoreType.DMA((n,))
    live = pltpu.SMEM((n_live,), f32)

    told = jnp.concatenate([block_lists, counts[:, None]], axis=1)
    share_rows = tok_rows // n_head
    steps = share_rows // 48
    share = pl.pallas_call(
        norm_kernel,
        in_specs=[far_off] * 2,
        out_specs=wide,
        out_shape=shape(bf16, share_rows, width),
        scratch_shapes=[
            pltpu.VMEM((share_rows, width), bf16),
            pltpu.VMEM((width,), bf16),
            sems(steps + 1),
        ],
        cost_estimate=cost(2),
        compiler_params=params(60),
    )(history, ln_gain)
    gain, told, share = barrier((ln_gain, told, share))
    upward = [(i, i + 2) for i in range(n_seq - 2)]
    downward = [(i, i - FAR) for i in range(FAR + 1, n_seq, 2)]
    share_1 = lax.ppermute(share, "seq", upward)
    told_x = crossed(told, "seq", 1)
    told_far = lax.ppermute(told, "seq", downward)

    gate, values, query, keys_t, tail, own_sums = pl.pallas_call(
        own_kernel,
        in_specs=[flat, far_off, far_off, wide],
        out_specs=[far_off] * 6,
        out_shape=[shape(bf16, *upright)] * 3
        + [shape(bf16, *lying), shape(bf16, 2, BLK, cols), shape(f32, *upright)],
        scratch_shapes=[pltpu.VMEM((tok_rows, width), bf16), pltpu.VMEM((width,), bf16)]
        + [pltpu.VMEM(upright, bf16)] * 3
        + [pltpu.VMEM(lying, bf16), pltpu.VMEM((2, BLK, cols), bf16), pltpu.VMEM(upright, f32), live]
        + [sems(1 + tok_rows // (2 * BLK)), sems(6)],
        compiler_params=params(),
        cost_estimate=cost(6),
    )(told, history, gain, w_in)
    query_x = crossed(query, "seq", 1)

    share_1, query, told_x, told_far = barrier((share_1, query, told_x, told_far))
    share_2 = lax.ppermute(share_1, "seq", upward)
    chunk_1 = spread(share_1, n_head // 2)
    query_far = lax.ppermute(query, "seq", downward)
    tail = lax.ppermute(tail, "seq", [(i, i + FAR + 1) for i in range(n_seq - FAR - 1)])
    cross_2 = crossed(share_2, "head", n_head // 2)
    near_2 = spread(share_2, n_head // 4)

    far = pl.pallas_call(
        far_kernel,
        in_specs=[flat, wide, far_off, far_off],
        out_specs=wide,
        out_shape=shape(bf16, *upright),
        scratch_shapes=[
            pltpu.VMEM(lying, bf16), pltpu.VMEM(upright, bf16), pltpu.VMEM(upright, f32), live, sems(2)
        ],
        compiler_params=params(),
        cost_estimate=cost(2),
    )(told_far, query_far, keys_t, values)

    sums, sums_x = pl.pallas_call(
        make_chunk_kernel(1, n_head),
        in_specs=[flat] * 2 + [wide] * (n_head + 1) + [far_off] * 5,
        out_specs=[far_off] * 2,
        out_shape=[shape(f32, *upright)] * 2,
        scratch_shapes=[
            pltpu.VMEM(dims, kind)
            for dims, kind in (
                (upright, bf16), (upright, bf16), (lying, bf16), (upright, bf16), (upright, f32),
                (upright, f32), (upright, f32), (lying, bf16), (upright, bf16),
            )
        ]
        + [live, sems(5), sems(2)],
        compiler_params=params(16),
        cost_estimate=cost(6),
    )(told, told_x, *chunk_1, w_in, query, query_x, keys_t, values, own_sums)

    cross_2, sums_x, far, tail = barrier((cross_2, sums_x, far, tail))
    far = lax.ppermute(far, "seq", [(i, i + FAR) for i in range(1, n_seq - FAR, 2)])
    send, keys_t, values = pl.pallas_call(
        make_last_kernel(PLANES, n_head),
        in_specs=[flat] + [wide] * (n_head + 1) + [far_off] * 2,
        out_specs=[wide] * 3,
        out_shape=[shape(bf16, *upright), shape(bf16, *lying), shape(bf16, *upright)],
        scratch_shapes=[
            pltpu.VMEM(upright, bf16), pltpu.VMEM(upright, f32), pltpu.VMEM(upright, f32), live, sems(2)
        ],
        compiler_params=params(),
        cost_estimate=cost(4),
    )(told_x, *near_2, *spread(cross_2, n_head // 4), w_in, query_x, sums_x)
    near = crossed(send, "seq", 1)
    w_out, send = barrier((w_out, send))
    w_mine = lax.all_to_all(w_out, "head", split_axis=1, concat_axis=0, tiled=True)
    mine = pl.pallas_call(
        make_own_last_kernel(PLANES),
        in_specs=[flat, far_off, wide, wide, wide, far_off],
        out_specs=wide,
        out_shape=shape(f32, *upright),
        scratch_shapes=[pltpu.VMEM(upright, bf16), live, sems(2)],
        compiler_params=params(),
        cost_estimate=cost(3),
    )(told, query, keys_t, values, tail, sums)
    near, mine, w_mine = barrier((near, mine, w_mine))
    gated = pl.pallas_call(
        finish_kernel,
        in_specs=[wide] * 5,
        out_specs=wide,
        out_shape=shape(bf16, *upright),
        compiler_params=params(),
        cost_estimate=cost(1),
    )(mine, near, far, gate, out_gain)

    out_cols = width // n_head
    cross_gated = crossed(gated, "head", n_head // 2)
    near_gated = spread(gated, n_head // 4)
    mixed = pl.pallas_call(
        near_out_kernel,
        in_specs=[wide] * (n_head // 2 + 1) + [far_off],
        out_specs=wide,
        out_shape=shape(f32, tok_rows, out_cols),
        scratch_shapes=[pltpu.VMEM((tok_rows, out_cols), bf16), pltpu.SemaphoreType.DMA],
        compiler_params=params(),
        cost_estimate=cost(2),
    )(*near_gated, w_mine, history)
    cross_gated, mixed = barrier((cross_gated, mixed))
    return pl.pallas_call(
        far_out_kernel,
        in_specs=[wide] * (n_head // 2 + 2),
        out_specs=wide,
        out_shape=shape(bf16, tok_rows, out_cols),
        compiler_params=params(),
        cost_estimate=cost(2),
    )(*spread(cross_gated, n_head // 4), w_mine, mixed)


def solution(mesh):
    placed = (
        P("seq", None),
        P(),
        P(None, None, "head"),
        P("head"),
        P("head", None),
        P("seq", None),
        P("seq"),
    )
    return jax.shard_map(
        body, mesh=mesh, in_specs=placed, out_specs=P("seq", "head"), check_vma=False
    )
```

```python
import jax
import jax.numpy as jnp
from jax import lax
from jax.experimental import pallas as pl
from jax.experimental.pallas import tpu as pltpu
from jax.sharding import PartitionSpec as P

DH = 128
BLK = 128
WIN = 32
MAXK = 16
EPS = 1e-05
PLANES = 2
FAR = 2 * PLANES + 1
SCALE = 0.5 * DH ** (-0.5)

NT = (((1,), (1,)), ((), ()))


def params(mib=12):
    return pltpu.CompilerParams(vmem_limit_bytes=mib << 20)


def cost(us):
    return pl.CostEstimate(flops=int(us * 1e9 * 0.3), bytes_accessed=int(us * 3e6 * 0.3), transcendentals=0)


def silu(v):
    half = 0.5 * v
    return half * jnp.tanh(half) + half


def project(rows, w):
    return silu(jnp.dot(rows, w, preferred_element_type=jnp.float32))


def normed(rows, gain):
    floats = rows.astype(jnp.float32)
    centre = jnp.mean(floats, axis=-1, keepdims=True)
    off = floats - centre
    spread_sq = jnp.mean(jnp.square(off), axis=-1, keepdims=True)
    return (off * lax.rsqrt(spread_sq + EPS) * gain.astype(jnp.float32)).astype(jnp.bfloat16)


def norm_kernel(history_ref, gain_ref, out_ref, rows_ref, gain_rows_ref, sems):
    share = out_ref.shape[0]
    steps = sems.shape[0] - 1
    step = share // steps
    first = lax.axis_index("head") * share
    gain_copy = pltpu.make_async_copy(gain_ref, gain_rows_ref, sems.at[steps])
    gain_copy.start()
    copies = []
    for i in range(steps):
        at = pl.ds(pl.multiple_of(first + i * step, step), step)
        copies.append(
            pltpu.make_async_copy(history_ref.at[at], rows_ref.at[pl.ds(i * step, step)], sems.at[i])
        )
        copies[i].start()
    gain_copy.wait()
    gain = gain_rows_ref[...].reshape(1, -1)
    for i in range(steps):
        copies[i].wait()
        at = pl.ds(i * step, step)
        out_ref[at, :] = normed(rows_ref[at, :], gain)


def mark(live_ref, told_ref, base, key_blocks, first):
    for b in range(told_ref.shape[0]):
        for g in range(key_blocks):
            live_ref[(first + b) * 8 + g] = 0.0

        def entry(t, unused):
            g = told_ref[b, t] - base
            live_ref[(first + b) * 8 + jnp.where((g >= 0) & (g < key_blocks), g, 7)] = SCALE
            return unused

        lax.fori_loop(0, told_ref[b, MAXK], entry, 0)


def tile(scores, factor):
    half = scores * factor
    return half * jnp.tanh(half) + half


def attend_dense(query_ref, rows, sums_ref, keys_t_ref, values_ref, factors):
    n, blocks = len(factors), len(factors[0])
    for h in range(query_ref.shape[1] // DH):
        cols = pl.ds(h * DH, DH)
        scores = jnp.dot(
            query_ref[rows, cols], keys_t_ref[cols, :], preferred_element_type=jnp.float32
        )
        weights = [
            jnp.concatenate(
                [
                    tile(scores[i * BLK : (i + 1) * BLK, g * BLK : (g + 1) * BLK], factors[i][g])
                    for i in range(n)
                ],
                axis=0,
            ).astype(jnp.bfloat16)
            for g in range(blocks)
        ]
        sums_ref[rows, cols] += jnp.dot(
            jnp.concatenate(weights, axis=1), values_ref[:, cols], preferred_element_type=jnp.float32
        )


def attend_all(query_ref, sums_ref, keys_t_ref, values_ref, live_ref, live_first, key_blocks):
    n = 2

    def some(p, unused):
        factors = [
            [live_ref[(live_first + n * p + i) * 8 + g] for g in range(key_blocks)] for i in range(n)
        ]

        @pl.when(sum(sum(f) for f in factors) > 0.0)
        def _():
            rows = pl.ds(pl.multiple_of(p * n * BLK, n * BLK), n * BLK)
            attend_dense(query_ref, rows, sums_ref, keys_t_ref, values_ref, factors)

        return unused

    lax.fori_loop(0, query_ref.shape[0] // (n * BLK), some, 0)


def fetch(pairs, sems):
    copies = [pltpu.make_async_copy(a, b, sems.at[i]) for i, (a, b) in enumerate(pairs)]
    for copy in copies:
        copy.start()
    return copies


def wait(copies):
    for copy in copies:
        copy.wait()


def own_kernel(
    history_hbm, gain_hbm, w_ref, gate_hbm, values_hbm, query_hbm, keys_t_hbm, tail_hbm,
    history_ref, gain_ref, gate_ref, values_ref, query_ref, keys_t_ref, tail_ref, sems, out_sems,
):
    rows = query_ref.shape[0]
    part = 2 * BLK
    parts = [pl.ds(p * part, part) for p in range(rows // part)]
    gain_copy, *copies = fetch(
        [(gain_hbm, gain_ref)] + [(history_hbm.at[at], history_ref.at[at]) for at in parts], sems
    )
    gain_copy.wait()
    gain = gain_ref[...].reshape(1, -1)
    for at, copy in zip(parts, copies):
        copy.wait()
        here = normed(history_ref[at, :], gain)
        query_ref[at, :] = project(here, w_ref[2]).astype(jnp.bfloat16)
        keys = project(here, w_ref[3])
        keys_t_ref[:, at] = keys.T.astype(jnp.bfloat16)
        values = project(here, w_ref[1]).astype(jnp.bfloat16)
        values_ref[at, :] = values
        gate_ref[at, :] = project(here, w_ref[0]).astype(jnp.bfloat16)
    tail_ref[0] = keys[-BLK:].astype(jnp.bfloat16)
    tail_ref[1] = values[-BLK:]
    wait(
        fetch(
            [
                (query_ref, query_hbm), (values_ref, values_hbm), (keys_t_ref, keys_t_hbm),
                (gate_ref, gate_hbm), (tail_ref, tail_hbm),
            ],
            out_sems,
        )
    )


def own_attend_kernel(
    told_ref, query_hbm, keys_t_hbm, values_hbm, sums_hbm, query_ref, keys_t_ref, values_ref, sums_ref, live_ref, sems
):
    rows, cols = query_ref.shape
    blocks = rows // BLK
    copies = fetch(
        [(query_hbm, query_ref), (keys_t_hbm, keys_t_ref), (values_hbm, values_ref)], sems
    )
    mark(live_ref, told_ref, lax.axis_index("seq") * blocks, blocks, 0)
    wait(copies)
    behind = lax.broadcasted_iota(jnp.int32, (BLK, BLK), 1) <= lax.broadcasted_iota(
        jnp.int32, (BLK, BLK), 0
    )
    for p in range(blocks // 2):
        q_rows = pl.ds(p * 2 * BLK, 2 * BLK)
        seen = pl.ds(0, (2 * p + 2) * BLK)
        for h in range(cols // DH):
            at = pl.ds(h * DH, DH)
            scores = jnp.dot(
                query_ref[q_rows, at], keys_t_ref[at, seen], preferred_element_type=jnp.float32
            )
            weights = []
            for g in range(2 * p + 2):
                column = []
                for i in range(2):
                    b = 2 * p + i
                    if g > b:
                        column.append(jnp.zeros((BLK, BLK), jnp.float32))
                        continue
                    some = tile(
                        scores[i * BLK : (i + 1) * BLK, g * BLK : (g + 1) * BLK], live_ref[b * 8 + g]
                    )
                    column.append(jnp.where(behind, some, 0.0) if g == b else some)
                weights.append(jnp.concatenate(column, axis=0).astype(jnp.bfloat16))
            sums_ref[q_rows, at] = jnp.dot(
                jnp.concatenate(weights, axis=1),
                values_ref[seen, at],
                preferred_element_type=jnp.float32,
            )
    wait(fetch([(sums_ref, sums_hbm)], sems))


def centred(part):
    return part - jnp.mean(part, axis=-1, keepdims=True)


def send_off(sums_ref, send_ref):
    for h in range(send_ref.shape[1] // DH):
        at = pl.ds(h * DH, DH)
        send_ref[:, at] = centred(sums_ref[:, at]).astype(jnp.bfloat16)


def far_kernel(
    told_ref, query_ref, keys_t_hbm, values_hbm, send_ref, keys_t_ref, values_ref, sums_ref, live_ref, sems
):
    blocks = query_ref.shape[0] // BLK
    here = lax.axis_index("seq")

    @pl.when((here % 2 == 1) & (here + FAR < lax.axis_size("seq")))
    def _():
        copies = fetch([(keys_t_hbm, keys_t_ref), (values_hbm, values_ref)], sems)
        mark(live_ref, told_ref, here * blocks, blocks, 0)
        sums_ref[...] = jnp.zeros_like(sums_ref)
        wait(copies)
        attend_all(query_ref, sums_ref, keys_t_ref, values_ref, live_ref, 0, blocks)
        send_off(sums_ref, send_ref)


def chunk_keys(pieces, w_ref, keys_ref, keys_t_ref, values_ref):
    share = pieces[0].shape[0]
    for m, piece in enumerate(pieces):
        at = pl.ds(pl.multiple_of((lax.axis_index("head") ^ m) * share, share), share)
        keys_ref[at, :] = project(piece[...], w_ref[3])
        values_ref[at, :] = project(piece[...], w_ref[1]).astype(jnp.bfloat16)
    keys_t_ref[...] = keys_ref[...].T.astype(jnp.bfloat16)


def make_chunk_kernel(back, n_head):
    def kernel(told_ref, told_x_ref, *refs):
        pieces, refs = refs[:n_head], refs[n_head:]
        w_ref, query_hbm, query_x_hbm, own_t_hbm, own_values_hbm, before_hbm, sums_hbm, sums_x_hbm = refs[:8]
        query_ref, query_x_ref, own_t_ref, own_values_ref, sums_ref, sums_x_ref = refs[8:14]
        keys_ref, keys_t_ref, values_ref, live_ref, sems, out_sems = refs[14:]
        blocks = query_ref.shape[0] // BLK
        here = lax.axis_index("seq")
        source = here - 2 * back
        copies = fetch(
            [
                (query_x_hbm, query_x_ref), (own_t_hbm, own_t_ref), (own_values_hbm, own_values_ref),
                (before_hbm, sums_ref), (query_hbm, query_ref),
            ],
            sems,
        )
        sums_x_ref[...] = jnp.zeros_like(sums_x_ref)
        mark(live_ref, told_x_ref, here * blocks, blocks, 0)

        @pl.when(source >= 0)
        def _():
            chunk_keys(pieces, w_ref, keys_ref, keys_t_ref, values_ref)

        wait(copies)
        attend_all(query_x_ref, sums_x_ref, own_t_ref, own_values_ref, live_ref, 0, blocks)

        @pl.when(source >= 0)
        def _():
            mark(live_ref, told_ref, source * blocks, blocks, 0)
            mark(live_ref, told_x_ref, source * blocks, blocks, blocks)
            attend_all(query_ref, sums_ref, keys_t_ref, values_ref, live_ref, 0, blocks)
            attend_all(query_x_ref, sums_x_ref, keys_t_ref, values_ref, live_ref, blocks, blocks)

        wait(fetch([(sums_ref, sums_hbm), (sums_x_ref, sums_x_hbm)], out_sems))

    return kernel


def make_last_kernel(back, n_head):
    def kernel(told_x_ref, *refs):
        pieces, refs = refs[:n_head], refs[n_head:]
        w_ref, query_x_hbm, before_hbm, send_ref, keys_t_ref, values_ref = refs[:6]
        query_x_ref, sums_ref, keys_ref, live_ref, sems = refs[6:]
        blocks = query_x_ref.shape[0] // BLK
        source = lax.axis_index("seq") - 2 * back
        copies = fetch([(query_x_hbm, query_x_ref), (before_hbm, sums_ref)], sems)

        @pl.when(source >= 0)
        def _():
            chunk_keys(pieces, w_ref, keys_ref, keys_t_ref, values_ref)
            mark(live_ref, told_x_ref, source * blocks, blocks, 0)

        wait(copies)

        @pl.when(source >= 0)
        def _():
            attend_all(query_x_ref, sums_ref, keys_t_ref, values_ref, live_ref, 0, blocks)

        send_off(sums_ref, send_ref)

    return kernel


def make_own_last_kernel(back):
    def kernel(
        told_ref, query_hbm, keys_t_ref, values_ref, tail_ref, before_hbm, gate_hbm, gain_ref,
        sums_ref, scale_ref, query_ref, gate_ref, live_ref, sems,
    ):
        rows, cols = query_ref.shape
        blocks = rows // BLK
        here = lax.axis_index("seq")
        source = here - 2 * back
        copies = fetch([(query_hbm, query_ref), (before_hbm, sums_ref), (gate_hbm, gate_ref)], sems)
        mark(live_ref, told_ref, source * blocks, blocks, 0)
        wait(copies)

        @pl.when(source >= 0)
        def _():
            attend_all(query_ref, sums_ref, keys_t_ref, values_ref, live_ref, 0, blocks)

        farthest = here - FAR - 1

        @pl.when(farthest >= 0)
        def _():
            mark(live_ref, told_ref, farthest * blocks + blocks - 1, 1, 0)
            for h in range(cols // DH):
                at = pl.ds(h * DH, DH)
                scores = lax.dot_general(
                    query_ref[0:BLK, at], tail_ref[0, :, at], NT, preferred_element_type=jnp.float32
                )
                weights = tile(scores, live_ref[0]).astype(jnp.bfloat16)
                sums_ref[0:BLK, at] += jnp.dot(
                    weights, tail_ref[1, :, at], preferred_element_type=jnp.float32
                )

        scale_ref[...] = gain_ref[...].reshape(1, -1).astype(jnp.float32) * gate_ref[...].astype(
            jnp.float32
        )
        for h in range(cols // DH):
            at = pl.ds(h * DH, DH)
            sums_ref[:, at] = centred(sums_ref[:, at])

    return kernel


def finish_kernel(sums_ref, near_ref, far_ref, scale_ref, out_ref):
    for h in range(sums_ref.shape[1] // DH):
        at = pl.ds(h * DH, DH)
        part = sums_ref[:, at] + near_ref[:, at].astype(jnp.float32) + far_ref[:, at].astype(jnp.float32)
        off = centred(part)
        spread_sq = jnp.mean(jnp.square(off), axis=-1, keepdims=True)
        out_ref[:, at] = (off * lax.rsqrt(spread_sq + EPS) * scale_ref[:, at]).astype(jnp.bfloat16)


def mix(total, pieces, w_ref):
    cols = pieces[0].shape[1]
    for m, piece in enumerate(pieces):
        w = w_ref[m * cols : (m + 1) * cols, :]
        total = total + jnp.dot(piece[...], w, preferred_element_type=jnp.float32)
    return total


def near_out_kernel(*refs):
    n = (len(refs) - 7) // 3
    pieces, w_hbm, refs = refs[:n], refs[n : 3 * n], refs[3 * n :]
    history_hbm, out_ref, w_far_ref, w_near_ref, history_ref, sems, w_sems = refs
    cols = out_ref.shape[1]
    rows = w_hbm[0].shape[0]
    at = pl.ds(pl.multiple_of(lax.axis_index("head") * cols, cols), cols)
    copies = fetch([(history_hbm.at[:, at], history_ref)], sems)
    w_copies = fetch(
        [
            (w.at[:, at], (w_near_ref if m < n else w_far_ref).at[pl.ds(m % n * rows, rows)])
            for m, w in enumerate(w_hbm)
        ],
        w_sems,
    )
    wait(copies)
    wait(w_copies)
    out_ref[...] = mix(history_ref[...].astype(jnp.float32), pieces, w_near_ref)


def far_out_kernel(*refs):
    *pieces, w_ref, near_ref, out_ref = refs
    out_ref[...] = mix(near_ref[...], pieces, w_ref).astype(jnp.bfloat16)


def crossed(array, axis, bit):
    return lax.ppermute(array, axis, [(i, i ^ bit) for i in range(lax.axis_size(axis))])


def spread(piece, bit):
    pieces = {0: piece}
    while bit:
        pieces.update({m + bit: crossed(p, "head", bit) for m, p in list(pieces.items())})
        bit //= 2
    return [pieces[m] for m in sorted(pieces)]


def body(history, ln_gain, w_in, out_gain, w_out, block_lists, counts):
    tok_rows, width = history.shape
    blocks = counts.shape[0]
    cols = w_in.shape[2]
    n_seq, n_head = lax.axis_size("seq"), lax.axis_size("head")
    assert 2 * (PLANES + 1) * blocks - (WIN - 1) == blocks - 1
    barrier = lax.optimization_barrier

    shape = lambda like, *dims: jax.ShapeDtypeStruct(dims, like)
    bf16, f32 = jnp.bfloat16, jnp.float32
    wide = pl.BlockSpec(memory_space=pltpu.VMEM)
    flat = pl.BlockSpec(memory_space=pltpu.SMEM)
    far_off = pl.BlockSpec(memory_space=pltpu.HBM)
    n_live = 2 * blocks * 8
    upright, lying = (tok_rows, cols), (cols, tok_rows)
    sems = lambda n: pltpu.SemaphoreType.DMA((n,))
    live = pltpu.SMEM((n_live,), f32)

    share_rows = tok_rows // n_head
    steps = share_rows // 48
    share = pl.pallas_call(
        norm_kernel,
        in_specs=[far_off] * 2,
        out_specs=wide,
        out_shape=shape(bf16, share_rows, width),
        scratch_shapes=[
            pltpu.VMEM((share_rows, width), bf16),
            pltpu.VMEM((width,), bf16),
            sems(steps + 1),
        ],
        cost_estimate=cost(2),
        compiler_params=params(60),
    )(history, ln_gain)
    gain, block_lists, counts, w_out, share = barrier((ln_gain, block_lists, counts, w_out, share))
    told = jnp.concatenate([block_lists, counts[:, None]], axis=1)
    upward = [(i, i + 2) for i in range(n_seq - 2)]
    downward = [(i, i - FAR) for i in range(FAR + 1, n_seq, 2)]
    share_1 = lax.ppermute(share, "seq", upward)

    gate, values, query, keys_t, tail = pl.pallas_call(
        own_kernel,
        in_specs=[far_off, far_off, wide],
        out_specs=[far_off] * 5,
        out_shape=[shape(bf16, *upright)] * 3 + [shape(bf16, *lying), shape(bf16, 2, BLK, cols)],
        scratch_shapes=[pltpu.VMEM((tok_rows, width), bf16), pltpu.VMEM((width,), bf16)]
        + [pltpu.VMEM(upright, bf16)] * 3
        + [pltpu.VMEM(lying, bf16), pltpu.VMEM((2, BLK, cols), bf16)]
        + [sems(1 + tok_rows // (2 * BLK)), sems(5)],
        compiler_params=params(),
        cost_estimate=cost(4),
    )(history, gain, w_in)

    w_cross = crossed(w_out, "head", n_head // 2)
    share_1, query, w_cross = barrier((share_1, query, w_cross))
    share_2 = lax.ppermute(share_1, "seq", upward)
    cross_1 = crossed(share_1, "head", n_head // 2)
    query_x, told_x = crossed(query, "seq", 1), crossed(told, "seq", 1)
    query_far, told_far = (lax.ppermute(a, "seq", downward) for a in (query, told))
    tail = lax.ppermute(tail, "seq", [(i, i + FAR + 1) for i in range(n_seq - FAR - 1)])
    told, told_x, told_far = barrier((told, told_x, told_far))
    own_sums = pl.pallas_call(
        own_attend_kernel,
        in_specs=[flat] + [far_off] * 3,
        out_specs=far_off,
        out_shape=shape(f32, *upright),
        scratch_shapes=[pltpu.VMEM(upright, bf16), pltpu.VMEM(lying, bf16), pltpu.VMEM(upright, bf16)]
        + [pltpu.VMEM(upright, f32), live, sems(3)],
        compiler_params=params(),
        cost_estimate=cost(4),
    )(told, query, keys_t, values)
    share_2, cross_1, own_sums = barrier((share_2, cross_1, own_sums))
    chunk_1 = spread(share_1, n_head // 4) + spread(cross_1, n_head // 4)
    cross_2 = crossed(share_2, "head", n_head // 2)
    near_2 = spread(share_2, n_head // 4)

    far = pl.pallas_call(
        far_kernel,
        in_specs=[flat, wide, far_off, far_off],
        out_specs=wide,
        out_shape=shape(bf16, *upright),
        scratch_shapes=[
            pltpu.VMEM(lying, bf16), pltpu.VMEM(upright, bf16), pltpu.VMEM(upright, f32), live, sems(2)
        ],
        compiler_params=params(),
        cost_estimate=cost(2),
    )(told_far, query_far, keys_t, values)

    sums, sums_x = pl.pallas_call(
        make_chunk_kernel(1, n_head),
        in_specs=[flat] * 2 + [wide] * (n_head + 1) + [far_off] * 5,
        out_specs=[far_off] * 2,
        out_shape=[shape(f32, *upright)] * 2,
        scratch_shapes=[
            pltpu.VMEM(dims, kind)
            for dims, kind in (
                (upright, bf16), (upright, bf16), (lying, bf16), (upright, bf16), (upright, f32),
                (upright, f32), (upright, f32), (lying, bf16), (upright, bf16),
            )
        ]
        + [live, sems(5), sems(2)],
        compiler_params=params(16),
        cost_estimate=cost(6),
    )(told, told_x, *chunk_1, w_in, query, query_x, keys_t, values, own_sums)

    cross_2, sums_x, far, tail = barrier((cross_2, sums_x, far, tail))
    far = lax.ppermute(far, "seq", [(i, i + FAR) for i in range(1, n_seq - FAR, 2)])
    send, keys_t, values = pl.pallas_call(
        make_last_kernel(PLANES, n_head),
        in_specs=[flat] + [wide] * (n_head + 1) + [far_off] * 2,
        out_specs=[wide] * 3,
        out_shape=[shape(bf16, *upright), shape(bf16, *lying), shape(bf16, *upright)],
        scratch_shapes=[
            pltpu.VMEM(upright, bf16), pltpu.VMEM(upright, f32), pltpu.VMEM(upright, f32), live, sems(2)
        ],
        compiler_params=params(),
        cost_estimate=cost(4),
    )(told_x, *near_2, *spread(cross_2, n_head // 4), w_in, query_x, sums_x)
    near = crossed(send, "seq", 1)
    send, w_out, w_cross = barrier((send, w_out, w_cross))
    w_all = spread(w_out, n_head // 4) + spread(w_cross, n_head // 4)
    mine, scale = pl.pallas_call(
        make_own_last_kernel(PLANES),
        in_specs=[flat, far_off, wide, wide, wide, far_off, far_off, wide],
        out_specs=[wide] * 2,
        out_shape=[shape(f32, *upright)] * 2,
        scratch_shapes=[pltpu.VMEM(upright, bf16)] * 2 + [live, sems(3)],
        compiler_params=params(),
        cost_estimate=cost(3),
    )(told, query, keys_t, values, tail, sums, gate, out_gain)
    near, mine, w_all = barrier((near, mine, tuple(w_all)))
    gated = pl.pallas_call(
        finish_kernel,
        in_specs=[wide] * 4,
        out_specs=wide,
        out_shape=shape(bf16, *upright),
        compiler_params=params(),
        cost_estimate=cost(1),
    )(mine, near, far, scale)

    out_cols = width // n_head
    cross_gated = crossed(gated, "head", n_head // 2)
    near_gated = spread(gated, n_head // 4)
    half = n_head // 2
    mixed, w_far = pl.pallas_call(
        near_out_kernel,
        in_specs=[wide] * half + [far_off] * (n_head + 1),
        out_specs=[wide] * 2,
        out_shape=[shape(f32, tok_rows, out_cols), shape(bf16, half * cols, out_cols)],
        scratch_shapes=[
            pltpu.VMEM((half * cols, out_cols), bf16), pltpu.VMEM((tok_rows, out_cols), bf16),
            sems(1), sems(n_head),
        ],
        compiler_params=params(),
        cost_estimate=cost(2),
    )(*near_gated, *w_all, history)
    cross_gated, mixed = barrier((cross_gated, mixed))
    return pl.pallas_call(
        far_out_kernel,
        in_specs=[wide] * (half + 2),
        out_specs=wide,
        out_shape=shape(bf16, tok_rows, out_cols),
        compiler_params=params(),
        cost_estimate=cost(2),
    )(*spread(cross_gated, n_head // 4), w_far, mixed)


def solution(mesh):
    placed = (
        P("seq", None),
        P(),
        P(None, None, "head"),
        P("head"),
        P("head", None),
        P("seq", None),
        P("seq"),
    )
    return jax.shard_map(
        body, mesh=mesh, in_specs=placed, out_specs=P("seq", "head"), check_vma=False
    )
```

```python
import jax
import jax.numpy as jnp
from jax import lax
from jax.experimental import pallas as pl
from jax.experimental.pallas import tpu as pltpu
from jax.sharding import PartitionSpec as P

DH = 128
BLK = 128
WIN = 32
MAXK = 16
EPS = 1e-05
PLANES = 2
FAR = 2 * PLANES + 1
SCALE = 0.5 * DH ** (-0.5)

NT = (((1,), (1,)), ((), ()))


def params(mib=12):
    return pltpu.CompilerParams(vmem_limit_bytes=mib << 20)


def cost(us):
    return pl.CostEstimate(flops=int(us * 1e9 * 0.3), bytes_accessed=int(us * 3e6 * 0.3), transcendentals=0)


def silu(v):
    half = 0.5 * v
    return half * jnp.tanh(half) + half


def project(rows, w):
    return silu(jnp.dot(rows, w, preferred_element_type=jnp.float32))


def normed(rows, gain):
    floats = rows.astype(jnp.float32)
    centre = jnp.mean(floats, axis=-1, keepdims=True)
    off = floats - centre
    spread_sq = jnp.mean(jnp.square(off), axis=-1, keepdims=True)
    return (off * lax.rsqrt(spread_sq + EPS) * gain.astype(jnp.float32)).astype(jnp.bfloat16)


def norm_kernel(history_ref, gain_ref, out_ref, rows_ref, gain_rows_ref, sems):
    share = out_ref.shape[0]
    steps = sems.shape[0] - 1
    step = share // steps
    first = lax.axis_index("head") * share
    gain_copy = pltpu.make_async_copy(gain_ref, gain_rows_ref, sems.at[steps])
    gain_copy.start()
    copies = []
    for i in range(steps):
        at = pl.ds(pl.multiple_of(first + i * step, step), step)
        copies.append(
            pltpu.make_async_copy(history_ref.at[at], rows_ref.at[pl.ds(i * step, step)], sems.at[i])
        )
        copies[i].start()
    gain_copy.wait()
    gain = gain_rows_ref[...].reshape(1, -1)
    for i in range(steps):
        copies[i].wait()
        at = pl.ds(i * step, step)
        out_ref[at, :] = normed(rows_ref[at, :], gain)


def mark(live_ref, told_ref, base, key_blocks, first):
    for b in range(told_ref.shape[0]):
        for g in range(key_blocks):
            live_ref[(first + b) * 8 + g] = 0.0

        def entry(t, unused):
            g = told_ref[b, t] - base
            live_ref[(first + b) * 8 + jnp.where((g >= 0) & (g < key_blocks), g, 7)] = SCALE
            return unused

        lax.fori_loop(0, told_ref[b, MAXK], entry, 0)


def tile(scores, factor):
    half = scores * factor
    return half * jnp.tanh(half) + half


def attend_dense(query_ref, rows, sums_ref, keys_t_ref, values_ref, factors):
    n, blocks = len(factors), len(factors[0])
    for h in range(query_ref.shape[1] // DH):
        cols = pl.ds(h * DH, DH)
        scores = jnp.dot(
            query_ref[rows, cols], keys_t_ref[cols, :], preferred_element_type=jnp.float32
        )
        weights = [
            jnp.concatenate(
                [
                    tile(scores[i * BLK : (i + 1) * BLK, g * BLK : (g + 1) * BLK], factors[i][g])
                    for i in range(n)
                ],
                axis=0,
            ).astype(jnp.bfloat16)
            for g in range(blocks)
        ]
        sums_ref[rows, cols] += jnp.dot(
            jnp.concatenate(weights, axis=1), values_ref[:, cols], preferred_element_type=jnp.float32
        )


def attend_all(query_ref, sums_ref, keys_t_ref, values_ref, live_ref, live_first, key_blocks):
    n = 2

    def some(p, unused):
        factors = [
            [live_ref[(live_first + n * p + i) * 8 + g] for g in range(key_blocks)] for i in range(n)
        ]

        @pl.when(sum(sum(f) for f in factors) > 0.0)
        def _():
            rows = pl.ds(pl.multiple_of(p * n * BLK, n * BLK), n * BLK)
            attend_dense(query_ref, rows, sums_ref, keys_t_ref, values_ref, factors)

        return unused

    lax.fori_loop(0, query_ref.shape[0] // (n * BLK), some, 0)


def fetch(pairs, sems):
    copies = [pltpu.make_async_copy(a, b, sems.at[i]) for i, (a, b) in enumerate(pairs)]
    for copy in copies:
        copy.start()
    return copies


def wait(copies):
    for copy in copies:
        copy.wait()


def own_kernel(
    history_hbm, gain_hbm, w_ref, gate_hbm, both_hbm, query_hbm, keys_t_hbm, tail_hbm,
    history_ref, gain_ref, gate_ref, both_ref, query_ref, keys_t_ref, sems, out_sems,
):
    rows = query_ref.shape[0]
    part = 2 * BLK
    parts = [pl.ds(p * part, part) for p in range(rows // part)]
    gain_copy, *copies = fetch(
        [(gain_hbm, gain_ref)] + [(history_hbm.at[at], history_ref.at[at]) for at in parts], sems
    )
    gain_copy.wait()
    gain = gain_ref[...].reshape(1, -1)
    for p, (at, copy) in enumerate(zip(parts, copies)):
        copy.wait()
        here = normed(history_ref[at, :], gain)
        query_ref[at, :] = project(here, w_ref[2]).astype(jnp.bfloat16)
        keys = project(here, w_ref[3])
        keys_t_ref[:, at] = keys.T.astype(jnp.bfloat16)
        both_ref[at, :] = keys.astype(jnp.bfloat16)
        both_ref[pl.ds(rows + p * part, part), :] = project(here, w_ref[1]).astype(jnp.bfloat16)
        gate_ref[at, :] = project(here, w_ref[0]).astype(jnp.bfloat16)
    wait(
        fetch(
            [
                (query_ref, query_hbm), (both_ref, both_hbm), (keys_t_ref, keys_t_hbm), (gate_ref, gate_hbm),
                (both_ref.at[pl.ds(rows - BLK, BLK)], tail_hbm.at[0]),
                (both_ref.at[pl.ds(2 * rows - BLK, BLK)], tail_hbm.at[1]),
            ],
            out_sems,
        )
    )


def own_attend_kernel(
    told_ref, query_hbm, keys_t_hbm, both_hbm, sums_hbm, query_ref, keys_t_ref, values_ref, sums_ref, live_ref, sems
):
    rows, cols = query_ref.shape
    blocks = rows // BLK
    copies = fetch(
        [
            (query_hbm, query_ref), (keys_t_hbm, keys_t_ref),
            (both_hbm.at[pl.ds(rows, rows)], values_ref),
        ],
        sems,
    )
    mark(live_ref, told_ref, lax.axis_index("seq") * blocks, blocks, 0)
    wait(copies)
    behind = lax.broadcasted_iota(jnp.int32, (BLK, BLK), 1) <= lax.broadcasted_iota(
        jnp.int32, (BLK, BLK), 0
    )
    for p in range(blocks // 2):
        q_rows = pl.ds(p * 2 * BLK, 2 * BLK)
        seen = pl.ds(0, (2 * p + 2) * BLK)
        for h in range(cols // DH):
            at = pl.ds(h * DH, DH)
            scores = jnp.dot(
                query_ref[q_rows, at], keys_t_ref[at, seen], preferred_element_type=jnp.float32
            )
            weights = []
            for g in range(2 * p + 2):
                column = []
                for i in range(2):
                    b = 2 * p + i
                    if g > b:
                        column.append(jnp.zeros((BLK, BLK), jnp.float32))
                        continue
                    some = tile(
                        scores[i * BLK : (i + 1) * BLK, g * BLK : (g + 1) * BLK], live_ref[b * 8 + g]
                    )
                    column.append(jnp.where(behind, some, 0.0) if g == b else some)
                weights.append(jnp.concatenate(column, axis=0).astype(jnp.bfloat16))
            sums_ref[q_rows, at] = jnp.dot(
                jnp.concatenate(weights, axis=1),
                values_ref[seen, at],
                preferred_element_type=jnp.float32,
            )
    wait(fetch([(sums_ref, sums_hbm)], sems))


def centred(part):
    return part - jnp.mean(part, axis=-1, keepdims=True)


def send_off(sums_ref, send_ref):
    for h in range(send_ref.shape[1] // DH):
        at = pl.ds(h * DH, DH)
        send_ref[:, at] = centred(sums_ref[:, at]).astype(jnp.bfloat16)


def chunk_keys(pieces, w_ref, keys_ref, keys_t_ref, values_ref):
    share = pieces[0].shape[0]
    for m, piece in enumerate(pieces):
        at = pl.ds(pl.multiple_of((lax.axis_index("head") ^ m) * share, share), share)
        keys_ref[at, :] = project(piece[...], w_ref[3])
        values_ref[at, :] = project(piece[...], w_ref[1]).astype(jnp.bfloat16)
    keys_t_ref[...] = keys_ref[...].T.astype(jnp.bfloat16)


def make_chunk_kernel(back, n_head):
    def kernel(told_ref, told_x_ref, *refs):
        pieces, refs = refs[:n_head], refs[n_head:]
        w_ref, query_hbm, query_x_hbm, own_t_hbm, own_both_hbm, before_hbm, sums_hbm, sums_x_hbm = refs[:8]
        query_ref, query_x_ref, own_t_ref, own_values_ref, sums_ref, sums_x_ref = refs[8:14]
        keys_ref, keys_t_ref, values_ref, live_ref, sems, out_sems = refs[14:]
        blocks = query_ref.shape[0] // BLK
        here = lax.axis_index("seq")
        source = here - 2 * back
        copies = fetch(
            [
                (query_x_hbm, query_x_ref), (own_t_hbm, own_t_ref),
                (own_both_hbm.at[pl.ds(blocks * BLK, blocks * BLK)], own_values_ref),
                (before_hbm, sums_ref), (query_hbm, query_ref),
            ],
            sems,
        )
        sums_x_ref[...] = jnp.zeros_like(sums_x_ref)
        mark(live_ref, told_x_ref, here * blocks, blocks, 0)

        @pl.when(source >= 0)
        def _():
            chunk_keys(pieces, w_ref, keys_ref, keys_t_ref, values_ref)

        wait(copies)
        attend_all(query_x_ref, sums_x_ref, own_t_ref, own_values_ref, live_ref, 0, blocks)

        @pl.when(source >= 0)
        def _():
            mark(live_ref, told_ref, source * blocks, blocks, 0)
            mark(live_ref, told_x_ref, source * blocks, blocks, blocks)
            attend_all(query_ref, sums_ref, keys_t_ref, values_ref, live_ref, 0, blocks)
            attend_all(query_x_ref, sums_x_ref, keys_t_ref, values_ref, live_ref, blocks, blocks)

        wait(fetch([(sums_ref, sums_hbm), (sums_x_ref, sums_x_hbm)], out_sems))

    return kernel


def make_last_kernel(back, n_head):
    def kernel(told_x_ref, *refs):
        pieces, refs = refs[:n_head], refs[n_head:]
        w_ref, query_x_hbm, before_hbm, send_ref, keys_t_ref, values_ref = refs[:6]
        query_x_ref, sums_ref, keys_ref, live_ref, sems = refs[6:]
        blocks = query_x_ref.shape[0] // BLK
        source = lax.axis_index("seq") - 2 * back
        copies = fetch([(query_x_hbm, query_x_ref), (before_hbm, sums_ref)], sems)

        @pl.when(source >= 0)
        def _():
            chunk_keys(pieces, w_ref, keys_ref, keys_t_ref, values_ref)
            mark(live_ref, told_x_ref, source * blocks, blocks, 0)

        wait(copies)

        @pl.when(source >= 0)
        def _():
            attend_all(query_x_ref, sums_ref, keys_t_ref, values_ref, live_ref, 0, blocks)

        send_off(sums_ref, send_ref)

    return kernel


def make_own_last_kernel(back):
    def kernel(
        told_ref, query_hbm, keys_t_ref, values_ref, tail_ref, far_hbm, before_hbm, gate_hbm, gain_ref,
        sums_ref, scale_ref, query_ref, gate_ref, far_ref, far_t_ref, live_ref, sems, far_sems,
    ):
        rows, cols = query_ref.shape
        blocks = rows // BLK
        here = lax.axis_index("seq")
        source = here - 2 * back
        copies = fetch([(query_hbm, query_ref), (before_hbm, sums_ref), (gate_hbm, gate_ref)], sems)
        far_copies = fetch([(far_hbm, far_ref)], far_sems)
        mark(live_ref, told_ref, source * blocks, blocks, 0)
        wait(copies)

        @pl.when(source >= 0)
        def _():
            attend_all(query_ref, sums_ref, keys_t_ref, values_ref, live_ref, 0, blocks)

        wait(far_copies)
        far = here - FAR

        @pl.when((far >= 0) & (here % 2 == 0))
        def _():
            far_t_ref[...] = far_ref[0:rows, :].astype(jnp.float32).T.astype(jnp.bfloat16)
            mark(live_ref, told_ref, far * blocks, blocks, 0)
            attend_all(query_ref, sums_ref, far_t_ref, far_ref.at[pl.ds(rows, rows)], live_ref, 0, blocks)

        farthest = here - FAR - 1

        @pl.when(farthest >= 0)
        def _():
            mark(live_ref, told_ref, farthest * blocks + blocks - 1, 1, 0)
            for h in range(cols // DH):
                at = pl.ds(h * DH, DH)
                scores = lax.dot_general(
                    query_ref[0:BLK, at], tail_ref[0, :, at], NT, preferred_element_type=jnp.float32
                )
                weights = tile(scores, live_ref[0]).astype(jnp.bfloat16)
                sums_ref[0:BLK, at] += jnp.dot(
                    weights, tail_ref[1, :, at], preferred_element_type=jnp.float32
                )

        scale_ref[...] = gain_ref[...].reshape(1, -1).astype(jnp.float32) * gate_ref[...].astype(
            jnp.float32
        )
        for h in range(cols // DH):
            at = pl.ds(h * DH, DH)
            sums_ref[:, at] = centred(sums_ref[:, at])

    return kernel


def finish_kernel(sums_ref, near_ref, scale_ref, out_ref):
    for h in range(sums_ref.shape[1] // DH):
        at = pl.ds(h * DH, DH)
        part = sums_ref[:, at] + near_ref[:, at].astype(jnp.float32)
        off = centred(part)
        spread_sq = jnp.mean(jnp.square(off), axis=-1, keepdims=True)
        out_ref[:, at] = (off * lax.rsqrt(spread_sq + EPS) * scale_ref[:, at]).astype(jnp.bfloat16)


def mix(total, pieces, w_ref):
    cols = pieces[0].shape[1]
    for m, piece in enumerate(pieces):
        w = w_ref[m * cols : (m + 1) * cols, :]
        total = total + jnp.dot(piece[...], w, preferred_element_type=jnp.float32)
    return total


def near_out_kernel(*refs):
    n = (len(refs) - 7) // 3
    pieces, w_hbm, refs = refs[:n], refs[n : 3 * n], refs[3 * n :]
    history_hbm, out_ref, w_far_ref, w_near_ref, history_ref, sems, w_sems = refs
    cols = out_ref.shape[1]
    rows = w_hbm[0].shape[0]
    at = pl.ds(pl.multiple_of(lax.axis_index("head") * cols, cols), cols)
    copies = fetch([(history_hbm.at[:, at], history_ref)], sems)
    w_copies = fetch(
        [
            (w.at[:, at], (w_near_ref if m < n else w_far_ref).at[pl.ds(m % n * rows, rows)])
            for m, w in enumerate(w_hbm)
        ],
        w_sems,
    )
    wait(copies)
    wait(w_copies)
    out_ref[...] = mix(history_ref[...].astype(jnp.float32), pieces, w_near_ref)


def far_out_kernel(*refs):
    *pieces, w_ref, near_ref, out_ref = refs
    out_ref[...] = mix(near_ref[...], pieces, w_ref).astype(jnp.bfloat16)


def crossed(array, axis, bit):
    return lax.ppermute(array, axis, [(i, i ^ bit) for i in range(lax.axis_size(axis))])


def spread(piece, bit):
    pieces = {0: piece}
    while bit:
        pieces.update({m + bit: crossed(p, "head", bit) for m, p in list(pieces.items())})
        bit //= 2
    return [pieces[m] for m in sorted(pieces)]


def body(history, ln_gain, w_in, out_gain, w_out, block_lists, counts):
    tok_rows, width = history.shape
    blocks = counts.shape[0]
    cols = w_in.shape[2]
    n_seq, n_head = lax.axis_size("seq"), lax.axis_size("head")
    assert 2 * (PLANES + 1) * blocks - (WIN - 1) == blocks - 1
    barrier = lax.optimization_barrier

    shape = lambda like, *dims: jax.ShapeDtypeStruct(dims, like)
    bf16, f32 = jnp.bfloat16, jnp.float32
    wide = pl.BlockSpec(memory_space=pltpu.VMEM)
    flat = pl.BlockSpec(memory_space=pltpu.SMEM)
    far_off = pl.BlockSpec(memory_space=pltpu.HBM)
    n_live = 2 * blocks * 8
    upright, lying = (tok_rows, cols), (cols, tok_rows)
    sems = lambda n: pltpu.SemaphoreType.DMA((n,))
    live = pltpu.SMEM((n_live,), f32)

    share_rows = tok_rows // n_head
    steps = share_rows // 48
    share = pl.pallas_call(
        norm_kernel,
        in_specs=[far_off] * 2,
        out_specs=wide,
        out_shape=shape(bf16, share_rows, width),
        scratch_shapes=[
            pltpu.VMEM((share_rows, width), bf16),
            pltpu.VMEM((width,), bf16),
            sems(steps + 1),
        ],
        cost_estimate=cost(2),
        compiler_params=params(60),
    )(history, ln_gain)
    gain, block_lists, counts, w_out, share = barrier((ln_gain, block_lists, counts, w_out, share))
    told = jnp.concatenate([block_lists, counts[:, None]], axis=1)
    upward = [(i, i + 2) for i in range(n_seq - 2)]
    share_1 = lax.ppermute(share, "seq", upward)

    gate, both, query, keys_t, tail = pl.pallas_call(
        own_kernel,
        in_specs=[far_off, far_off, wide],
        out_specs=[far_off] * 5,
        out_shape=[
            shape(bf16, *upright), shape(bf16, 2 * tok_rows, cols), shape(bf16, *upright),
            shape(bf16, *lying), shape(bf16, 2, BLK, cols),
        ],
        scratch_shapes=[
            pltpu.VMEM((tok_rows, width), bf16), pltpu.VMEM((width,), bf16), pltpu.VMEM(upright, bf16),
            pltpu.VMEM((2 * tok_rows, cols), bf16), pltpu.VMEM(upright, bf16), pltpu.VMEM(lying, bf16),
            sems(1 + tok_rows // (2 * BLK)), sems(6),
        ],
        compiler_params=params(60),
        cost_estimate=cost(4),
    )(history, gain, w_in)

    w_cross = crossed(w_out, "head", n_head // 2)
    share_1, query, w_cross = barrier((share_1, query, w_cross))
    share_2 = lax.ppermute(share_1, "seq", upward)
    cross_1 = crossed(share_1, "head", n_head // 2)
    query_x, told_x = crossed(query, "seq", 1), crossed(told, "seq", 1)
    tail = lax.ppermute(tail, "seq", [(i, i + FAR + 1) for i in range(n_seq - FAR - 1)])
    told, told_x = barrier((told, told_x))
    own_sums = pl.pallas_call(
        own_attend_kernel,
        in_specs=[flat] + [far_off] * 3,
        out_specs=far_off,
        out_shape=shape(f32, *upright),
        scratch_shapes=[pltpu.VMEM(upright, bf16), pltpu.VMEM(lying, bf16), pltpu.VMEM(upright, bf16)]
        + [pltpu.VMEM(upright, f32), live, sems(3)],
        compiler_params=params(),
        cost_estimate=cost(4),
    )(told, query, keys_t, both)
    share_2, cross_1, own_sums = barrier((share_2, cross_1, own_sums))
    chunk_1 = spread(share_1, n_head // 4) + spread(cross_1, n_head // 4)
    cross_2 = crossed(share_2, "head", n_head // 2)
    near_2 = spread(share_2, n_head // 4)

    both, share_2 = barrier((both, share_2))
    far = lax.ppermute(both, "seq", [(i, i + FAR) for i in range(1, n_seq - FAR, 2)])

    sums, sums_x = pl.pallas_call(
        make_chunk_kernel(1, n_head),
        in_specs=[flat] * 2 + [wide] * (n_head + 1) + [far_off] * 5,
        out_specs=[far_off] * 2,
        out_shape=[shape(f32, *upright)] * 2,
        scratch_shapes=[
            pltpu.VMEM(dims, kind)
            for dims, kind in (
                (upright, bf16), (upright, bf16), (lying, bf16), (upright, bf16), (upright, f32),
                (upright, f32), (upright, f32), (lying, bf16), (upright, bf16),
            )
        ]
        + [live, sems(5), sems(2)],
        compiler_params=params(16),
        cost_estimate=cost(6),
    )(told, told_x, *chunk_1, w_in, query, query_x, keys_t, both, own_sums)

    cross_2, sums_x, far, tail = barrier((cross_2, sums_x, far, tail))
    send, keys_t, values = pl.pallas_call(
        make_last_kernel(PLANES, n_head),
        in_specs=[flat] + [wide] * (n_head + 1) + [far_off] * 2,
        out_specs=[wide] * 3,
        out_shape=[shape(bf16, *upright), shape(bf16, *lying), shape(bf16, *upright)],
        scratch_shapes=[
            pltpu.VMEM(upright, bf16), pltpu.VMEM(upright, f32), pltpu.VMEM(upright, f32), live, sems(2)
        ],
        compiler_params=params(),
        cost_estimate=cost(4),
    )(told_x, *near_2, *spread(cross_2, n_head // 4), w_in, query_x, sums_x)
    near = crossed(send, "seq", 1)
    send, w_out, w_cross = barrier((send, w_out, w_cross))
    w_all = spread(w_out, n_head // 4) + spread(w_cross, n_head // 4)
    mine, scale = pl.pallas_call(
        make_own_last_kernel(PLANES),
        in_specs=[flat, far_off, wide, wide, wide, far_off, far_off, far_off, wide],
        out_specs=[wide] * 2,
        out_shape=[shape(f32, *upright)] * 2,
        scratch_shapes=[pltpu.VMEM(upright, bf16)] * 2
        + [pltpu.VMEM((2 * tok_rows, cols), bf16), pltpu.VMEM(lying, bf16), live, sems(3), sems(1)],
        compiler_params=params(),
        cost_estimate=cost(3),
    )(told, query, keys_t, values, tail, far, sums, gate, out_gain)
    near, mine, w_all = barrier((near, mine, tuple(w_all)))
    gated = pl.pallas_call(
        finish_kernel,
        in_specs=[wide] * 3,
        out_specs=wide,
        out_shape=shape(bf16, *upright),
        compiler_params=params(),
        cost_estimate=cost(1),
    )(mine, near, scale)

    out_cols = width // n_head
    cross_gated = crossed(gated, "head", n_head // 2)
    near_gated = spread(gated, n_head // 4)
    half = n_head // 2
    mixed, w_far = pl.pallas_call(
        near_out_kernel,
        in_specs=[wide] * half + [far_off] * (n_head + 1),
        out_specs=[wide] * 2,
        out_shape=[shape(f32, tok_rows, out_cols), shape(bf16, half * cols, out_cols)],
        scratch_shapes=[
            pltpu.VMEM((half * cols, out_cols), bf16), pltpu.VMEM((tok_rows, out_cols), bf16),
            sems(1), sems(n_head),
        ],
        compiler_params=params(),
        cost_estimate=cost(2),
    )(*near_gated, *w_all, history)
    cross_gated, mixed = barrier((cross_gated, mixed))
    return pl.pallas_call(
        far_out_kernel,
        in_specs=[wide] * (half + 2),
        out_specs=wide,
        out_shape=shape(bf16, tok_rows, out_cols),
        compiler_params=params(),
        cost_estimate=cost(2),
    )(*spread(cross_gated, n_head // 4), w_far, mixed)


def solution(mesh):
    placed = (
        P("seq", None),
        P(),
        P(None, None, "head"),
        P("head"),
        P("head", None),
        P("seq", None),
        P("seq"),
    )
    return jax.shard_map(
        body, mesh=mesh, in_specs=placed, out_specs=P("seq", "head"), check_vma=False
    )
```

```python
import jax
import jax.numpy as jnp
from jax import lax
from jax.experimental import pallas as pl
from jax.experimental.pallas import tpu as pltpu
from jax.sharding import PartitionSpec as P

DH = 128
BLK = 128
WIN = 32
MAXK = 16
EPS = 1e-05
PLANES = 2
FAR = 2 * PLANES + 1
SCALE = 0.5 * DH ** (-0.5)

NT = (((1,), (1,)), ((), ()))


def params(mib=12):
    return pltpu.CompilerParams(vmem_limit_bytes=mib << 20)


def cost(us):
    return pl.CostEstimate(flops=int(us * 1e9 * 0.3), bytes_accessed=int(us * 3e6 * 0.3), transcendentals=0)


def silu(v):
    half = 0.5 * v
    return half * jnp.tanh(half) + half


def project(rows, w):
    return silu(jnp.dot(rows, w, preferred_element_type=jnp.float32))


def normed(rows, gain):
    floats = rows.astype(jnp.float32)
    centre = jnp.mean(floats, axis=-1, keepdims=True)
    off = floats - centre
    spread_sq = jnp.mean(jnp.square(off), axis=-1, keepdims=True)
    return (off * lax.rsqrt(spread_sq + EPS) * gain.astype(jnp.float32)).astype(jnp.bfloat16)


def norm_kernel(history_ref, gain_ref, out_ref, rows_ref, gain_rows_ref, sems):
    share = out_ref.shape[0]
    steps = sems.shape[0] - 1
    step = share // steps
    first = lax.axis_index("head") * share
    gain_copy = pltpu.make_async_copy(gain_ref, gain_rows_ref, sems.at[steps])
    gain_copy.start()
    copies = []
    for i in range(steps):
        at = pl.ds(pl.multiple_of(first + i * step, step), step)
        copies.append(
            pltpu.make_async_copy(history_ref.at[at], rows_ref.at[pl.ds(i * step, step)], sems.at[i])
        )
        copies[i].start()
    gain_copy.wait()
    gain = gain_rows_ref[...].reshape(1, -1)
    for i in range(steps):
        copies[i].wait()
        at = pl.ds(i * step, step)
        out_ref[at, :] = normed(rows_ref[at, :], gain)


def mark(live_ref, told_ref, base, key_blocks, first):
    for b in range(told_ref.shape[0]):
        for g in range(key_blocks):
            live_ref[(first + b) * 8 + g] = 0.0

        def entry(t, unused):
            g = told_ref[b, t] - base
            live_ref[(first + b) * 8 + jnp.where((g >= 0) & (g < key_blocks), g, 7)] = SCALE
            return unused

        lax.fori_loop(0, told_ref[b, MAXK], entry, 0)


def tile(scores, factor):
    half = scores * factor
    return half * jnp.tanh(half) + half


def attend_dense(query_ref, rows, sums_ref, keys_t_ref, values_ref, factors):
    n, blocks = len(factors), len(factors[0])
    for h in range(query_ref.shape[1] // DH):
        cols = pl.ds(h * DH, DH)
        scores = jnp.dot(
            query_ref[rows, cols], keys_t_ref[cols, :], preferred_element_type=jnp.float32
        )
        weights = [
            jnp.concatenate(
                [
                    tile(scores[i * BLK : (i + 1) * BLK, g * BLK : (g + 1) * BLK], factors[i][g])
                    for i in range(n)
                ],
                axis=0,
            ).astype(jnp.bfloat16)
            for g in range(blocks)
        ]
        sums_ref[rows, cols] += jnp.dot(
            jnp.concatenate(weights, axis=1), values_ref[:, cols], preferred_element_type=jnp.float32
        )


def attend_all(query_ref, sums_ref, keys_t_ref, values_ref, live_ref, live_first, key_blocks):
    n = 2

    def some(p, unused):
        factors = [
            [live_ref[(live_first + n * p + i) * 8 + g] for g in range(key_blocks)] for i in range(n)
        ]

        @pl.when(sum(sum(f) for f in factors) > 0.0)
        def _():
            rows = pl.ds(pl.multiple_of(p * n * BLK, n * BLK), n * BLK)
            attend_dense(query_ref, rows, sums_ref, keys_t_ref, values_ref, factors)

        return unused

    lax.fori_loop(0, query_ref.shape[0] // (n * BLK), some, 0)


def fetch(pairs, sems):
    copies = [pltpu.make_async_copy(a, b, sems.at[i]) for i, (a, b) in enumerate(pairs)]
    for copy in copies:
        copy.start()
    return copies


def wait(copies):
    for copy in copies:
        copy.wait()


def own_kernel(
    history_hbm, gain_hbm, w_ref, gate_hbm, both_hbm, query_hbm, keys_t_hbm, tail_hbm,
    history_ref, gain_ref, gate_ref, both_ref, query_ref, keys_t_ref, sems, out_sems,
):
    rows = query_ref.shape[0]
    part = 2 * BLK
    parts = [pl.ds(p * part, part) for p in range(rows // part)]
    gain_copy, *copies = fetch(
        [(gain_hbm, gain_ref)] + [(history_hbm.at[at], history_ref.at[at]) for at in parts], sems
    )
    gain_copy.wait()
    gain = gain_ref[...].reshape(1, -1)
    for p, (at, copy) in enumerate(zip(parts, copies)):
        copy.wait()
        here = normed(history_ref[at, :], gain)
        query_ref[at, :] = project(here, w_ref[2]).astype(jnp.bfloat16)
        keys = project(here, w_ref[3])
        keys_t_ref[:, at] = keys.T.astype(jnp.bfloat16)
        both_ref[at, :] = keys.astype(jnp.bfloat16)
        both_ref[pl.ds(rows + p * part, part), :] = project(here, w_ref[1]).astype(jnp.bfloat16)
        gate_ref[at, :] = project(here, w_ref[0]).astype(jnp.bfloat16)
    wait(
        fetch(
            [
                (query_ref, query_hbm), (both_ref, both_hbm), (keys_t_ref, keys_t_hbm), (gate_ref, gate_hbm),
                (both_ref.at[pl.ds(rows - BLK, BLK)], tail_hbm.at[0]),
                (both_ref.at[pl.ds(2 * rows - BLK, BLK)], tail_hbm.at[1]),
            ],
            out_sems,
        )
    )


def own_attend_kernel(
    told_ref, query_hbm, keys_t_hbm, both_hbm, sums_hbm, query_ref, keys_t_ref, values_ref, sums_ref, live_ref, sems
):
    rows, cols = query_ref.shape
    blocks = rows // BLK
    copies = fetch(
        [
            (query_hbm, query_ref), (keys_t_hbm, keys_t_ref),
            (both_hbm.at[pl.ds(rows, rows)], values_ref),
        ],
        sems,
    )
    mark(live_ref, told_ref, lax.axis_index("seq") * blocks, blocks, 0)
    wait(copies)
    behind = lax.broadcasted_iota(jnp.int32, (BLK, BLK), 1) <= lax.broadcasted_iota(
        jnp.int32, (BLK, BLK), 0
    )
    for p in range(blocks // 2):
        q_rows = pl.ds(p * 2 * BLK, 2 * BLK)
        seen = pl.ds(0, (2 * p + 2) * BLK)
        for h in range(cols // DH):
            at = pl.ds(h * DH, DH)
            scores = jnp.dot(
                query_ref[q_rows, at], keys_t_ref[at, seen], preferred_element_type=jnp.float32
            )
            weights = []
            for g in range(2 * p + 2):
                column = []
                for i in range(2):
                    b = 2 * p + i
                    if g > b:
                        column.append(jnp.zeros((BLK, BLK), jnp.float32))
                        continue
                    some = tile(
                        scores[i * BLK : (i + 1) * BLK, g * BLK : (g + 1) * BLK], live_ref[b * 8 + g]
                    )
                    column.append(jnp.where(behind, some, 0.0) if g == b else some)
                weights.append(jnp.concatenate(column, axis=0).astype(jnp.bfloat16))
            sums_ref[q_rows, at] = jnp.dot(
                jnp.concatenate(weights, axis=1),
                values_ref[seen, at],
                preferred_element_type=jnp.float32,
            )
    wait(fetch([(sums_ref, sums_hbm)], sems))


def centred(part):
    return part - jnp.mean(part, axis=-1, keepdims=True)


def send_off(sums_ref, send_ref):
    for h in range(send_ref.shape[1] // DH):
        at = pl.ds(h * DH, DH)
        send_ref[:, at] = centred(sums_ref[:, at]).astype(jnp.bfloat16)


def chunk_keys(pieces, w_ref, keys_ref, keys_t_ref, values_ref):
    share = pieces[0].shape[0]
    for m, piece in enumerate(pieces):
        at = pl.ds(pl.multiple_of((lax.axis_index("head") ^ m) * share, share), share)
        keys_ref[at, :] = project(piece[...], w_ref[3])
        values_ref[at, :] = project(piece[...], w_ref[1]).astype(jnp.bfloat16)
    keys_t_ref[...] = keys_ref[...].T.astype(jnp.bfloat16)


def make_chunk_kernel(back, n_head):
    def kernel(told_ref, told_x_ref, *refs):
        pieces, refs = refs[:n_head], refs[n_head:]
        w_ref, query_hbm, query_x_hbm, own_t_hbm, own_both_hbm, before_hbm, sums_hbm, sums_x_hbm = refs[:8]
        query_ref, query_x_ref, own_t_ref, own_values_ref, sums_ref, sums_x_ref = refs[8:14]
        keys_ref, keys_t_ref, values_ref, live_ref, sems, out_sems = refs[14:]
        blocks = query_ref.shape[0] // BLK
        here = lax.axis_index("seq")
        source = here - 2 * back
        copies = fetch(
            [
                (query_x_hbm, query_x_ref), (own_t_hbm, own_t_ref),
                (own_both_hbm.at[pl.ds(blocks * BLK, blocks * BLK)], own_values_ref),
                (before_hbm, sums_ref), (query_hbm, query_ref),
            ],
            sems,
        )
        sums_x_ref[...] = jnp.zeros_like(sums_x_ref)
        mark(live_ref, told_x_ref, here * blocks, blocks, 0)

        @pl.when(source >= 0)
        def _():
            chunk_keys(pieces, w_ref, keys_ref, keys_t_ref, values_ref)

        wait(copies)
        attend_all(query_x_ref, sums_x_ref, own_t_ref, own_values_ref, live_ref, 0, blocks)

        @pl.when(source >= 0)
        def _():
            mark(live_ref, told_ref, source * blocks, blocks, 0)
            mark(live_ref, told_x_ref, source * blocks, blocks, blocks)
            attend_all(query_ref, sums_ref, keys_t_ref, values_ref, live_ref, 0, blocks)
            attend_all(query_x_ref, sums_x_ref, keys_t_ref, values_ref, live_ref, blocks, blocks)

        wait(fetch([(sums_ref, sums_hbm), (sums_x_ref, sums_x_hbm)], out_sems))

    return kernel


def make_last_kernel(back, n_head):
    def kernel(told_x_ref, *refs):
        pieces, refs = refs[:n_head], refs[n_head:]
        w_ref, query_x_hbm, before_hbm, send_ref, keys_t_ref, values_ref = refs[:6]
        query_x_ref, sums_ref, keys_ref, live_ref, sems = refs[6:]
        blocks = query_x_ref.shape[0] // BLK
        source = lax.axis_index("seq") - 2 * back
        copies = fetch([(query_x_hbm, query_x_ref), (before_hbm, sums_ref)], sems)

        @pl.when(source >= 0)
        def _():
            chunk_keys(pieces, w_ref, keys_ref, keys_t_ref, values_ref)
            mark(live_ref, told_x_ref, source * blocks, blocks, 0)

        wait(copies)

        @pl.when(source >= 0)
        def _():
            attend_all(query_x_ref, sums_ref, keys_t_ref, values_ref, live_ref, 0, blocks)

        send_off(sums_ref, send_ref)

    return kernel


def make_own_last_kernel(back):
    def kernel(
        told_ref, query_hbm, keys_t_ref, values_ref, tail_ref, far_hbm, before_hbm, gate_hbm, gain_ref,
        sums_ref, scale_ref, query_ref, gate_ref, far_ref, far_t_ref, live_ref, sems, far_sems,
    ):
        rows, cols = query_ref.shape
        blocks = rows // BLK
        here = lax.axis_index("seq")
        source = here - 2 * back
        copies = fetch([(query_hbm, query_ref), (before_hbm, sums_ref), (gate_hbm, gate_ref)], sems)
        far_copies = fetch([(far_hbm, far_ref)], far_sems)
        mark(live_ref, told_ref, source * blocks, blocks, 0)
        wait(copies)

        @pl.when(source >= 0)
        def _():
            attend_all(query_ref, sums_ref, keys_t_ref, values_ref, live_ref, 0, blocks)

        wait(far_copies)
        far = here - FAR

        @pl.when((far >= 0) & (here % 2 == 0))
        def _():
            far_t_ref[...] = far_ref[0:rows, :].astype(jnp.float32).T.astype(jnp.bfloat16)
            mark(live_ref, told_ref, far * blocks, blocks, 0)
            attend_all(query_ref, sums_ref, far_t_ref, far_ref.at[pl.ds(rows, rows)], live_ref, 0, blocks)

        farthest = here - FAR - 1

        @pl.when(farthest >= 0)
        def _():
            mark(live_ref, told_ref, farthest * blocks + blocks - 1, 1, 0)
            for h in range(cols // DH):
                at = pl.ds(h * DH, DH)
                scores = lax.dot_general(
                    query_ref[0:BLK, at], tail_ref[0, :, at], NT, preferred_element_type=jnp.float32
                )
                weights = tile(scores, live_ref[0]).astype(jnp.bfloat16)
                sums_ref[0:BLK, at] += jnp.dot(
                    weights, tail_ref[1, :, at], preferred_element_type=jnp.float32
                )

        scale_ref[...] = gain_ref[...].reshape(1, -1).astype(jnp.float32) * gate_ref[...].astype(
            jnp.float32
        )
        for h in range(cols // DH):
            at = pl.ds(h * DH, DH)
            sums_ref[:, at] = centred(sums_ref[:, at])

    return kernel


def finish_kernel(sums_ref, near_ref, scale_ref, out_ref):
    for h in range(sums_ref.shape[1] // DH):
        at = pl.ds(h * DH, DH)
        part = sums_ref[:, at] + near_ref[:, at].astype(jnp.float32)
        off = centred(part)
        spread_sq = jnp.mean(jnp.square(off), axis=-1, keepdims=True)
        out_ref[:, at] = (off * lax.rsqrt(spread_sq + EPS) * scale_ref[:, at]).astype(jnp.bfloat16)


def mix(total, pieces, w_ref):
    cols = pieces[0].shape[1]
    for m, piece in enumerate(pieces):
        w = w_ref[m * cols : (m + 1) * cols, :]
        total = total + jnp.dot(piece[...], w, preferred_element_type=jnp.float32)
    return total


def near_out_kernel(*refs):
    n = (len(refs) - 7) // 3
    pieces, w_hbm, refs = refs[:n], refs[n : 3 * n], refs[3 * n :]
    history_hbm, out_ref, w_far_ref, w_near_ref, history_ref, sems, w_sems = refs
    cols = out_ref.shape[1]
    rows = w_hbm[0].shape[0]
    at = pl.ds(pl.multiple_of(lax.axis_index("head") * cols, cols), cols)
    copies = fetch([(history_hbm.at[:, at], history_ref)], sems)
    w_copies = fetch(
        [
            (w.at[:, at], (w_near_ref if m < n else w_far_ref).at[pl.ds(m % n * rows, rows)])
            for m, w in enumerate(w_hbm)
        ],
        w_sems,
    )
    wait(copies)
    wait(w_copies)
    out_ref[...] = mix(history_ref[...].astype(jnp.float32), pieces, w_near_ref)


def far_out_kernel(*refs):
    *pieces, w_ref, near_ref, out_ref = refs
    out_ref[...] = mix(near_ref[...], pieces, w_ref).astype(jnp.bfloat16)


def crossed(array, axis, bit):
    return lax.ppermute(array, axis, [(i, i ^ bit) for i in range(lax.axis_size(axis))])


def spread(piece, bit):
    pieces = {0: piece}
    while bit:
        pieces.update({m + bit: crossed(p, "head", bit) for m, p in list(pieces.items())})
        bit //= 2
    return [pieces[m] for m in sorted(pieces)]


def body(history, ln_gain, w_in, out_gain, w_out, block_lists, counts):
    tok_rows, width = history.shape
    blocks = counts.shape[0]
    cols = w_in.shape[2]
    n_seq, n_head = lax.axis_size("seq"), lax.axis_size("head")
    assert 2 * (PLANES + 1) * blocks - (WIN - 1) == blocks - 1
    barrier = lax.optimization_barrier

    shape = lambda like, *dims: jax.ShapeDtypeStruct(dims, like)
    bf16, f32 = jnp.bfloat16, jnp.float32
    wide = pl.BlockSpec(memory_space=pltpu.VMEM)
    flat = pl.BlockSpec(memory_space=pltpu.SMEM)
    far_off = pl.BlockSpec(memory_space=pltpu.HBM)
    n_live = 2 * blocks * 8
    upright, lying = (tok_rows, cols), (cols, tok_rows)
    sems = lambda n: pltpu.SemaphoreType.DMA((n,))
    live = pltpu.SMEM((n_live,), f32)

    share_rows = tok_rows // n_head
    steps = share_rows // 48
    share = pl.pallas_call(
        norm_kernel,
        in_specs=[far_off] * 2,
        out_specs=wide,
        out_shape=shape(bf16, share_rows, width),
        scratch_shapes=[
            pltpu.VMEM((share_rows, width), bf16),
            pltpu.VMEM((width,), bf16),
            sems(steps + 1),
        ],
        cost_estimate=cost(2),
        compiler_params=params(60),
    )(history, ln_gain)
    gain, block_lists, counts, w_out, share = barrier((ln_gain, block_lists, counts, w_out, share))
    told = jnp.concatenate([block_lists, counts[:, None]], axis=1)
    upward = [(i, i + 2) for i in range(n_seq - 2)]
    share_1 = lax.ppermute(share, "seq", upward)

    gate, both, query, keys_t, tail = pl.pallas_call(
        own_kernel,
        in_specs=[far_off, far_off, wide],
        out_specs=[far_off] * 5,
        out_shape=[
            shape(bf16, *upright), shape(bf16, 2 * tok_rows, cols), shape(bf16, *upright),
            shape(bf16, *lying), shape(bf16, 2, BLK, cols),
        ],
        scratch_shapes=[
            pltpu.VMEM((tok_rows, width), bf16), pltpu.VMEM((width,), bf16), pltpu.VMEM(upright, bf16),
            pltpu.VMEM((2 * tok_rows, cols), bf16), pltpu.VMEM(upright, bf16), pltpu.VMEM(lying, bf16),
            sems(1 + tok_rows // (2 * BLK)), sems(6),
        ],
        compiler_params=params(60),
        cost_estimate=cost(4),
    )(history, gain, w_in)

    w_cross = crossed(w_out, "head", n_head // 2)
    query_x = crossed(query, "seq", 1)
    share_1, query, w_cross = barrier((share_1, query, w_cross))
    share_2 = lax.ppermute(share_1, "seq", upward)
    cross_1 = crossed(share_1, "head", n_head // 2)
    told_x = crossed(told, "seq", 1)
    tail = lax.ppermute(tail, "seq", [(i, i + FAR + 1) for i in range(n_seq - FAR - 1)])
    told, told_x = barrier((told, told_x))
    own_sums = pl.pallas_call(
        own_attend_kernel,
        in_specs=[flat] + [far_off] * 3,
        out_specs=far_off,
        out_shape=shape(f32, *upright),
        scratch_shapes=[pltpu.VMEM(upright, bf16), pltpu.VMEM(lying, bf16), pltpu.VMEM(upright, bf16)]
        + [pltpu.VMEM(upright, f32), live, sems(3)],
        compiler_params=params(),
        cost_estimate=cost(4),
    )(told, query, keys_t, both)
    share_2, cross_1, own_sums, query_x = barrier((share_2, cross_1, own_sums, query_x))
    chunk_1 = spread(share_1, n_head // 4) + spread(cross_1, n_head // 4)
    cross_2 = crossed(share_2, "head", n_head // 2)
    near_2 = spread(share_2, n_head // 4)

    both, query_x, share_2 = barrier((both, query_x, share_2))
    far = lax.ppermute(both, "seq", [(i, i + FAR) for i in range(1, n_seq - FAR, 2)])

    sums, sums_x = pl.pallas_call(
        make_chunk_kernel(1, n_head),
        in_specs=[flat] * 2 + [wide] * (n_head + 1) + [far_off] * 5,
        out_specs=[far_off] * 2,
        out_shape=[shape(f32, *upright)] * 2,
        scratch_shapes=[
            pltpu.VMEM(dims, kind)
            for dims, kind in (
                (upright, bf16), (upright, bf16), (lying, bf16), (upright, bf16), (upright, f32),
                (upright, f32), (upright, f32), (lying, bf16), (upright, bf16),
            )
        ]
        + [live, sems(5), sems(2)],
        compiler_params=params(16),
        cost_estimate=cost(6),
    )(told, told_x, *chunk_1, w_in, query, query_x, keys_t, both, own_sums)

    cross_2, sums_x, tail = barrier((cross_2, sums_x, tail))
    send, keys_t, values = pl.pallas_call(
        make_last_kernel(PLANES, n_head),
        in_specs=[flat] + [wide] * (n_head + 1) + [far_off] * 2,
        out_specs=[wide] * 3,
        out_shape=[shape(bf16, *upright), shape(bf16, *lying), shape(bf16, *upright)],
        scratch_shapes=[
            pltpu.VMEM(upright, bf16), pltpu.VMEM(upright, f32), pltpu.VMEM(upright, f32), live, sems(2)
        ],
        compiler_params=params(),
        cost_estimate=cost(4),
    )(told_x, *near_2, *spread(cross_2, n_head // 4), w_in, query_x, sums_x)
    send, far = barrier((send, far))
    near = crossed(send, "seq", 1)
    send, w_out, w_cross = barrier((send, w_out, w_cross))
    w_all = spread(w_out, n_head // 4) + spread(w_cross, n_head // 4)
    mine, scale = pl.pallas_call(
        make_own_last_kernel(PLANES),
        in_specs=[flat, far_off, wide, wide, wide, far_off, far_off, far_off, wide],
        out_specs=[wide] * 2,
        out_shape=[shape(f32, *upright)] * 2,
        scratch_shapes=[pltpu.VMEM(upright, bf16)] * 2
        + [pltpu.VMEM((2 * tok_rows, cols), bf16), pltpu.VMEM(lying, bf16), live, sems(3), sems(1)],
        compiler_params=params(),
        cost_estimate=cost(3),
    )(told, query, keys_t, values, tail, far, sums, gate, out_gain)
    near, mine, w_all = barrier((near, mine, tuple(w_all)))
    gated = pl.pallas_call(
        finish_kernel,
        in_specs=[wide] * 3,
        out_specs=wide,
        out_shape=shape(bf16, *upright),
        compiler_params=params(),
        cost_estimate=cost(1),
    )(mine, near, scale)

    out_cols = width // n_head
    cross_gated = crossed(gated, "head", n_head // 2)
    near_gated = spread(gated, n_head // 4)
    half = n_head // 2
    mixed, w_far = pl.pallas_call(
        near_out_kernel,
        in_specs=[wide] * half + [far_off] * (n_head + 1),
        out_specs=[wide] * 2,
        out_shape=[shape(f32, tok_rows, out_cols), shape(bf16, half * cols, out_cols)],
        scratch_shapes=[
            pltpu.VMEM((half * cols, out_cols), bf16), pltpu.VMEM((tok_rows, out_cols), bf16),
            sems(1), sems(n_head),
        ],
        compiler_params=params(),
        cost_estimate=cost(2),
    )(*near_gated, *w_all, history)
    cross_gated, mixed = barrier((cross_gated, mixed))
    return pl.pallas_call(
        far_out_kernel,
        in_specs=[wide] * (half + 2),
        out_specs=wide,
        out_shape=shape(bf16, tok_rows, out_cols),
        compiler_params=params(),
        cost_estimate=cost(2),
    )(*spread(cross_gated, n_head // 4), w_far, mixed)


def solution(mesh):
    placed = (
        P("seq", None),
        P(),
        P(None, None, "head"),
        P("head"),
        P("head", None),
        P("seq", None),
        P("seq"),
    )
    return jax.shard_map(
        body, mesh=mesh, in_specs=placed, out_specs=P("seq", "head"), check_vma=False
    )
```

```python
import jax
import jax.numpy as jnp
from jax import lax
from jax.experimental import pallas as pl
from jax.experimental.pallas import tpu as pltpu
from jax.sharding import PartitionSpec as P

DH = 128
BLK = 128
WIN = 32
MAXK = 16
EPS = 1e-05
PLANES = 2
FAR = 2 * PLANES + 1
SCALE = 0.5 * DH ** (-0.5)

NT = (((1,), (1,)), ((), ()))


def params(mib=12):
    return pltpu.CompilerParams(vmem_limit_bytes=mib << 20)


def cost(us):
    return pl.CostEstimate(flops=int(us * 1e9 * 0.3), bytes_accessed=int(us * 3e6 * 0.3), transcendentals=0)


def silu(v):
    half = 0.5 * v
    return half * jnp.tanh(half) + half


def project(rows, w):
    return silu(jnp.dot(rows, w, preferred_element_type=jnp.float32))


def normed(rows, gain):
    floats = rows.astype(jnp.float32)
    centre = jnp.mean(floats, axis=-1, keepdims=True)
    off = floats - centre
    spread_sq = jnp.mean(jnp.square(off), axis=-1, keepdims=True)
    return (off * lax.rsqrt(spread_sq + EPS) * gain.astype(jnp.float32)).astype(jnp.bfloat16)


def norm_kernel(history_ref, gain_ref, out_ref, rows_ref, gain_rows_ref, sems):
    share = out_ref.shape[0]
    steps = sems.shape[0] - 1
    step = share // steps
    first = lax.axis_index("head") * share
    gain_copy = pltpu.make_async_copy(gain_ref, gain_rows_ref, sems.at[steps])
    gain_copy.start()
    copies = []
    for i in range(steps):
        at = pl.ds(pl.multiple_of(first + i * step, step), step)
        copies.append(
            pltpu.make_async_copy(history_ref.at[at], rows_ref.at[pl.ds(i * step, step)], sems.at[i])
        )
        copies[i].start()
    gain_copy.wait()
    gain = gain_rows_ref[...].reshape(1, -1)
    for i in range(steps):
        copies[i].wait()
        at = pl.ds(i * step, step)
        out_ref[at, :] = normed(rows_ref[at, :], gain)


def mark(live_ref, told_ref, base, key_blocks, first):
    for b in range(told_ref.shape[0]):
        for g in range(key_blocks):
            live_ref[(first + b) * 8 + g] = 0.0

        def entry(t, unused):
            g = told_ref[b, t] - base
            live_ref[(first + b) * 8 + jnp.where((g >= 0) & (g < key_blocks), g, 7)] = SCALE
            return unused

        lax.fori_loop(0, told_ref[b, MAXK], entry, 0)


def tile(scores, factor):
    half = scores * factor
    return half * jnp.tanh(half) + half


def attend_dense(query_ref, rows, sums_ref, keys_t_ref, values_ref, factors):
    n, blocks = len(factors), len(factors[0])
    for h in range(query_ref.shape[1] // DH):
        cols = pl.ds(h * DH, DH)
        scores = jnp.dot(
            query_ref[rows, cols], keys_t_ref[cols, :], preferred_element_type=jnp.float32
        )
        weights = [
            jnp.concatenate(
                [
                    tile(scores[i * BLK : (i + 1) * BLK, g * BLK : (g + 1) * BLK], factors[i][g])
                    for i in range(n)
                ],
                axis=0,
            ).astype(jnp.bfloat16)
            for g in range(blocks)
        ]
        sums_ref[rows, cols] += jnp.dot(
            jnp.concatenate(weights, axis=1), values_ref[:, cols], preferred_element_type=jnp.float32
        )


def attend_all(query_ref, sums_ref, keys_t_ref, values_ref, live_ref, live_first, key_blocks):
    n = 2

    def some(p, unused):
        factors = [
            [live_ref[(live_first + n * p + i) * 8 + g] for g in range(key_blocks)] for i in range(n)
        ]

        @pl.when(sum(sum(f) for f in factors) > 0.0)
        def _():
            rows = pl.ds(pl.multiple_of(p * n * BLK, n * BLK), n * BLK)
            attend_dense(query_ref, rows, sums_ref, keys_t_ref, values_ref, factors)

        return unused

    lax.fori_loop(0, query_ref.shape[0] // (n * BLK), some, 0)


def fetch(pairs, sems):
    copies = [pltpu.make_async_copy(a, b, sems.at[i]) for i, (a, b) in enumerate(pairs)]
    for copy in copies:
        copy.start()
    return copies


def wait(copies):
    for copy in copies:
        copy.wait()


def own_kernel(
    history_hbm, gain_hbm, w_ref, gate_hbm, both_hbm, query_hbm, keys_t_hbm, tail_hbm,
    history_ref, gain_ref, gate_ref, both_ref, query_ref, keys_t_ref, sems, out_sems,
):
    rows = query_ref.shape[0]
    part = 2 * BLK
    parts = [pl.ds(p * part, part) for p in range(rows // part)]
    gain_copy, *copies = fetch(
        [(gain_hbm, gain_ref)] + [(history_hbm.at[at], history_ref.at[at]) for at in parts], sems
    )
    gain_copy.wait()
    gain = gain_ref[...].reshape(1, -1)
    for p, (at, copy) in enumerate(zip(parts, copies)):
        copy.wait()
        here = normed(history_ref[at, :], gain)
        query_ref[at, :] = project(here, w_ref[2]).astype(jnp.bfloat16)
        keys = project(here, w_ref[3])
        keys_t_ref[:, at] = keys.T.astype(jnp.bfloat16)
        both_ref[at, :] = keys.astype(jnp.bfloat16)
        both_ref[pl.ds(rows + p * part, part), :] = project(here, w_ref[1]).astype(jnp.bfloat16)
        gate_ref[at, :] = project(here, w_ref[0]).astype(jnp.bfloat16)
    wait(
        fetch(
            [
                (query_ref, query_hbm), (both_ref, both_hbm), (keys_t_ref, keys_t_hbm), (gate_ref, gate_hbm),
                (both_ref.at[pl.ds(rows - BLK, BLK)], tail_hbm.at[0]),
                (both_ref.at[pl.ds(2 * rows - BLK, BLK)], tail_hbm.at[1]),
            ],
            out_sems,
        )
    )


def own_attend_kernel(
    told_ref, query_hbm, keys_t_hbm, both_hbm, sums_hbm, query_ref, keys_t_ref, values_ref, sums_ref, live_ref, sems
):
    rows, cols = query_ref.shape
    blocks = rows // BLK
    copies = fetch(
        [
            (query_hbm, query_ref), (keys_t_hbm, keys_t_ref),
            (both_hbm.at[pl.ds(rows, rows)], values_ref),
        ],
        sems,
    )
    mark(live_ref, told_ref, lax.axis_index("seq") * blocks, blocks, 0)
    wait(copies)
    behind = lax.broadcasted_iota(jnp.int32, (BLK, BLK), 1) <= lax.broadcasted_iota(
        jnp.int32, (BLK, BLK), 0
    )
    for p in range(blocks // 2):
        q_rows = pl.ds(p * 2 * BLK, 2 * BLK)
        seen = pl.ds(0, (2 * p + 2) * BLK)
        for h in range(cols // DH):
            at = pl.ds(h * DH, DH)
            scores = jnp.dot(
                query_ref[q_rows, at], keys_t_ref[at, seen], preferred_element_type=jnp.float32
            )
            weights = []
            for g in range(2 * p + 2):
                column = []
                for i in range(2):
                    b = 2 * p + i
                    if g > b:
                        column.append(jnp.zeros((BLK, BLK), jnp.float32))
                        continue
                    some = tile(
                        scores[i * BLK : (i + 1) * BLK, g * BLK : (g + 1) * BLK], live_ref[b * 8 + g]
                    )
                    column.append(jnp.where(behind, some, 0.0) if g == b else some)
                weights.append(jnp.concatenate(column, axis=0).astype(jnp.bfloat16))
            sums_ref[q_rows, at] = jnp.dot(
                jnp.concatenate(weights, axis=1),
                values_ref[seen, at],
                preferred_element_type=jnp.float32,
            )
    wait(fetch([(sums_ref, sums_hbm)], sems))


def centred(part):
    return part - jnp.mean(part, axis=-1, keepdims=True)


def send_off(sums_ref, send_ref):
    for h in range(send_ref.shape[1] // DH):
        at = pl.ds(h * DH, DH)
        send_ref[:, at] = centred(sums_ref[:, at]).astype(jnp.bfloat16)


def chunk_keys(pieces, w_ref, keys_ref, keys_t_ref, values_ref):
    share = pieces[0].shape[0]
    for m, piece in enumerate(pieces):
        at = pl.ds(pl.multiple_of((lax.axis_index("head") ^ m) * share, share), share)
        keys_ref[at, :] = project(piece[...], w_ref[3])
        values_ref[at, :] = project(piece[...], w_ref[1]).astype(jnp.bfloat16)
    keys_t_ref[...] = keys_ref[...].T.astype(jnp.bfloat16)


def make_chunk_kernel(back, n_head):
    def kernel(told_ref, told_x_ref, *refs):
        pieces, refs = refs[:n_head], refs[n_head:]
        w_ref, query_hbm, query_x_hbm, own_t_hbm, own_both_hbm, before_hbm, sums_hbm, sums_x_hbm = refs[:8]
        query_ref, query_x_ref, own_t_ref, own_values_ref, sums_ref, sums_x_ref = refs[8:14]
        keys_ref, keys_t_ref, values_ref, live_ref, sems, out_sems = refs[14:]
        blocks = query_ref.shape[0] // BLK
        here = lax.axis_index("seq")
        source = here - 2 * back
        copies = fetch(
            [
                (query_x_hbm, query_x_ref), (own_t_hbm, own_t_ref),
                (own_both_hbm.at[pl.ds(blocks * BLK, blocks * BLK)], own_values_ref),
                (before_hbm, sums_ref), (query_hbm, query_ref),
            ],
            sems,
        )
        sums_x_ref[...] = jnp.zeros_like(sums_x_ref)
        mark(live_ref, told_x_ref, here * blocks, blocks, 0)

        @pl.when(source >= 0)
        def _():
            chunk_keys(pieces, w_ref, keys_ref, keys_t_ref, values_ref)

        wait(copies)
        attend_all(query_x_ref, sums_x_ref, own_t_ref, own_values_ref, live_ref, 0, blocks)

        @pl.when(source >= 0)
        def _():
            mark(live_ref, told_ref, source * blocks, blocks, 0)
            mark(live_ref, told_x_ref, source * blocks, blocks, blocks)
            attend_all(query_ref, sums_ref, keys_t_ref, values_ref, live_ref, 0, blocks)
            attend_all(query_x_ref, sums_x_ref, keys_t_ref, values_ref, live_ref, blocks, blocks)

        wait(fetch([(sums_ref, sums_hbm), (sums_x_ref, sums_x_hbm)], out_sems))

    return kernel


def make_last_kernel(back, n_head):
    def kernel(told_x_ref, *refs):
        pieces, refs = refs[:n_head], refs[n_head:]
        w_ref, query_x_hbm, before_hbm, send_ref, keys_t_ref, values_ref = refs[:6]
        query_x_ref, sums_ref, keys_ref, live_ref, sems = refs[6:]
        blocks = query_x_ref.shape[0] // BLK
        source = lax.axis_index("seq") - 2 * back
        copies = fetch([(query_x_hbm, query_x_ref), (before_hbm, sums_ref)], sems)

        @pl.when(source >= 0)
        def _():
            chunk_keys(pieces, w_ref, keys_ref, keys_t_ref, values_ref)
            mark(live_ref, told_x_ref, source * blocks, blocks, 0)

        wait(copies)

        @pl.when(source >= 0)
        def _():
            attend_all(query_x_ref, sums_ref, keys_t_ref, values_ref, live_ref, 0, blocks)

        send_off(sums_ref, send_ref)

    return kernel


def make_own_last_kernel(back):
    def kernel(
        told_ref, query_hbm, keys_t_ref, values_ref, tail_ref, far_hbm, before_hbm, gate_hbm, gain_ref,
        sums_ref, scale_ref, query_ref, gate_ref, far_ref, far_t_ref, live_ref, sems, far_sems,
    ):
        rows, cols = query_ref.shape
        blocks = rows // BLK
        here = lax.axis_index("seq")
        source = here - 2 * back
        copies = fetch([(query_hbm, query_ref), (before_hbm, sums_ref), (gate_hbm, gate_ref)], sems)
        far_copies = fetch([(far_hbm, far_ref)], far_sems)
        mark(live_ref, told_ref, source * blocks, blocks, 0)
        wait(copies)

        @pl.when(source >= 0)
        def _():
            attend_all(query_ref, sums_ref, keys_t_ref, values_ref, live_ref, 0, blocks)

        wait(far_copies)
        far = here - FAR

        @pl.when((far >= 0) & (here % 2 == 0))
        def _():
            far_t_ref[...] = far_ref[0:rows, :].astype(jnp.float32).T.astype(jnp.bfloat16)
            mark(live_ref, told_ref, far * blocks, blocks, 0)
            attend_all(query_ref, sums_ref, far_t_ref, far_ref.at[pl.ds(rows, rows)], live_ref, 0, blocks)

        farthest = here - FAR - 1

        @pl.when(farthest >= 0)
        def _():
            mark(live_ref, told_ref, farthest * blocks + blocks - 1, 1, 0)
            for h in range(cols // DH):
                at = pl.ds(h * DH, DH)
                scores = lax.dot_general(
                    query_ref[0:BLK, at], tail_ref[0, :, at], NT, preferred_element_type=jnp.float32
                )
                weights = tile(scores, live_ref[0]).astype(jnp.bfloat16)
                sums_ref[0:BLK, at] += jnp.dot(
                    weights, tail_ref[1, :, at], preferred_element_type=jnp.float32
                )

        scale_ref[...] = gain_ref[...].reshape(1, -1).astype(jnp.float32) * gate_ref[...].astype(
            jnp.float32
        )
        for h in range(cols // DH):
            at = pl.ds(h * DH, DH)
            sums_ref[:, at] = centred(sums_ref[:, at])

    return kernel


def finish_kernel(sums_ref, near_ref, scale_ref, out_ref):
    for h in range(sums_ref.shape[1] // DH):
        at = pl.ds(h * DH, DH)
        part = sums_ref[:, at] + near_ref[:, at].astype(jnp.float32)
        off = centred(part)
        spread_sq = jnp.mean(jnp.square(off), axis=-1, keepdims=True)
        out_ref[:, at] = (off * lax.rsqrt(spread_sq + EPS) * scale_ref[:, at]).astype(jnp.bfloat16)


def mix(total, pieces, w_ref):
    cols = pieces[0].shape[1]
    for m, piece in enumerate(pieces):
        w = w_ref[m * cols : (m + 1) * cols, :]
        total = total + jnp.dot(piece[...], w, preferred_element_type=jnp.float32)
    return total


def near_out_kernel(*refs):
    n = (len(refs) - 7) // 3
    pieces, w_hbm, refs = refs[:n], refs[n : 3 * n], refs[3 * n :]
    history_hbm, out_ref, w_far_ref, w_near_ref, history_ref, sems, w_sems = refs
    cols = out_ref.shape[1]
    rows = w_hbm[0].shape[0]
    at = pl.ds(pl.multiple_of(lax.axis_index("head") * cols, cols), cols)
    copies = fetch([(history_hbm.at[:, at], history_ref)], sems)
    w_copies = fetch(
        [
            (w.at[:, at], (w_near_ref if m < n else w_far_ref).at[pl.ds(m % n * rows, rows)])
            for m, w in enumerate(w_hbm)
        ],
        w_sems,
    )
    wait(copies)
    wait(w_copies)
    out_ref[...] = mix(history_ref[...].astype(jnp.float32), pieces, w_near_ref)


def far_out_kernel(*refs):
    *pieces, w_ref, near_ref, out_ref = refs
    out_ref[...] = mix(near_ref[...], pieces, w_ref).astype(jnp.bfloat16)


def crossed(array, axis, bit):
    return lax.ppermute(array, axis, [(i, i ^ bit) for i in range(lax.axis_size(axis))])


def spread(piece, bit):
    pieces = {0: piece}
    while bit:
        pieces.update({m + bit: crossed(p, "head", bit) for m, p in list(pieces.items())})
        bit //= 2
    return [pieces[m] for m in sorted(pieces)]


def body(history, ln_gain, w_in, out_gain, w_out, block_lists, counts):
    tok_rows, width = history.shape
    blocks = counts.shape[0]
    cols = w_in.shape[2]
    n_seq, n_head = lax.axis_size("seq"), lax.axis_size("head")
    assert 2 * (PLANES + 1) * blocks - (WIN - 1) == blocks - 1
    barrier = lax.optimization_barrier

    shape = lambda like, *dims: jax.ShapeDtypeStruct(dims, like)
    bf16, f32 = jnp.bfloat16, jnp.float32
    wide = pl.BlockSpec(memory_space=pltpu.VMEM)
    flat = pl.BlockSpec(memory_space=pltpu.SMEM)
    far_off = pl.BlockSpec(memory_space=pltpu.HBM)
    n_live = 2 * blocks * 8
    upright, lying = (tok_rows, cols), (cols, tok_rows)
    sems = lambda n: pltpu.SemaphoreType.DMA((n,))
    live = pltpu.SMEM((n_live,), f32)

    share_rows = tok_rows // n_head
    steps = share_rows // 48
    share = pl.pallas_call(
        norm_kernel,
        in_specs=[far_off] * 2,
        out_specs=wide,
        out_shape=shape(bf16, share_rows, width),
        scratch_shapes=[
            pltpu.VMEM((share_rows, width), bf16),
            pltpu.VMEM((width,), bf16),
            sems(steps + 1),
        ],
        cost_estimate=cost(2),
        compiler_params=params(60),
    )(history, ln_gain)
    gain, block_lists, counts, w_out, share = barrier((ln_gain, block_lists, counts, w_out, share))
    told = jnp.concatenate([block_lists, counts[:, None]], axis=1)
    upward = [(i, i + 2) for i in range(n_seq - 2)]
    share_1 = lax.ppermute(share, "seq", upward)

    gate, both, query, keys_t, tail = pl.pallas_call(
        own_kernel,
        in_specs=[far_off, far_off, wide],
        out_specs=[far_off] * 5,
        out_shape=[
            shape(bf16, *upright), shape(bf16, 2 * tok_rows, cols), shape(bf16, *upright),
            shape(bf16, *lying), shape(bf16, 2, BLK, cols),
        ],
        scratch_shapes=[
            pltpu.VMEM((tok_rows, width), bf16), pltpu.VMEM((width,), bf16), pltpu.VMEM(upright, bf16),
            pltpu.VMEM((2 * tok_rows, cols), bf16), pltpu.VMEM(upright, bf16), pltpu.VMEM(lying, bf16),
            sems(1 + tok_rows // (2 * BLK)), sems(6),
        ],
        compiler_params=params(60),
        cost_estimate=cost(4),
    )(history, gain, w_in)

    w_cross = crossed(w_out, "head", n_head // 2)
    query_x = crossed(query, "seq", 1)
    share_1, query, w_cross = barrier((share_1, query, w_cross))
    share_2 = lax.ppermute(share_1, "seq", upward[2:])
    cross_1 = crossed(share_1, "head", n_head // 2)
    told_x = crossed(told, "seq", 1)
    told, told_x, tail = barrier((told, told_x, tail))
    tail = lax.ppermute(tail, "seq", [(i, i + FAR + 1) for i in range(n_seq - FAR - 1)])
    own_sums = pl.pallas_call(
        own_attend_kernel,
        in_specs=[flat] + [far_off] * 3,
        out_specs=far_off,
        out_shape=shape(f32, *upright),
        scratch_shapes=[pltpu.VMEM(upright, bf16), pltpu.VMEM(lying, bf16), pltpu.VMEM(upright, bf16)]
        + [pltpu.VMEM(upright, f32), live, sems(3)],
        compiler_params=params(),
        cost_estimate=cost(4),
    )(told, query, keys_t, both)
    share_2, cross_1, own_sums, query_x, tail = barrier((share_2, cross_1, own_sums, query_x, tail))
    chunk_1 = spread(share_1, n_head // 4) + spread(cross_1, n_head // 4)
    cross_2 = crossed(share_2, "head", n_head // 2)
    near_2 = spread(share_2, n_head // 4)

    both, query_x, share_2, tail = barrier((both, query_x, share_2, tail))
    far = lax.ppermute(both, "seq", [(i, i + FAR) for i in range(1, n_seq - FAR, 2)])

    sums, sums_x = pl.pallas_call(
        make_chunk_kernel(1, n_head),
        in_specs=[flat] * 2 + [wide] * (n_head + 1) + [far_off] * 5,
        out_specs=[far_off] * 2,
        out_shape=[shape(f32, *upright)] * 2,
        scratch_shapes=[
            pltpu.VMEM(dims, kind)
            for dims, kind in (
                (upright, bf16), (upright, bf16), (lying, bf16), (upright, bf16), (upright, f32),
                (upright, f32), (upright, f32), (lying, bf16), (upright, bf16),
            )
        ]
        + [live, sems(5), sems(2)],
        compiler_params=params(16),
        cost_estimate=cost(6),
    )(told, told_x, *chunk_1, w_in, query, query_x, keys_t, both, own_sums)

    cross_2, sums_x = barrier((cross_2, sums_x))
    send, keys_t, values = pl.pallas_call(
        make_last_kernel(PLANES, n_head),
        in_specs=[flat] + [wide] * (n_head + 1) + [far_off] * 2,
        out_specs=[wide] * 3,
        out_shape=[shape(bf16, *upright), shape(bf16, *lying), shape(bf16, *upright)],
        scratch_shapes=[
            pltpu.VMEM(upright, bf16), pltpu.VMEM(upright, f32), pltpu.VMEM(upright, f32), live, sems(2)
        ],
        compiler_params=params(),
        cost_estimate=cost(4),
    )(told_x, *near_2, *spread(cross_2, n_head // 4), w_in, query_x, sums_x)
    near = crossed(send, "seq", 1)
    far, send, w_out, w_cross = barrier((far, send, w_out, w_cross))
    w_all = spread(w_out, n_head // 4) + spread(w_cross, n_head // 4)
    mine, scale = pl.pallas_call(
        make_own_last_kernel(PLANES),
        in_specs=[flat, far_off, wide, wide, wide, far_off, far_off, far_off, wide],
        out_specs=[wide] * 2,
        out_shape=[shape(f32, *upright)] * 2,
        scratch_shapes=[pltpu.VMEM(upright, bf16)] * 2
        + [pltpu.VMEM((2 * tok_rows, cols), bf16), pltpu.VMEM(lying, bf16), live, sems(3), sems(1)],
        compiler_params=params(),
        cost_estimate=cost(3),
    )(told, query, keys_t, values, tail, far, sums, gate, out_gain)
    near, mine, w_all = barrier((near, mine, tuple(w_all)))
    gated = pl.pallas_call(
        finish_kernel,
        in_specs=[wide] * 3,
        out_specs=wide,
        out_shape=shape(bf16, *upright),
        compiler_params=params(),
        cost_estimate=cost(1),
    )(mine, near, scale)

    out_cols = width // n_head
    cross_gated = crossed(gated, "head", n_head // 2)
    near_gated = spread(gated, n_head // 4)
    half = n_head // 2
    mixed, w_far = pl.pallas_call(
        near_out_kernel,
        in_specs=[wide] * half + [far_off] * (n_head + 1),
        out_specs=[wide] * 2,
        out_shape=[shape(f32, tok_rows, out_cols), shape(bf16, half * cols, out_cols)],
        scratch_shapes=[
            pltpu.VMEM((half * cols, out_cols), bf16), pltpu.VMEM((tok_rows, out_cols), bf16),
            sems(1), sems(n_head),
        ],
        compiler_params=params(),
        cost_estimate=cost(2),
    )(*near_gated, *w_all, history)
    cross_gated, mixed = barrier((cross_gated, mixed))
    return pl.pallas_call(
        far_out_kernel,
        in_specs=[wide] * (half + 2),
        out_specs=wide,
        out_shape=shape(bf16, tok_rows, out_cols),
        compiler_params=params(),
        cost_estimate=cost(2),
    )(*spread(cross_gated, n_head // 4), w_far, mixed)


def solution(mesh):
    placed = (
        P("seq", None),
        P(),
        P(None, None, "head"),
        P("head"),
        P("head", None),
        P("seq", None),
        P("seq"),
    )
    return jax.shard_map(
        body, mesh=mesh, in_specs=placed, out_specs=P("seq", "head"), check_vma=False
    )
```

```python
import jax
import jax.numpy as jnp
from jax import lax
from jax.experimental import pallas as pl
from jax.experimental.pallas import tpu as pltpu
from jax.sharding import PartitionSpec as P

DH = 128
BLK = 128
WIN = 32
MAXK = 16
EPS = 1e-05
PLANES = 2
FAR = 2 * PLANES + 1
SCALE = 0.5 * DH ** (-0.5)

NT = (((1,), (1,)), ((), ()))


def params(mib=12):
    return pltpu.CompilerParams(vmem_limit_bytes=mib << 20)


def cost(us):
    return pl.CostEstimate(flops=int(us * 1e9 * 0.3), bytes_accessed=int(us * 3e6 * 0.3), transcendentals=0)


def silu(v):
    half = 0.5 * v
    return half * jnp.tanh(half) + half


def project(rows, w):
    return silu(jnp.dot(rows, w, preferred_element_type=jnp.float32))


def normed(rows, gain):
    floats = rows.astype(jnp.float32)
    centre = jnp.mean(floats, axis=-1, keepdims=True)
    off = floats - centre
    spread_sq = jnp.mean(jnp.square(off), axis=-1, keepdims=True)
    return (off * lax.rsqrt(spread_sq + EPS) * gain.astype(jnp.float32)).astype(jnp.bfloat16)


def norm_kernel(history_ref, gain_ref, out_ref, rows_ref, gain_rows_ref, sems):
    share = out_ref.shape[0]
    steps = sems.shape[0] - 1
    step = share // steps
    first = lax.axis_index("head") * share
    gain_copy = pltpu.make_async_copy(gain_ref, gain_rows_ref, sems.at[steps])
    gain_copy.start()
    copies = []
    for i in range(steps):
        at = pl.ds(pl.multiple_of(first + i * step, step), step)
        copies.append(
            pltpu.make_async_copy(history_ref.at[at], rows_ref.at[pl.ds(i * step, step)], sems.at[i])
        )
        copies[i].start()
    gain_copy.wait()
    gain = gain_rows_ref[...].reshape(1, -1)
    for i in range(steps):
        copies[i].wait()
        at = pl.ds(i * step, step)
        out_ref[at, :] = normed(rows_ref[at, :], gain)


def mark(live_ref, told_ref, base, key_blocks, first):
    for b in range(told_ref.shape[0]):
        for g in range(key_blocks):
            live_ref[(first + b) * 8 + g] = 0.0

        def entry(t, unused):
            g = told_ref[b, t] - base
            live_ref[(first + b) * 8 + jnp.where((g >= 0) & (g < key_blocks), g, 7)] = SCALE
            return unused

        lax.fori_loop(0, told_ref[b, MAXK], entry, 0)


def tile(scores, factor):
    half = scores * factor
    return half * jnp.tanh(half) + half


def attend_dense(query_ref, rows, sums_ref, keys_t_ref, values_ref, factors):
    n, blocks = len(factors), len(factors[0])
    for h in range(query_ref.shape[1] // DH):
        cols = pl.ds(h * DH, DH)
        scores = jnp.dot(
            query_ref[rows, cols], keys_t_ref[cols, :], preferred_element_type=jnp.float32
        )
        weights = [
            jnp.concatenate(
                [
                    tile(scores[i * BLK : (i + 1) * BLK, g * BLK : (g + 1) * BLK], factors[i][g])
                    for i in range(n)
                ],
                axis=0,
            ).astype(jnp.bfloat16)
            for g in range(blocks)
        ]
        sums_ref[rows, cols] += jnp.dot(
            jnp.concatenate(weights, axis=1), values_ref[:, cols], preferred_element_type=jnp.float32
        )


def attend_all(query_ref, sums_ref, keys_t_ref, values_ref, live_ref, live_first, key_blocks):
    n = 2

    def some(p, unused):
        factors = [
            [live_ref[(live_first + n * p + i) * 8 + g] for g in range(key_blocks)] for i in range(n)
        ]

        @pl.when(sum(sum(f) for f in factors) > 0.0)
        def _():
            rows = pl.ds(pl.multiple_of(p * n * BLK, n * BLK), n * BLK)
            attend_dense(query_ref, rows, sums_ref, keys_t_ref, values_ref, factors)

        return unused

    lax.fori_loop(0, query_ref.shape[0] // (n * BLK), some, 0)


def fetch(pairs, sems):
    copies = [pltpu.make_async_copy(a, b, sems.at[i]) for i, (a, b) in enumerate(pairs)]
    for copy in copies:
        copy.start()
    return copies


def wait(copies):
    for copy in copies:
        copy.wait()


def own_kernel(
    history_hbm, gain_hbm, w_ref, gate_hbm, both_hbm, query_hbm, keys_t_hbm, tail_hbm,
    history_ref, gain_ref, gate_ref, both_ref, query_ref, keys_t_ref, sems, out_sems,
):
    rows = query_ref.shape[0]
    part = 2 * BLK
    parts = [pl.ds(p * part, part) for p in range(rows // part)]
    gain_copy, *copies = fetch(
        [(gain_hbm, gain_ref)] + [(history_hbm.at[at], history_ref.at[at]) for at in parts], sems
    )
    gain_copy.wait()
    gain = gain_ref[...].reshape(1, -1)
    for p, (at, copy) in enumerate(zip(parts, copies)):
        copy.wait()
        here = normed(history_ref[at, :], gain)
        query_ref[at, :] = project(here, w_ref[2]).astype(jnp.bfloat16)
        keys = project(here, w_ref[3])
        keys_t_ref[:, at] = keys.T.astype(jnp.bfloat16)
        both_ref[at, :] = keys.astype(jnp.bfloat16)
        both_ref[pl.ds(rows + p * part, part), :] = project(here, w_ref[1]).astype(jnp.bfloat16)
        gate_ref[at, :] = project(here, w_ref[0]).astype(jnp.bfloat16)
    wait(
        fetch(
            [
                (query_ref, query_hbm), (both_ref, both_hbm), (keys_t_ref, keys_t_hbm), (gate_ref, gate_hbm),
                (both_ref.at[pl.ds(rows - BLK, BLK)], tail_hbm.at[0]),
                (both_ref.at[pl.ds(2 * rows - BLK, BLK)], tail_hbm.at[1]),
            ],
            out_sems,
        )
    )


def own_attend_kernel(
    told_ref, query_hbm, keys_t_hbm, both_hbm, sums_hbm, query_ref, keys_t_ref, values_ref, sums_ref, live_ref, sems
):
    rows, cols = query_ref.shape
    blocks = rows // BLK
    copies = fetch(
        [
            (query_hbm, query_ref), (keys_t_hbm, keys_t_ref),
            (both_hbm.at[pl.ds(rows, rows)], values_ref),
        ],
        sems,
    )
    mark(live_ref, told_ref, lax.axis_index("seq") * blocks, blocks, 0)
    wait(copies)
    behind = lax.broadcasted_iota(jnp.int32, (BLK, BLK), 1) <= lax.broadcasted_iota(
        jnp.int32, (BLK, BLK), 0
    )
    for p in range(blocks // 2):
        q_rows = pl.ds(p * 2 * BLK, 2 * BLK)
        seen = pl.ds(0, (2 * p + 2) * BLK)
        for h in range(cols // DH):
            at = pl.ds(h * DH, DH)
            scores = jnp.dot(
                query_ref[q_rows, at], keys_t_ref[at, seen], preferred_element_type=jnp.float32
            )
            weights = []
            for g in range(2 * p + 2):
                column = []
                for i in range(2):
                    b = 2 * p + i
                    if g > b:
                        column.append(jnp.zeros((BLK, BLK), jnp.float32))
                        continue
                    some = tile(
                        scores[i * BLK : (i + 1) * BLK, g * BLK : (g + 1) * BLK], live_ref[b * 8 + g]
                    )
                    column.append(jnp.where(behind, some, 0.0) if g == b else some)
                weights.append(jnp.concatenate(column, axis=0).astype(jnp.bfloat16))
            sums_ref[q_rows, at] = jnp.dot(
                jnp.concatenate(weights, axis=1),
                values_ref[seen, at],
                preferred_element_type=jnp.float32,
            )
    wait(fetch([(sums_ref, sums_hbm)], sems))


def centred(part):
    return part - jnp.mean(part, axis=-1, keepdims=True)


def send_off(sums_ref, send_ref):
    for h in range(send_ref.shape[1] // DH):
        at = pl.ds(h * DH, DH)
        send_ref[:, at] = centred(sums_ref[:, at]).astype(jnp.bfloat16)


def chunk_keys(pieces, w_ref, keys_ref, keys_t_ref, values_ref):
    share = pieces[0].shape[0]
    for m, piece in enumerate(pieces):
        at = pl.ds(pl.multiple_of((lax.axis_index("head") ^ m) * share, share), share)
        keys_ref[at, :] = project(piece[...], w_ref[3])
        values_ref[at, :] = project(piece[...], w_ref[1]).astype(jnp.bfloat16)
    keys_t_ref[...] = keys_ref[...].T.astype(jnp.bfloat16)


def make_chunk_kernel(back, n_head):
    def kernel(told_ref, told_x_ref, *refs):
        pieces, refs = refs[:n_head], refs[n_head:]
        w_ref, query_hbm, query_x_hbm, own_t_hbm, own_both_hbm, before_hbm, sums_hbm, sums_x_hbm = refs[:8]
        query_ref, query_x_ref, own_t_ref, own_values_ref, sums_ref, sums_x_ref = refs[8:14]
        keys_ref, keys_t_ref, values_ref, live_ref, sems, out_sems = refs[14:]
        blocks = query_ref.shape[0] // BLK
        here = lax.axis_index("seq")
        source = here - 2 * back
        copies = fetch(
            [
                (query_x_hbm, query_x_ref), (own_t_hbm, own_t_ref),
                (own_both_hbm.at[pl.ds(blocks * BLK, blocks * BLK)], own_values_ref),
                (before_hbm, sums_ref), (query_hbm, query_ref),
            ],
            sems,
        )
        sums_x_ref[...] = jnp.zeros_like(sums_x_ref)
        mark(live_ref, told_x_ref, here * blocks, blocks, 0)

        @pl.when(source >= 0)
        def _():
            chunk_keys(pieces, w_ref, keys_ref, keys_t_ref, values_ref)

        wait(copies)
        attend_all(query_x_ref, sums_x_ref, own_t_ref, own_values_ref, live_ref, 0, blocks)

        @pl.when(source >= 0)
        def _():
            mark(live_ref, told_ref, source * blocks, blocks, 0)
            mark(live_ref, told_x_ref, source * blocks, blocks, blocks)
            attend_all(query_ref, sums_ref, keys_t_ref, values_ref, live_ref, 0, blocks)
            attend_all(query_x_ref, sums_x_ref, keys_t_ref, values_ref, live_ref, blocks, blocks)

        wait(fetch([(sums_ref, sums_hbm), (sums_x_ref, sums_x_hbm)], out_sems))

    return kernel


def make_last_kernel(back, n_head):
    def kernel(told_x_ref, *refs):
        pieces, refs = refs[:n_head], refs[n_head:]
        w_ref, query_x_hbm, before_hbm, send_ref, keys_t_ref, values_ref = refs[:6]
        query_x_ref, sums_ref, keys_ref, live_ref, sems = refs[6:]
        blocks = query_x_ref.shape[0] // BLK
        source = lax.axis_index("seq") - 2 * back
        copies = fetch([(query_x_hbm, query_x_ref), (before_hbm, sums_ref)], sems)

        @pl.when(source >= 0)
        def _():
            chunk_keys(pieces, w_ref, keys_ref, keys_t_ref, values_ref)
            mark(live_ref, told_x_ref, source * blocks, blocks, 0)

        wait(copies)

        @pl.when(source >= 0)
        def _():
            attend_all(query_x_ref, sums_ref, keys_t_ref, values_ref, live_ref, 0, blocks)

        send_off(sums_ref, send_ref)

    return kernel


def make_own_last_kernel(back):
    def kernel(
        told_ref, query_hbm, keys_t_ref, values_ref, tail_ref, far_hbm, before_hbm, gate_hbm, gain_ref,
        sums_ref, scale_ref, query_ref, gate_ref, far_ref, far_t_ref, live_ref, sems, far_sems,
    ):
        rows, cols = query_ref.shape
        blocks = rows // BLK
        here = lax.axis_index("seq")
        source = here - 2 * back
        copies = fetch([(query_hbm, query_ref), (before_hbm, sums_ref), (gate_hbm, gate_ref)], sems)
        far_copies = fetch([(far_hbm, far_ref)], far_sems)
        mark(live_ref, told_ref, source * blocks, blocks, 0)
        wait(copies)

        @pl.when(source >= 0)
        def _():
            attend_all(query_ref, sums_ref, keys_t_ref, values_ref, live_ref, 0, blocks)

        wait(far_copies)
        far = here - FAR

        @pl.when((far >= 0) & (here % 2 == 0))
        def _():
            far_t_ref[...] = far_ref[0:rows, :].astype(jnp.float32).T.astype(jnp.bfloat16)
            mark(live_ref, told_ref, far * blocks, blocks, 0)
            attend_all(query_ref, sums_ref, far_t_ref, far_ref.at[pl.ds(rows, rows)], live_ref, 0, blocks)

        farthest = here - FAR - 1

        @pl.when(farthest >= 0)
        def _():
            mark(live_ref, told_ref, farthest * blocks + blocks - 1, 1, 0)
            for h in range(cols // DH):
                at = pl.ds(h * DH, DH)
                scores = lax.dot_general(
                    query_ref[0:BLK, at], tail_ref[0, :, at], NT, preferred_element_type=jnp.float32
                )
                weights = tile(scores, live_ref[0]).astype(jnp.bfloat16)
                sums_ref[0:BLK, at] += jnp.dot(
                    weights, tail_ref[1, :, at], preferred_element_type=jnp.float32
                )

        scale_ref[...] = gain_ref[...].reshape(1, -1).astype(jnp.float32) * gate_ref[...].astype(
            jnp.float32
        )
        for h in range(cols // DH):
            at = pl.ds(h * DH, DH)
            sums_ref[:, at] = centred(sums_ref[:, at])

    return kernel


def finish_kernel(sums_ref, near_ref, scale_ref, out_ref):
    for h in range(sums_ref.shape[1] // DH):
        at = pl.ds(h * DH, DH)
        part = sums_ref[:, at] + near_ref[:, at].astype(jnp.float32)
        off = centred(part)
        spread_sq = jnp.mean(jnp.square(off), axis=-1, keepdims=True)
        out_ref[:, at] = (off * lax.rsqrt(spread_sq + EPS) * scale_ref[:, at]).astype(jnp.bfloat16)


def mix(total, pieces, w_ref):
    cols = pieces[0].shape[1]
    for m, piece in enumerate(pieces):
        w = w_ref[m * cols : (m + 1) * cols, :]
        total = total + jnp.dot(piece[...], w, preferred_element_type=jnp.float32)
    return total


def near_out_kernel(*refs):
    n = (len(refs) - 7) // 3
    pieces, w_hbm, refs = refs[:n], refs[n : 3 * n], refs[3 * n :]
    history_hbm, out_ref, w_far_ref, w_near_ref, history_ref, sems, w_sems = refs
    cols = out_ref.shape[1]
    rows = w_hbm[0].shape[0]
    at = pl.ds(pl.multiple_of(lax.axis_index("head") * cols, cols), cols)
    copies = fetch([(history_hbm.at[:, at], history_ref)], sems)
    w_copies = fetch(
        [
            (w.at[:, at], (w_near_ref if m < n else w_far_ref).at[pl.ds(m % n * rows, rows)])
            for m, w in enumerate(w_hbm)
        ],
        w_sems,
    )
    wait(copies)
    wait(w_copies)
    out_ref[...] = mix(history_ref[...].astype(jnp.float32), pieces, w_near_ref)


def far_out_kernel(*refs):
    *pieces, w_ref, near_ref, out_ref = refs
    out_ref[...] = mix(near_ref[...], pieces, w_ref).astype(jnp.bfloat16)


def crossed(array, axis, bit):
    return lax.ppermute(array, axis, [(i, i ^ bit) for i in range(lax.axis_size(axis))])


def spread(piece, bit):
    pieces = {0: piece}
    while bit:
        pieces.update({m + bit: crossed(p, "head", bit) for m, p in list(pieces.items())})
        bit //= 2
    return [pieces[m] for m in sorted(pieces)]


def body(history, ln_gain, w_in, out_gain, w_out, block_lists, counts):
    tok_rows, width = history.shape
    blocks = counts.shape[0]
    cols = w_in.shape[2]
    n_seq, n_head = lax.axis_size("seq"), lax.axis_size("head")
    assert 2 * (PLANES + 1) * blocks - (WIN - 1) == blocks - 1
    barrier = lax.optimization_barrier

    shape = lambda like, *dims: jax.ShapeDtypeStruct(dims, like)
    bf16, f32 = jnp.bfloat16, jnp.float32
    wide = pl.BlockSpec(memory_space=pltpu.VMEM)
    flat = pl.BlockSpec(memory_space=pltpu.SMEM)
    far_off = pl.BlockSpec(memory_space=pltpu.HBM)
    n_live = 2 * blocks * 8
    upright, lying = (tok_rows, cols), (cols, tok_rows)
    sems = lambda n: pltpu.SemaphoreType.DMA((n,))
    live = pltpu.SMEM((n_live,), f32)

    share_rows = tok_rows // n_head
    steps = share_rows // 48
    share = pl.pallas_call(
        norm_kernel,
        in_specs=[far_off] * 2,
        out_specs=wide,
        out_shape=shape(bf16, share_rows, width),
        scratch_shapes=[
            pltpu.VMEM((share_rows, width), bf16),
            pltpu.VMEM((width,), bf16),
            sems(steps + 1),
        ],
        cost_estimate=cost(2),
        compiler_params=params(60),
    )(history, ln_gain)
    gain, block_lists, counts, w_out, share = barrier((ln_gain, block_lists, counts, w_out, share))
    told = jnp.concatenate([block_lists, counts[:, None]], axis=1)
    upward = [(i, i + 2) for i in range(n_seq - 2)]
    share_1 = lax.ppermute(share, "seq", upward)

    gate, both, query, keys_t, tail = pl.pallas_call(
        own_kernel,
        in_specs=[far_off, far_off, wide],
        out_specs=[far_off] * 5,
        out_shape=[
            shape(bf16, *upright), shape(bf16, 2 * tok_rows, cols), shape(bf16, *upright),
            shape(bf16, *lying), shape(bf16, 2, BLK, cols),
        ],
        scratch_shapes=[
            pltpu.VMEM((tok_rows, width), bf16), pltpu.VMEM((width,), bf16), pltpu.VMEM(upright, bf16),
            pltpu.VMEM((2 * tok_rows, cols), bf16), pltpu.VMEM(upright, bf16), pltpu.VMEM(lying, bf16),
            sems(1 + tok_rows // (2 * BLK)), sems(6),
        ],
        compiler_params=params(60),
        cost_estimate=cost(4),
    )(history, gain, w_in)

    w_cross = crossed(w_out, "head", n_head // 2)
    query_x = crossed(query, "seq", 1)
    share_1, query, w_cross = barrier((share_1, query, w_cross))
    share_2 = lax.ppermute(share_1, "seq", upward[2:])
    cross_1 = crossed(share_1, "head", n_head // 2)
    told_x = crossed(told, "seq", 1)
    told, told_x, tail = barrier((told, told_x, tail))
    tail = lax.ppermute(tail, "seq", [(i, i + FAR + 1) for i in range(n_seq - FAR - 1)])
    own_sums = pl.pallas_call(
        own_attend_kernel,
        in_specs=[flat] + [far_off] * 3,
        out_specs=far_off,
        out_shape=shape(f32, *upright),
        scratch_shapes=[pltpu.VMEM(upright, bf16), pltpu.VMEM(lying, bf16), pltpu.VMEM(upright, bf16)]
        + [pltpu.VMEM(upright, f32), live, sems(3)],
        compiler_params=params(),
        cost_estimate=cost(4),
    )(told, query, keys_t, both)
    share_2, cross_1, own_sums, query_x, tail = barrier((share_2, cross_1, own_sums, query_x, tail))
    chunk_1 = spread(share_1, n_head // 4) + spread(cross_1, n_head // 4)
    cross_2 = crossed(share_2, "head", n_head // 2)
    near_2 = spread(share_2, n_head // 4)

    both, query_x, share_2, tail = barrier((both, query_x, share_2, tail))
    far = lax.ppermute(both, "seq", [(i, i + FAR) for i in range(1, n_seq - FAR, 2)])

    sums, sums_x = pl.pallas_call(
        make_chunk_kernel(1, n_head),
        in_specs=[flat] * 2 + [wide] * (n_head + 1) + [far_off] * 5,
        out_specs=[far_off] * 2,
        out_shape=[shape(f32, *upright)] * 2,
        scratch_shapes=[
            pltpu.VMEM(dims, kind)
            for dims, kind in (
                (upright, bf16), (upright, bf16), (lying, bf16), (upright, bf16), (upright, f32),
                (upright, f32), (upright, f32), (lying, bf16), (upright, bf16),
            )
        ]
        + [live, sems(5), sems(2)],
        compiler_params=params(16),
        cost_estimate=cost(0.05),
    )(told, told_x, *chunk_1, w_in, query, query_x, keys_t, both, own_sums)

    cross_2, sums_x = barrier((cross_2, sums_x))
    send, keys_t, values = pl.pallas_call(
        make_last_kernel(PLANES, n_head),
        in_specs=[flat] + [wide] * (n_head + 1) + [far_off] * 2,
        out_specs=[wide] * 3,
        out_shape=[shape(bf16, *upright), shape(bf16, *lying), shape(bf16, *upright)],
        scratch_shapes=[
            pltpu.VMEM(upright, bf16), pltpu.VMEM(upright, f32), pltpu.VMEM(upright, f32), live, sems(2)
        ],
        compiler_params=params(),
        cost_estimate=cost(0.05),
    )(told_x, *near_2, *spread(cross_2, n_head // 4), w_in, query_x, sums_x)
    near = crossed(send, "seq", 1)
    send, w_out, w_cross = barrier((send, w_out, w_cross))
    w_all = spread(w_out, n_head // 4) + spread(w_cross, n_head // 4)
    mine, scale = pl.pallas_call(
        make_own_last_kernel(PLANES),
        in_specs=[flat, far_off, wide, wide, wide, far_off, far_off, far_off, wide],
        out_specs=[wide] * 2,
        out_shape=[shape(f32, *upright)] * 2,
        scratch_shapes=[pltpu.VMEM(upright, bf16)] * 2
        + [pltpu.VMEM((2 * tok_rows, cols), bf16), pltpu.VMEM(lying, bf16), live, sems(3), sems(1)],
        compiler_params=params(),
        cost_estimate=cost(9),
    )(told, query, keys_t, values, tail, far, sums, gate, out_gain)
    near, mine, w_all = barrier((near, mine, tuple(w_all)))
    gated = pl.pallas_call(
        finish_kernel,
        in_specs=[wide] * 3,
        out_specs=wide,
        out_shape=shape(bf16, *upright),
        compiler_params=params(),
        cost_estimate=cost(1),
    )(mine, near, scale)

    out_cols = width // n_head
    cross_gated = crossed(gated, "head", n_head // 2)
    near_gated = spread(gated, n_head // 4)
    half = n_head // 2
    mixed, w_far = pl.pallas_call(
        near_out_kernel,
        in_specs=[wide] * half + [far_off] * (n_head + 1),
        out_specs=[wide] * 2,
        out_shape=[shape(f32, tok_rows, out_cols), shape(bf16, half * cols, out_cols)],
        scratch_shapes=[
            pltpu.VMEM((half * cols, out_cols), bf16), pltpu.VMEM((tok_rows, out_cols), bf16),
            sems(1), sems(n_head),
        ],
        compiler_params=params(),
        cost_estimate=cost(2),
    )(*near_gated, *w_all, history)
    cross_gated, mixed = barrier((cross_gated, mixed))
    return pl.pallas_call(
        far_out_kernel,
        in_specs=[wide] * (half + 2),
        out_specs=wide,
        out_shape=shape(bf16, tok_rows, out_cols),
        compiler_params=params(),
        cost_estimate=cost(2),
    )(*spread(cross_gated, n_head // 4), w_far, mixed)


def solution(mesh):
    placed = (
        P("seq", None),
        P(),
        P(None, None, "head"),
        P("head"),
        P("head", None),
        P("seq", None),
        P("seq"),
    )
    return jax.shard_map(
        body, mesh=mesh, in_specs=placed, out_specs=P("seq", "head"), check_vma=False
    )
```

```python
import jax
import jax.numpy as jnp
from jax import lax
from jax.experimental import pallas as pl
from jax.experimental.pallas import tpu as pltpu
from jax.sharding import PartitionSpec as P

DH = 128
BLK = 128
WIN = 32
MAXK = 16
EPS = 1e-05
PLANES = 2
FAR = 2 * PLANES + 1
SCALE = 0.5 * DH ** (-0.5)

NT = (((1,), (1,)), ((), ()))


def params(mib=12):
    return pltpu.CompilerParams(vmem_limit_bytes=mib << 20)


def cost(us):
    return pl.CostEstimate(flops=int(us * 1e9 * 0.3), bytes_accessed=int(us * 3e6 * 0.3), transcendentals=0)


def silu(v):
    half = 0.5 * v
    return half * jnp.tanh(half) + half


def project(rows, w):
    return silu(jnp.dot(rows, w, preferred_element_type=jnp.float32))


def normed(rows, gain):
    floats = rows.astype(jnp.float32)
    centre = jnp.mean(floats, axis=-1, keepdims=True)
    off = floats - centre
    spread_sq = jnp.mean(jnp.square(off), axis=-1, keepdims=True)
    return (off * lax.rsqrt(spread_sq + EPS) * gain.astype(jnp.float32)).astype(jnp.bfloat16)


def norm_kernel(history_ref, gain_ref, out_ref, rows_ref, gain_rows_ref, sems):
    share = out_ref.shape[0]
    steps = sems.shape[0] - 1
    step = share // steps
    first = lax.axis_index("head") * share
    gain_copy = pltpu.make_async_copy(gain_ref, gain_rows_ref, sems.at[steps])
    gain_copy.start()
    copies = []
    for i in range(steps):
        at = pl.ds(pl.multiple_of(first + i * step, step), step)
        copies.append(
            pltpu.make_async_copy(history_ref.at[at], rows_ref.at[pl.ds(i * step, step)], sems.at[i])
        )
        copies[i].start()
    gain_copy.wait()
    gain = gain_rows_ref[...].reshape(1, -1)
    for i in range(steps):
        copies[i].wait()
        at = pl.ds(i * step, step)
        out_ref[at, :] = normed(rows_ref[at, :], gain)


def mark(live_ref, told_ref, base, key_blocks, first):
    for b in range(told_ref.shape[0]):
        for g in range(key_blocks):
            live_ref[(first + b) * 8 + g] = 0.0

        def entry(t, unused):
            g = told_ref[b, t] - base
            live_ref[(first + b) * 8 + jnp.where((g >= 0) & (g < key_blocks), g, 7)] = SCALE
            return unused

        lax.fori_loop(0, told_ref[b, MAXK], entry, 0)


def tile(scores, factor):
    half = scores * factor
    return half * jnp.tanh(half) + half


def attend_dense(query_ref, rows, sums_ref, keys_t_ref, values_ref, factors):
    n, blocks = len(factors), len(factors[0])
    for h in range(query_ref.shape[1] // DH):
        cols = pl.ds(h * DH, DH)
        scores = jnp.dot(
            query_ref[rows, cols], keys_t_ref[cols, :], preferred_element_type=jnp.float32
        )
        weights = [
            jnp.concatenate(
                [
                    tile(scores[i * BLK : (i + 1) * BLK, g * BLK : (g + 1) * BLK], factors[i][g])
                    for i in range(n)
                ],
                axis=0,
            ).astype(jnp.bfloat16)
            for g in range(blocks)
        ]
        sums_ref[rows, cols] += jnp.dot(
            jnp.concatenate(weights, axis=1), values_ref[:, cols], preferred_element_type=jnp.float32
        )


def attend_all(query_ref, sums_ref, keys_t_ref, values_ref, live_ref, live_first, key_blocks):
    n = 2

    def some(p, unused):
        factors = [
            [live_ref[(live_first + n * p + i) * 8 + g] for g in range(key_blocks)] for i in range(n)
        ]

        @pl.when(sum(sum(f) for f in factors) > 0.0)
        def _():
            rows = pl.ds(pl.multiple_of(p * n * BLK, n * BLK), n * BLK)
            attend_dense(query_ref, rows, sums_ref, keys_t_ref, values_ref, factors)

        return unused

    lax.fori_loop(0, query_ref.shape[0] // (n * BLK), some, 0)


def fetch(pairs, sems):
    copies = [pltpu.make_async_copy(a, b, sems.at[i]) for i, (a, b) in enumerate(pairs)]
    for copy in copies:
        copy.start()
    return copies


def wait(copies):
    for copy in copies:
        copy.wait()


def own_kernel(
    history_hbm, gain_hbm, w_ref, gate_hbm, both_hbm, query_hbm, keys_t_hbm, tail_hbm,
    history_ref, gain_ref, gate_ref, both_ref, query_ref, keys_t_ref, sems, out_sems,
):
    rows = query_ref.shape[0]
    part = 2 * BLK
    parts = [pl.ds(p * part, part) for p in range(rows // part)]
    gain_copy, *copies = fetch(
        [(gain_hbm, gain_ref)] + [(history_hbm.at[at], history_ref.at[at]) for at in parts], sems
    )
    gain_copy.wait()
    gain = gain_ref[...].reshape(1, -1)
    for p, (at, copy) in enumerate(zip(parts, copies)):
        copy.wait()
        here = normed(history_ref[at, :], gain)
        query_ref[at, :] = project(here, w_ref[2]).astype(jnp.bfloat16)
        keys = project(here, w_ref[3])
        keys_t_ref[:, at] = keys.T.astype(jnp.bfloat16)
        both_ref[at, :] = keys.astype(jnp.bfloat16)
        both_ref[pl.ds(rows + p * part, part), :] = project(here, w_ref[1]).astype(jnp.bfloat16)
        gate_ref[at, :] = project(here, w_ref[0]).astype(jnp.bfloat16)
    wait(
        fetch(
            [
                (query_ref, query_hbm), (both_ref, both_hbm), (keys_t_ref, keys_t_hbm), (gate_ref, gate_hbm),
                (both_ref.at[pl.ds(rows - BLK, BLK)], tail_hbm.at[0]),
                (both_ref.at[pl.ds(2 * rows - BLK, BLK)], tail_hbm.at[1]),
            ],
            out_sems,
        )
    )


def own_attend_kernel(
    told_ref, query_hbm, keys_t_hbm, both_hbm, sums_hbm, query_ref, keys_t_ref, values_ref, sums_ref, live_ref, sems
):
    rows, cols = query_ref.shape
    blocks = rows // BLK
    copies = fetch(
        [
            (query_hbm, query_ref), (keys_t_hbm, keys_t_ref),
            (both_hbm.at[pl.ds(rows, rows)], values_ref),
        ],
        sems,
    )
    mark(live_ref, told_ref, lax.axis_index("seq") * blocks, blocks, 0)
    wait(copies)
    behind = lax.broadcasted_iota(jnp.int32, (BLK, BLK), 1) <= lax.broadcasted_iota(
        jnp.int32, (BLK, BLK), 0
    )
    for p in range(blocks // 2):
        q_rows = pl.ds(p * 2 * BLK, 2 * BLK)
        seen = pl.ds(0, (2 * p + 2) * BLK)
        for h in range(cols // DH):
            at = pl.ds(h * DH, DH)
            scores = jnp.dot(
                query_ref[q_rows, at], keys_t_ref[at, seen], preferred_element_type=jnp.float32
            )
            weights = []
            for g in range(2 * p + 2):
                column = []
                for i in range(2):
                    b = 2 * p + i
                    if g > b:
                        column.append(jnp.zeros((BLK, BLK), jnp.float32))
                        continue
                    some = tile(
                        scores[i * BLK : (i + 1) * BLK, g * BLK : (g + 1) * BLK], live_ref[b * 8 + g]
                    )
                    column.append(jnp.where(behind, some, 0.0) if g == b else some)
                weights.append(jnp.concatenate(column, axis=0).astype(jnp.bfloat16))
            sums_ref[q_rows, at] = jnp.dot(
                jnp.concatenate(weights, axis=1),
                values_ref[seen, at],
                preferred_element_type=jnp.float32,
            )
    wait(fetch([(sums_ref, sums_hbm)], sems))


def centred(part):
    return part - jnp.mean(part, axis=-1, keepdims=True)


def send_off(sums_ref, send_ref):
    for h in range(send_ref.shape[1] // DH):
        at = pl.ds(h * DH, DH)
        send_ref[:, at] = centred(sums_ref[:, at]).astype(jnp.bfloat16)


def chunk_keys(pieces, w_ref, keys_ref, keys_t_ref, values_ref):
    share = pieces[0].shape[0]
    for m, piece in enumerate(pieces):
        at = pl.ds(pl.multiple_of((lax.axis_index("head") ^ m) * share, share), share)
        keys_ref[at, :] = project(piece[...], w_ref[3])
        values_ref[at, :] = project(piece[...], w_ref[1]).astype(jnp.bfloat16)
    keys_t_ref[...] = keys_ref[...].T.astype(jnp.bfloat16)


def make_chunk_kernel(back, n_head):
    def kernel(told_ref, told_x_ref, *refs):
        pieces, refs = refs[:n_head], refs[n_head:]
        w_ref, query_hbm, query_x_hbm, own_t_hbm, own_both_hbm, before_hbm, sums_hbm, sums_x_hbm = refs[:8]
        query_ref, query_x_ref, own_t_ref, own_values_ref, sums_ref, sums_x_ref = refs[8:14]
        keys_ref, keys_t_ref, values_ref, live_ref, sems, out_sems = refs[14:]
        blocks = query_ref.shape[0] // BLK
        here = lax.axis_index("seq")
        source = here - 2 * back
        copies = fetch(
            [
                (query_x_hbm, query_x_ref), (own_t_hbm, own_t_ref),
                (own_both_hbm.at[pl.ds(blocks * BLK, blocks * BLK)], own_values_ref),
                (before_hbm, sums_ref), (query_hbm, query_ref),
            ],
            sems,
        )
        sums_x_ref[...] = jnp.zeros_like(sums_x_ref)
        mark(live_ref, told_x_ref, here * blocks, blocks, 0)

        @pl.when(source >= 0)
        def _():
            chunk_keys(pieces, w_ref, keys_ref, keys_t_ref, values_ref)

        wait(copies)
        attend_all(query_x_ref, sums_x_ref, own_t_ref, own_values_ref, live_ref, 0, blocks)

        @pl.when(source >= 0)
        def _():
            mark(live_ref, told_ref, source * blocks, blocks, 0)
            mark(live_ref, told_x_ref, source * blocks, blocks, blocks)
            attend_all(query_ref, sums_ref, keys_t_ref, values_ref, live_ref, 0, blocks)
            attend_all(query_x_ref, sums_x_ref, keys_t_ref, values_ref, live_ref, blocks, blocks)

        wait(fetch([(sums_ref, sums_hbm), (sums_x_ref, sums_x_hbm)], out_sems))

    return kernel


def make_last_kernel(back, n_head):
    def kernel(told_x_ref, *refs):
        pieces, refs = refs[:n_head], refs[n_head:]
        w_ref, query_x_hbm, before_hbm, send_ref, keys_t_ref, values_ref = refs[:6]
        query_x_ref, sums_ref, keys_ref, live_ref, sems = refs[6:]
        blocks = query_x_ref.shape[0] // BLK
        source = lax.axis_index("seq") - 2 * back
        copies = fetch([(query_x_hbm, query_x_ref), (before_hbm, sums_ref)], sems)

        @pl.when(source >= 0)
        def _():
            chunk_keys(pieces, w_ref, keys_ref, keys_t_ref, values_ref)
            mark(live_ref, told_x_ref, source * blocks, blocks, 0)

        wait(copies)

        @pl.when(source >= 0)
        def _():
            attend_all(query_x_ref, sums_ref, keys_t_ref, values_ref, live_ref, 0, blocks)

        send_off(sums_ref, send_ref)

    return kernel


def make_own_last_kernel(back):
    def kernel(
        told_ref, query_hbm, keys_t_ref, values_ref, tail_ref, far_hbm, before_hbm, gate_hbm, gain_ref,
        sums_ref, scale_ref, query_ref, gate_ref, far_ref, far_t_ref, live_ref, sems, far_sems,
    ):
        rows, cols = query_ref.shape
        blocks = rows // BLK
        here = lax.axis_index("seq")
        source = here - 2 * back
        copies = fetch([(query_hbm, query_ref), (before_hbm, sums_ref), (gate_hbm, gate_ref)], sems)
        far_copies = fetch([(far_hbm, far_ref)], far_sems)
        mark(live_ref, told_ref, source * blocks, blocks, 0)
        wait(copies)

        @pl.when(source >= 0)
        def _():
            attend_all(query_ref, sums_ref, keys_t_ref, values_ref, live_ref, 0, blocks)

        wait(far_copies)
        far = here - FAR

        @pl.when((far >= 0) & (here % 2 == 0))
        def _():
            far_t_ref[...] = far_ref[0:rows, :].astype(jnp.float32).T.astype(jnp.bfloat16)
            mark(live_ref, told_ref, far * blocks, blocks, 0)
            attend_all(query_ref, sums_ref, far_t_ref, far_ref.at[pl.ds(rows, rows)], live_ref, 0, blocks)

        farthest = here - FAR - 1

        @pl.when(farthest >= 0)
        def _():
            mark(live_ref, told_ref, farthest * blocks + blocks - 1, 1, 0)
            for h in range(cols // DH):
                at = pl.ds(h * DH, DH)
                scores = lax.dot_general(
                    query_ref[0:BLK, at], tail_ref[0, :, at], NT, preferred_element_type=jnp.float32
                )
                weights = tile(scores, live_ref[0]).astype(jnp.bfloat16)
                sums_ref[0:BLK, at] += jnp.dot(
                    weights, tail_ref[1, :, at], preferred_element_type=jnp.float32
                )

        scale_ref[...] = gain_ref[...].reshape(1, -1).astype(jnp.float32) * gate_ref[...].astype(
            jnp.float32
        )
        for h in range(cols // DH):
            at = pl.ds(h * DH, DH)
            sums_ref[:, at] = centred(sums_ref[:, at])

    return kernel


def finish_kernel(sums_ref, near_ref, scale_ref, out_ref):
    for h in range(sums_ref.shape[1] // DH):
        at = pl.ds(h * DH, DH)
        part = sums_ref[:, at] + near_ref[:, at].astype(jnp.float32)
        off = centred(part)
        spread_sq = jnp.mean(jnp.square(off), axis=-1, keepdims=True)
        out_ref[:, at] = (off * lax.rsqrt(spread_sq + EPS) * scale_ref[:, at]).astype(jnp.bfloat16)


def mix(total, pieces, w_ref):
    cols = pieces[0].shape[1]
    for m, piece in enumerate(pieces):
        w = w_ref[m * cols : (m + 1) * cols, :]
        total = total + jnp.dot(piece[...], w, preferred_element_type=jnp.float32)
    return total


def near_out_kernel(*refs):
    n = (len(refs) - 7) // 3
    pieces, w_hbm, refs = refs[:n], refs[n : 3 * n], refs[3 * n :]
    history_hbm, out_ref, w_far_ref, w_near_ref, history_ref, sems, w_sems = refs
    cols = out_ref.shape[1]
    rows = w_hbm[0].shape[0]
    at = pl.ds(pl.multiple_of(lax.axis_index("head") * cols, cols), cols)
    copies = fetch([(history_hbm.at[:, at], history_ref)], sems)
    w_copies = fetch(
        [
            (w.at[:, at], (w_near_ref if m < n else w_far_ref).at[pl.ds(m % n * rows, rows)])
            for m, w in enumerate(w_hbm)
        ],
        w_sems,
    )
    wait(copies)
    wait(w_copies)
    out_ref[...] = mix(history_ref[...].astype(jnp.float32), pieces, w_near_ref)


def far_out_kernel(*refs):
    *pieces, w_ref, near_ref, out_ref = refs
    out_ref[...] = mix(near_ref[...], pieces, w_ref).astype(jnp.bfloat16)


def crossed(array, axis, bit):
    return lax.ppermute(array, axis, [(i, i ^ bit) for i in range(lax.axis_size(axis))])


def spread(piece, bit):
    pieces = {0: piece}
    while bit:
        pieces.update({m + bit: crossed(p, "head", bit) for m, p in list(pieces.items())})
        bit //= 2
    return [pieces[m] for m in sorted(pieces)]


def body(history, ln_gain, w_in, out_gain, w_out, block_lists, counts):
    tok_rows, width = history.shape
    blocks = counts.shape[0]
    cols = w_in.shape[2]
    n_seq, n_head = lax.axis_size("seq"), lax.axis_size("head")
    assert 2 * (PLANES + 1) * blocks - (WIN - 1) == blocks - 1
    barrier = lax.optimization_barrier

    shape = lambda like, *dims: jax.ShapeDtypeStruct(dims, like)
    bf16, f32 = jnp.bfloat16, jnp.float32
    wide = pl.BlockSpec(memory_space=pltpu.VMEM)
    flat = pl.BlockSpec(memory_space=pltpu.SMEM)
    far_off = pl.BlockSpec(memory_space=pltpu.HBM)
    n_live = 2 * blocks * 8
    upright, lying = (tok_rows, cols), (cols, tok_rows)
    sems = lambda n: pltpu.SemaphoreType.DMA((n,))
    live = pltpu.SMEM((n_live,), f32)

    share_rows = tok_rows // n_head
    steps = share_rows // 48
    share = pl.pallas_call(
        norm_kernel,
        in_specs=[far_off] * 2,
        out_specs=wide,
        out_shape=shape(bf16, share_rows, width),
        scratch_shapes=[
            pltpu.VMEM((share_rows, width), bf16),
            pltpu.VMEM((width,), bf16),
            sems(steps + 1),
        ],
        cost_estimate=cost(2),
        compiler_params=params(60),
    )(history, ln_gain)
    gain, block_lists, counts, w_out, share = barrier((ln_gain, block_lists, counts, w_out, share))
    told = jnp.concatenate([block_lists, counts[:, None]], axis=1)
    upward = [(i, i + 2) for i in range(n_seq - 2)]
    share_1 = lax.ppermute(share, "seq", upward)

    gate, both, query, keys_t, tail = pl.pallas_call(
        own_kernel,
        in_specs=[far_off, far_off, wide],
        out_specs=[far_off] * 5,
        out_shape=[
            shape(bf16, *upright), shape(bf16, 2 * tok_rows, cols), shape(bf16, *upright),
            shape(bf16, *lying), shape(bf16, 2, BLK, cols),
        ],
        scratch_shapes=[
            pltpu.VMEM((tok_rows, width), bf16), pltpu.VMEM((width,), bf16), pltpu.VMEM(upright, bf16),
            pltpu.VMEM((2 * tok_rows, cols), bf16), pltpu.VMEM(upright, bf16), pltpu.VMEM(lying, bf16),
            sems(1 + tok_rows // (2 * BLK)), sems(6),
        ],
        compiler_params=params(60),
        cost_estimate=cost(4),
    )(history, gain, w_in)

    w_cross = crossed(w_out, "head", n_head // 2)
    query_x = crossed(query, "seq", 1)
    share_1, query, w_cross = barrier((share_1, query, w_cross))
    share_2 = lax.ppermute(share_1, "seq", upward[2:])
    cross_1 = crossed(share_1, "head", n_head // 2)
    told_x = crossed(told, "seq", 1)
    told, told_x, tail = barrier((told, told_x, tail))
    tail = lax.ppermute(tail, "seq", [(i, i + FAR + 1) for i in range(n_seq - FAR - 1)])
    own_sums = pl.pallas_call(
        own_attend_kernel,
        in_specs=[flat] + [far_off] * 3,
        out_specs=far_off,
        out_shape=shape(f32, *upright),
        scratch_shapes=[pltpu.VMEM(upright, bf16), pltpu.VMEM(lying, bf16), pltpu.VMEM(upright, bf16)]
        + [pltpu.VMEM(upright, f32), live, sems(3)],
        compiler_params=params(),
        cost_estimate=cost(4),
    )(told, query, keys_t, both)
    share_2, cross_1, own_sums, query_x = barrier((share_2, cross_1, own_sums, query_x))
    chunk_1 = spread(share_1, n_head // 4) + spread(cross_1, n_head // 4)
    cross_2 = crossed(share_2, "head", n_head // 2)
    near_2 = spread(share_2, n_head // 4)

    both, query_x, share_2 = barrier((both, query_x, share_2))
    far = lax.ppermute(both, "seq", [(i, i + FAR) for i in range(1, n_seq - FAR, 2)])

    sums, sums_x = pl.pallas_call(
        make_chunk_kernel(1, n_head),
        in_specs=[flat] * 2 + [wide] * (n_head + 1) + [far_off] * 5,
        out_specs=[far_off] * 2,
        out_shape=[shape(f32, *upright)] * 2,
        scratch_shapes=[
            pltpu.VMEM(dims, kind)
            for dims, kind in (
                (upright, bf16), (upright, bf16), (lying, bf16), (upright, bf16), (upright, f32),
                (upright, f32), (upright, f32), (lying, bf16), (upright, bf16),
            )
        ]
        + [live, sems(5), sems(2)],
        compiler_params=params(16),
        cost_estimate=cost(0.05),
    )(told, told_x, *chunk_1, w_in, query, query_x, keys_t, both, own_sums)

    cross_2, sums_x = barrier((cross_2, sums_x))
    send, keys_t, values = pl.pallas_call(
        make_last_kernel(PLANES, n_head),
        in_specs=[flat] + [wide] * (n_head + 1) + [far_off] * 2,
        out_specs=[wide] * 3,
        out_shape=[shape(bf16, *upright), shape(bf16, *lying), shape(bf16, *upright)],
        scratch_shapes=[
            pltpu.VMEM(upright, bf16), pltpu.VMEM(upright, f32), pltpu.VMEM(upright, f32), live, sems(2)
        ],
        compiler_params=params(),
        cost_estimate=cost(0.05),
    )(told_x, *near_2, *spread(cross_2, n_head // 4), w_in, query_x, sums_x)
    near = crossed(send, "seq", 1)
    send, w_out, w_cross = barrier((send, w_out, w_cross))
    w_all = spread(w_out, n_head // 4) + spread(w_cross, n_head // 4)
    mine, scale = pl.pallas_call(
        make_own_last_kernel(PLANES),
        in_specs=[flat, far_off, wide, wide, wide, far_off, far_off, far_off, wide],
        out_specs=[wide] * 2,
        out_shape=[shape(f32, *upright)] * 2,
        scratch_shapes=[pltpu.VMEM(upright, bf16)] * 2
        + [pltpu.VMEM((2 * tok_rows, cols), bf16), pltpu.VMEM(lying, bf16), live, sems(3), sems(1)],
        compiler_params=params(),
        cost_estimate=cost(9),
    )(told, query, keys_t, values, tail, far, sums, gate, out_gain)
    near, mine, w_all = barrier((near, mine, tuple(w_all)))
    gated = pl.pallas_call(
        finish_kernel,
        in_specs=[wide] * 3,
        out_specs=wide,
        out_shape=shape(bf16, *upright),
        compiler_params=params(),
        cost_estimate=cost(1),
    )(mine, near, scale)

    out_cols = width // n_head
    cross_gated = crossed(gated, "head", n_head // 2)
    near_gated = spread(gated, n_head // 4)
    half = n_head // 2
    mixed, w_far = pl.pallas_call(
        near_out_kernel,
        in_specs=[wide] * half + [far_off] * (n_head + 1),
        out_specs=[wide] * 2,
        out_shape=[shape(f32, tok_rows, out_cols), shape(bf16, half * cols, out_cols)],
        scratch_shapes=[
            pltpu.VMEM((half * cols, out_cols), bf16), pltpu.VMEM((tok_rows, out_cols), bf16),
            sems(1), sems(n_head),
        ],
        compiler_params=params(),
        cost_estimate=cost(2),
    )(*near_gated, *w_all, history)
    cross_gated, mixed = barrier((cross_gated, mixed))
    return pl.pallas_call(
        far_out_kernel,
        in_specs=[wide] * (half + 2),
        out_specs=wide,
        out_shape=shape(bf16, tok_rows, out_cols),
        compiler_params=params(),
        cost_estimate=cost(2),
    )(*spread(cross_gated, n_head // 4), w_far, mixed)


def solution(mesh):
    placed = (
        P("seq", None),
        P(),
        P(None, None, "head"),
        P("head"),
        P("head", None),
        P("seq", None),
        P("seq"),
    )
    return jax.shard_map(
        body, mesh=mesh, in_specs=placed, out_specs=P("seq", "head"), check_vma=False
    )
```

```python
import jax
import jax.numpy as jnp
from jax import lax
from jax.experimental import pallas as pl
from jax.experimental.pallas import tpu as pltpu
from jax.sharding import PartitionSpec as P

DH = 128
BLK = 128
WIN = 32
MAXK = 16
EPS = 1e-05
PLANES = 2
FAR = 2 * PLANES + 1
SCALE = 0.5 * DH ** (-0.5)

NT = (((1,), (1,)), ((), ()))


def params(mib=12):
    return pltpu.CompilerParams(vmem_limit_bytes=mib << 20)


def cost(us):
    return pl.CostEstimate(flops=int(us * 1e9 * 0.3), bytes_accessed=int(us * 3e6 * 0.3), transcendentals=0)


def silu(v):
    half = 0.5 * v
    return half * jnp.tanh(half) + half


def project(rows, w):
    return silu(jnp.dot(rows, w, preferred_element_type=jnp.float32))


def normed(rows, gain):
    floats = rows.astype(jnp.float32)
    centre = jnp.mean(floats, axis=-1, keepdims=True)
    off = floats - centre
    spread_sq = jnp.mean(jnp.square(off), axis=-1, keepdims=True)
    return (off * lax.rsqrt(spread_sq + EPS) * gain.astype(jnp.float32)).astype(jnp.bfloat16)


def norm_kernel(history_ref, gain_ref, out_ref, rows_ref, gain_rows_ref, sems):
    share = out_ref.shape[0]
    steps = sems.shape[0] - 1
    step = share // steps
    first = lax.axis_index("head") * share
    gain_copy = pltpu.make_async_copy(gain_ref, gain_rows_ref, sems.at[steps])
    gain_copy.start()
    copies = []
    for i in range(steps):
        at = pl.ds(pl.multiple_of(first + i * step, step), step)
        copies.append(
            pltpu.make_async_copy(history_ref.at[at], rows_ref.at[pl.ds(i * step, step)], sems.at[i])
        )
        copies[i].start()
    gain_copy.wait()
    gain = gain_rows_ref[...].reshape(1, -1)
    for i in range(steps):
        copies[i].wait()
        at = pl.ds(i * step, step)
        out_ref[at, :] = normed(rows_ref[at, :], gain)


def mark(live_ref, told_ref, base, key_blocks, first):
    for b in range(told_ref.shape[0]):
        for g in range(key_blocks):
            live_ref[(first + b) * 8 + g] = 0.0

        def entry(t, unused):
            g = told_ref[b, t] - base
            live_ref[(first + b) * 8 + jnp.where((g >= 0) & (g < key_blocks), g, 7)] = SCALE
            return unused

        lax.fori_loop(0, told_ref[b, MAXK], entry, 0)


def tile(scores, factor):
    half = scores * factor
    return half * jnp.tanh(half) + half


def attend_dense(query_ref, rows, sums_ref, keys_t_ref, values_ref, factors):
    n, blocks = len(factors), len(factors[0])
    for h in range(query_ref.shape[1] // DH):
        cols = pl.ds(h * DH, DH)
        scores = jnp.dot(
            query_ref[rows, cols], keys_t_ref[cols, :], preferred_element_type=jnp.float32
        )
        weights = [
            jnp.concatenate(
                [
                    tile(scores[i * BLK : (i + 1) * BLK, g * BLK : (g + 1) * BLK], factors[i][g])
                    for i in range(n)
                ],
                axis=0,
            ).astype(jnp.bfloat16)
            for g in range(blocks)
        ]
        sums_ref[rows, cols] += jnp.dot(
            jnp.concatenate(weights, axis=1), values_ref[:, cols], preferred_element_type=jnp.float32
        )


def attend_all(query_ref, sums_ref, keys_t_ref, values_ref, live_ref, live_first, key_blocks):
    n = 2

    def some(p, unused):
        factors = [
            [live_ref[(live_first + n * p + i) * 8 + g] for g in range(key_blocks)] for i in range(n)
        ]

        @pl.when(sum(sum(f) for f in factors) > 0.0)
        def _():
            rows = pl.ds(pl.multiple_of(p * n * BLK, n * BLK), n * BLK)
            attend_dense(query_ref, rows, sums_ref, keys_t_ref, values_ref, factors)

        return unused

    lax.fori_loop(0, query_ref.shape[0] // (n * BLK), some, 0)


def fetch(pairs, sems):
    copies = [pltpu.make_async_copy(a, b, sems.at[i]) for i, (a, b) in enumerate(pairs)]
    for copy in copies:
        copy.start()
    return copies


def wait(copies):
    for copy in copies:
        copy.wait()


def own_kernel(
    history_hbm, gain_hbm, w_ref, gate_hbm, both_hbm, query_hbm, keys_t_hbm, tail_hbm,
    history_ref, gain_ref, gate_ref, both_ref, query_ref, keys_t_ref, sems, out_sems,
):
    rows = query_ref.shape[0]
    part = 2 * BLK
    parts = [pl.ds(p * part, part) for p in range(rows // part)]
    gain_copy, *copies = fetch(
        [(gain_hbm, gain_ref)] + [(history_hbm.at[at], history_ref.at[at]) for at in parts], sems
    )
    gain_copy.wait()
    gain = gain_ref[...].reshape(1, -1)
    for p, (at, copy) in enumerate(zip(parts, copies)):
        copy.wait()
        here = normed(history_ref[at, :], gain)
        query_ref[at, :] = project(here, w_ref[2]).astype(jnp.bfloat16)
        keys = project(here, w_ref[3])
        keys_t_ref[:, at] = keys.T.astype(jnp.bfloat16)
        both_ref[at, :] = keys.astype(jnp.bfloat16)
        both_ref[pl.ds(rows + p * part, part), :] = project(here, w_ref[1]).astype(jnp.bfloat16)
        gate_ref[at, :] = project(here, w_ref[0]).astype(jnp.bfloat16)
    wait(
        fetch(
            [
                (query_ref, query_hbm), (both_ref, both_hbm), (keys_t_ref, keys_t_hbm), (gate_ref, gate_hbm),
                (both_ref.at[pl.ds(rows - BLK, BLK)], tail_hbm.at[0]),
                (both_ref.at[pl.ds(2 * rows - BLK, BLK)], tail_hbm.at[1]),
            ],
            out_sems,
        )
    )


def own_attend_kernel(
    told_ref, query_hbm, keys_t_hbm, both_hbm, sums_hbm, query_ref, keys_t_ref, values_ref, sums_ref, live_ref, sems
):
    rows, cols = query_ref.shape
    blocks = rows // BLK
    copies = fetch(
        [
            (query_hbm, query_ref), (keys_t_hbm, keys_t_ref),
            (both_hbm.at[pl.ds(rows, rows)], values_ref),
        ],
        sems,
    )
    mark(live_ref, told_ref, lax.axis_index("seq") * blocks, blocks, 0)
    wait(copies)
    behind = lax.broadcasted_iota(jnp.int32, (BLK, BLK), 1) <= lax.broadcasted_iota(
        jnp.int32, (BLK, BLK), 0
    )
    for p in range(blocks // 2):
        q_rows = pl.ds(p * 2 * BLK, 2 * BLK)
        seen = pl.ds(0, (2 * p + 2) * BLK)
        for h in range(cols // DH):
            at = pl.ds(h * DH, DH)
            scores = jnp.dot(
                query_ref[q_rows, at], keys_t_ref[at, seen], preferred_element_type=jnp.float32
            )
            weights = []
            for g in range(2 * p + 2):
                column = []
                for i in range(2):
                    b = 2 * p + i
                    if g > b:
                        column.append(jnp.zeros((BLK, BLK), jnp.float32))
                        continue
                    some = tile(
                        scores[i * BLK : (i + 1) * BLK, g * BLK : (g + 1) * BLK], live_ref[b * 8 + g]
                    )
                    column.append(jnp.where(behind, some, 0.0) if g == b else some)
                weights.append(jnp.concatenate(column, axis=0).astype(jnp.bfloat16))
            sums_ref[q_rows, at] = jnp.dot(
                jnp.concatenate(weights, axis=1),
                values_ref[seen, at],
                preferred_element_type=jnp.float32,
            )
    wait(fetch([(sums_ref, sums_hbm)], sems))


def centred(part):
    return part - jnp.mean(part, axis=-1, keepdims=True)


def send_off(sums_ref, send_ref):
    for h in range(send_ref.shape[1] // DH):
        at = pl.ds(h * DH, DH)
        send_ref[:, at] = centred(sums_ref[:, at]).astype(jnp.bfloat16)


def chunk_keys(pieces, w_ref, keys_ref, keys_t_ref, values_ref):
    share = pieces[0].shape[0]
    for m, piece in enumerate(pieces):
        at = pl.ds(pl.multiple_of((lax.axis_index("head") ^ m) * share, share), share)
        keys_ref[at, :] = project(piece[...], w_ref[3])
        values_ref[at, :] = project(piece[...], w_ref[1]).astype(jnp.bfloat16)
    keys_t_ref[...] = keys_ref[...].T.astype(jnp.bfloat16)


def make_chunk_kernel(back, n_head):
    def kernel(told_ref, told_x_ref, *refs):
        pieces, refs = refs[:n_head], refs[n_head:]
        w_ref, query_hbm, query_x_hbm, own_t_hbm, own_both_hbm, before_hbm, sums_hbm, sums_x_hbm = refs[:8]
        query_ref, query_x_ref, own_t_ref, own_values_ref, sums_ref, sums_x_ref = refs[8:14]
        keys_ref, keys_t_ref, values_ref, live_ref, sems, out_sems = refs[14:]
        blocks = query_ref.shape[0] // BLK
        here = lax.axis_index("seq")
        source = here - 2 * back
        copies = fetch(
            [
                (query_x_hbm, query_x_ref), (own_t_hbm, own_t_ref),
                (own_both_hbm.at[pl.ds(blocks * BLK, blocks * BLK)], own_values_ref),
                (before_hbm, sums_ref), (query_hbm, query_ref),
            ],
            sems,
        )
        sums_x_ref[...] = jnp.zeros_like(sums_x_ref)
        mark(live_ref, told_x_ref, here * blocks, blocks, 0)

        @pl.when(source >= 0)
        def _():
            chunk_keys(pieces, w_ref, keys_ref, keys_t_ref, values_ref)

        wait(copies)
        attend_all(query_x_ref, sums_x_ref, own_t_ref, own_values_ref, live_ref, 0, blocks)

        @pl.when(source >= 0)
        def _():
            mark(live_ref, told_ref, source * blocks, blocks, 0)
            mark(live_ref, told_x_ref, source * blocks, blocks, blocks)
            attend_all(query_ref, sums_ref, keys_t_ref, values_ref, live_ref, 0, blocks)
            attend_all(query_x_ref, sums_x_ref, keys_t_ref, values_ref, live_ref, blocks, blocks)

        wait(fetch([(sums_ref, sums_hbm), (sums_x_ref, sums_x_hbm)], out_sems))

    return kernel


def make_last_kernel(back, n_head):
    def kernel(told_x_ref, *refs):
        pieces, refs = refs[:n_head], refs[n_head:]
        w_ref, query_x_hbm, before_hbm, send_ref, keys_t_ref, values_ref = refs[:6]
        query_x_ref, sums_ref, keys_ref, live_ref, sems = refs[6:]
        blocks = query_x_ref.shape[0] // BLK
        source = lax.axis_index("seq") - 2 * back
        copies = fetch([(query_x_hbm, query_x_ref), (before_hbm, sums_ref)], sems)

        @pl.when(source >= 0)
        def _():
            chunk_keys(pieces, w_ref, keys_ref, keys_t_ref, values_ref)
            mark(live_ref, told_x_ref, source * blocks, blocks, 0)

        wait(copies)

        @pl.when(source >= 0)
        def _():
            attend_all(query_x_ref, sums_ref, keys_t_ref, values_ref, live_ref, 0, blocks)

        send_off(sums_ref, send_ref)

    return kernel


def make_own_last_kernel(back):
    def kernel(
        told_ref, query_hbm, keys_t_ref, values_ref, before_hbm, gate_hbm, gain_ref,
        sums_ref, scale_ref, query_ref, gate_ref, live_ref, sems,
    ):
        blocks = query_ref.shape[0] // BLK
        source = lax.axis_index("seq") - 2 * back
        copies = fetch([(query_hbm, query_ref), (before_hbm, sums_ref), (gate_hbm, gate_ref)], sems)
        mark(live_ref, told_ref, source * blocks, blocks, 0)
        wait(copies)

        @pl.when(source >= 0)
        def _():
            attend_all(query_ref, sums_ref, keys_t_ref, values_ref, live_ref, 0, blocks)

        scale_ref[...] = gain_ref[...].reshape(1, -1).astype(jnp.float32) * gate_ref[...].astype(
            jnp.float32
        )

    return kernel


def far_kernel(
    told_ref, query_hbm, tail_ref, far_hbm, unused, sums_ref, query_ref, far_ref, far_t_ref, live_ref, sems, far_sems
):
    rows, cols = query_ref.shape
    blocks = rows // BLK
    here = lax.axis_index("seq")
    far = here - FAR
    farthest = here - FAR - 1

    @pl.when(far >= 0)
    def _():
        copies = fetch([(query_hbm, query_ref)], sems)
        far_copies = fetch([(far_hbm, far_ref)], far_sems)
        mark(live_ref, told_ref, far * blocks, blocks, 0)
        wait(copies)
        wait(far_copies)

        @pl.when(here % 2 == 0)
        def _():
            far_t_ref[...] = far_ref[0:rows, :].astype(jnp.float32).T.astype(jnp.bfloat16)
            attend_all(query_ref, sums_ref, far_t_ref, far_ref.at[pl.ds(rows, rows)], live_ref, 0, blocks)

    @pl.when(farthest >= 0)
    def _():
        mark(live_ref, told_ref, farthest * blocks + blocks - 1, 1, 0)
        for h in range(cols // DH):
            at = pl.ds(h * DH, DH)
            scores = lax.dot_general(
                query_ref[0:BLK, at], tail_ref[0, :, at], NT, preferred_element_type=jnp.float32
            )
            weights = tile(scores, live_ref[0]).astype(jnp.bfloat16)
            sums_ref[0:BLK, at] += jnp.dot(
                weights, tail_ref[1, :, at], preferred_element_type=jnp.float32
            )

    for h in range(cols // DH):
        at = pl.ds(h * DH, DH)
        sums_ref[:, at] = centred(sums_ref[:, at])


def finish_kernel(sums_ref, near_ref, scale_ref, out_ref):
    for h in range(sums_ref.shape[1] // DH):
        at = pl.ds(h * DH, DH)
        part = sums_ref[:, at] + near_ref[:, at].astype(jnp.float32)
        off = centred(part)
        spread_sq = jnp.mean(jnp.square(off), axis=-1, keepdims=True)
        out_ref[:, at] = (off * lax.rsqrt(spread_sq + EPS) * scale_ref[:, at]).astype(jnp.bfloat16)


def mix(total, pieces, w_ref):
    cols = pieces[0].shape[1]
    for m, piece in enumerate(pieces):
        w = w_ref[m * cols : (m + 1) * cols, :]
        total = total + jnp.dot(piece[...], w, preferred_element_type=jnp.float32)
    return total


def near_out_kernel(*refs):
    n = (len(refs) - 7) // 3
    pieces, w_hbm, refs = refs[:n], refs[n : 3 * n], refs[3 * n :]
    history_hbm, out_ref, w_far_ref, w_near_ref, history_ref, sems, w_sems = refs
    cols = out_ref.shape[1]
    rows = w_hbm[0].shape[0]
    at = pl.ds(pl.multiple_of(lax.axis_index("head") * cols, cols), cols)
    copies = fetch([(history_hbm.at[:, at], history_ref)], sems)
    w_copies = fetch(
        [
            (w.at[:, at], (w_near_ref if m < n else w_far_ref).at[pl.ds(m % n * rows, rows)])
            for m, w in enumerate(w_hbm)
        ],
        w_sems,
    )
    wait(copies)
    wait(w_copies)
    out_ref[...] = mix(history_ref[...].astype(jnp.float32), pieces, w_near_ref)


def far_out_kernel(*refs):
    *pieces, w_ref, near_ref, out_ref = refs
    out_ref[...] = mix(near_ref[...], pieces, w_ref).astype(jnp.bfloat16)


def crossed(array, axis, bit):
    return lax.ppermute(array, axis, [(i, i ^ bit) for i in range(lax.axis_size(axis))])


def spread(piece, bit):
    pieces = {0: piece}
    while bit:
        pieces.update({m + bit: crossed(p, "head", bit) for m, p in list(pieces.items())})
        bit //= 2
    return [pieces[m] for m in sorted(pieces)]


def body(history, ln_gain, w_in, out_gain, w_out, block_lists, counts):
    tok_rows, width = history.shape
    blocks = counts.shape[0]
    cols = w_in.shape[2]
    n_seq, n_head = lax.axis_size("seq"), lax.axis_size("head")
    assert 2 * (PLANES + 1) * blocks - (WIN - 1) == blocks - 1
    barrier = lax.optimization_barrier

    shape = lambda like, *dims: jax.ShapeDtypeStruct(dims, like)
    bf16, f32 = jnp.bfloat16, jnp.float32
    wide = pl.BlockSpec(memory_space=pltpu.VMEM)
    flat = pl.BlockSpec(memory_space=pltpu.SMEM)
    far_off = pl.BlockSpec(memory_space=pltpu.HBM)
    n_live = 2 * blocks * 8
    upright, lying = (tok_rows, cols), (cols, tok_rows)
    sems = lambda n: pltpu.SemaphoreType.DMA((n,))
    live = pltpu.SMEM((n_live,), f32)

    share_rows = tok_rows // n_head
    steps = share_rows // 48
    share = pl.pallas_call(
        norm_kernel,
        in_specs=[far_off] * 2,
        out_specs=wide,
        out_shape=shape(bf16, share_rows, width),
        scratch_shapes=[
            pltpu.VMEM((share_rows, width), bf16),
            pltpu.VMEM((width,), bf16),
            sems(steps + 1),
        ],
        cost_estimate=cost(2),
        compiler_params=params(60),
    )(history, ln_gain)
    gain, block_lists, counts, w_out, share = barrier((ln_gain, block_lists, counts, w_out, share))
    told = jnp.concatenate([block_lists, counts[:, None]], axis=1)
    upward = [(i, i + 2) for i in range(n_seq - 2)]
    share_1 = lax.ppermute(share, "seq", upward)

    gate, both, query, keys_t, tail = pl.pallas_call(
        own_kernel,
        in_specs=[far_off, far_off, wide],
        out_specs=[far_off] * 5,
        out_shape=[
            shape(bf16, *upright), shape(bf16, 2 * tok_rows, cols), shape(bf16, *upright),
            shape(bf16, *lying), shape(bf16, 2, BLK, cols),
        ],
        scratch_shapes=[
            pltpu.VMEM((tok_rows, width), bf16), pltpu.VMEM((width,), bf16), pltpu.VMEM(upright, bf16),
            pltpu.VMEM((2 * tok_rows, cols), bf16), pltpu.VMEM(upright, bf16), pltpu.VMEM(lying, bf16),
            sems(1 + tok_rows // (2 * BLK)), sems(6),
        ],
        compiler_params=params(60),
        cost_estimate=cost(4),
    )(history, gain, w_in)

    w_cross = crossed(w_out, "head", n_head // 2)
    query_x = crossed(query, "seq", 1)
    share_1, query, w_cross = barrier((share_1, query, w_cross))
    share_2 = lax.ppermute(share_1, "seq", upward[2:])
    cross_1 = crossed(share_1, "head", n_head // 2)
    told_x = crossed(told, "seq", 1)
    told, told_x, tail = barrier((told, told_x, tail))
    tail = lax.ppermute(tail, "seq", [(i, i + FAR + 1) for i in range(n_seq - FAR - 1)])
    own_sums = pl.pallas_call(
        own_attend_kernel,
        in_specs=[flat] + [far_off] * 3,
        out_specs=far_off,
        out_shape=shape(f32, *upright),
        scratch_shapes=[pltpu.VMEM(upright, bf16), pltpu.VMEM(lying, bf16), pltpu.VMEM(upright, bf16)]
        + [pltpu.VMEM(upright, f32), live, sems(3)],
        compiler_params=params(),
        cost_estimate=cost(4),
    )(told, query, keys_t, both)
    share_2, cross_1, own_sums, query_x = barrier((share_2, cross_1, own_sums, query_x))
    chunk_1 = spread(share_1, n_head // 4) + spread(cross_1, n_head // 4)
    cross_2 = crossed(share_2, "head", n_head // 2)
    near_2 = spread(share_2, n_head // 4)

    both, query_x, share_2 = barrier((both, query_x, share_2))
    far = lax.ppermute(both, "seq", [(i, i + FAR) for i in range(1, n_seq - FAR, 2)])

    sums, sums_x = pl.pallas_call(
        make_chunk_kernel(1, n_head),
        in_specs=[flat] * 2 + [wide] * (n_head + 1) + [far_off] * 5,
        out_specs=[far_off] * 2,
        out_shape=[shape(f32, *upright)] * 2,
        scratch_shapes=[
            pltpu.VMEM(dims, kind)
            for dims, kind in (
                (upright, bf16), (upright, bf16), (lying, bf16), (upright, bf16), (upright, f32),
                (upright, f32), (upright, f32), (lying, bf16), (upright, bf16),
            )
        ]
        + [live, sems(5), sems(2)],
        compiler_params=params(16),
        cost_estimate=cost(0.05),
    )(told, told_x, *chunk_1, w_in, query, query_x, keys_t, both, own_sums)

    cross_2, sums_x = barrier((cross_2, sums_x))
    send, keys_t, values = pl.pallas_call(
        make_last_kernel(PLANES, n_head),
        in_specs=[flat] + [wide] * (n_head + 1) + [far_off] * 2,
        out_specs=[wide] * 3,
        out_shape=[shape(bf16, *upright), shape(bf16, *lying), shape(bf16, *upright)],
        scratch_shapes=[
            pltpu.VMEM(upright, bf16), pltpu.VMEM(upright, f32), pltpu.VMEM(upright, f32), live, sems(2)
        ],
        compiler_params=params(),
        cost_estimate=cost(0.05),
    )(told_x, *near_2, *spread(cross_2, n_head // 4), w_in, query_x, sums_x)
    near = crossed(send, "seq", 1)
    send, w_out, w_cross = barrier((send, w_out, w_cross))
    w_all = spread(w_out, n_head // 4) + spread(w_cross, n_head // 4)
    mine, scale = pl.pallas_call(
        make_own_last_kernel(PLANES),
        in_specs=[flat, far_off, wide, wide, far_off, far_off, wide],
        out_specs=[wide] * 2,
        out_shape=[shape(f32, *upright)] * 2,
        scratch_shapes=[pltpu.VMEM(upright, bf16)] * 2 + [live, sems(3)],
        compiler_params=params(),
        cost_estimate=cost(0.05),
    )(told, query, keys_t, values, sums, gate, out_gain)
    far, tail, mine = barrier((far, tail, mine))
    mine = pl.pallas_call(
        far_kernel,
        in_specs=[flat, far_off, wide, far_off, wide],
        out_specs=wide,
        out_shape=shape(f32, *upright),
        input_output_aliases={4: 0},
        scratch_shapes=[
            pltpu.VMEM(upright, bf16), pltpu.VMEM((2 * tok_rows, cols), bf16), pltpu.VMEM(lying, bf16), live,
            sems(1), sems(1),
        ],
        compiler_params=params(),
        cost_estimate=cost(9),
    )(told, query, tail, far, mine)
    near, mine, w_all = barrier((near, mine, tuple(w_all)))
    gated = pl.pallas_call(
        finish_kernel,
        in_specs=[wide] * 3,
        out_specs=wide,
        out_shape=shape(bf16, *upright),
        compiler_params=params(),
        cost_estimate=cost(1),
    )(mine, near, scale)

    out_cols = width // n_head
    cross_gated = crossed(gated, "head", n_head // 2)
    near_gated = spread(gated, n_head // 4)
    half = n_head // 2
    mixed, w_far = pl.pallas_call(
        near_out_kernel,
        in_specs=[wide] * half + [far_off] * (n_head + 1),
        out_specs=[wide] * 2,
        out_shape=[shape(f32, tok_rows, out_cols), shape(bf16, half * cols, out_cols)],
        scratch_shapes=[
            pltpu.VMEM((half * cols, out_cols), bf16), pltpu.VMEM((tok_rows, out_cols), bf16),
            sems(1), sems(n_head),
        ],
        compiler_params=params(),
        cost_estimate=cost(2),
    )(*near_gated, *w_all, history)
    cross_gated, mixed = barrier((cross_gated, mixed))
    return pl.pallas_call(
        far_out_kernel,
        in_specs=[wide] * (half + 2),
        out_specs=wide,
        out_shape=shape(bf16, tok_rows, out_cols),
        compiler_params=params(),
        cost_estimate=cost(2),
    )(*spread(cross_gated, n_head // 4), w_far, mixed)


def solution(mesh):
    placed = (
        P("seq", None),
        P(),
        P(None, None, "head"),
        P("head"),
        P("head", None),
        P("seq", None),
        P("seq"),
    )
    return jax.shard_map(
        body, mesh=mesh, in_specs=placed, out_specs=P("seq", "head"), check_vma=False
    )
```

```python
import jax
import jax.numpy as jnp
from jax import lax
from jax.experimental import pallas as pl
from jax.experimental.pallas import tpu as pltpu
from jax.sharding import PartitionSpec as P

DH = 128
BLK = 128
WIN = 32
MAXK = 16
EPS = 1e-05
PLANES = 2
FAR = 2 * PLANES + 1
SCALE = 0.5 * DH ** (-0.5)

NT = (((1,), (1,)), ((), ()))


def params(mib=12):
    return pltpu.CompilerParams(vmem_limit_bytes=mib << 20)


def cost(us):
    return pl.CostEstimate(flops=int(us * 1e9 * 0.3), bytes_accessed=int(us * 3e6 * 0.3), transcendentals=0)


def silu(v):
    half = 0.5 * v
    return half * jnp.tanh(half) + half


def project(rows, w):
    return silu(jnp.dot(rows, w, preferred_element_type=jnp.float32))


def normed(rows, gain):
    floats = rows.astype(jnp.float32)
    centre = jnp.mean(floats, axis=-1, keepdims=True)
    off = floats - centre
    spread_sq = jnp.mean(jnp.square(off), axis=-1, keepdims=True)
    return (off * lax.rsqrt(spread_sq + EPS) * gain.astype(jnp.float32)).astype(jnp.bfloat16)


def norm_kernel(history_ref, gain_ref, out_ref, rows_ref, gain_rows_ref, sems):
    share = out_ref.shape[0]
    steps = sems.shape[0] - 1
    step = share // steps
    first = lax.axis_index("head") * share
    gain_copy = pltpu.make_async_copy(gain_ref, gain_rows_ref, sems.at[steps])
    gain_copy.start()
    copies = []
    for i in range(steps):
        at = pl.ds(pl.multiple_of(first + i * step, step), step)
        copies.append(
            pltpu.make_async_copy(history_ref.at[at], rows_ref.at[pl.ds(i * step, step)], sems.at[i])
        )
        copies[i].start()
    gain_copy.wait()
    gain = gain_rows_ref[...].reshape(1, -1)
    for i in range(steps):
        copies[i].wait()
        at = pl.ds(i * step, step)
        out_ref[at, :] = normed(rows_ref[at, :], gain)


def mark(live_ref, told_ref, base, key_blocks, first):
    for b in range(told_ref.shape[0]):
        for g in range(key_blocks):
            live_ref[(first + b) * 8 + g] = 0.0

        def entry(t, unused):
            g = told_ref[b, t] - base
            live_ref[(first + b) * 8 + jnp.where((g >= 0) & (g < key_blocks), g, 7)] = SCALE
            return unused

        lax.fori_loop(0, told_ref[b, MAXK], entry, 0)


def tile(scores, factor):
    half = scores * factor
    return half * jnp.tanh(half) + half


def attend_dense(query_ref, rows, sums_ref, keys_t_ref, values_ref, factors):
    n, blocks = len(factors), len(factors[0])
    for h in range(query_ref.shape[1] // DH):
        cols = pl.ds(h * DH, DH)
        scores = jnp.dot(
            query_ref[rows, cols], keys_t_ref[cols, :], preferred_element_type=jnp.float32
        )
        weights = [
            jnp.concatenate(
                [
                    tile(scores[i * BLK : (i + 1) * BLK, g * BLK : (g + 1) * BLK], factors[i][g])
                    for i in range(n)
                ],
                axis=0,
            ).astype(jnp.bfloat16)
            for g in range(blocks)
        ]
        sums_ref[rows, cols] += jnp.dot(
            jnp.concatenate(weights, axis=1), values_ref[:, cols], preferred_element_type=jnp.float32
        )


def attend_all(query_ref, sums_ref, keys_t_ref, values_ref, live_ref, live_first, key_blocks):
    n = 2

    def some(p, unused):
        factors = [
            [live_ref[(live_first + n * p + i) * 8 + g] for g in range(key_blocks)] for i in range(n)
        ]

        @pl.when(sum(sum(f) for f in factors) > 0.0)
        def _():
            rows = pl.ds(pl.multiple_of(p * n * BLK, n * BLK), n * BLK)
            attend_dense(query_ref, rows, sums_ref, keys_t_ref, values_ref, factors)

        return unused

    lax.fori_loop(0, query_ref.shape[0] // (n * BLK), some, 0)


def fetch(pairs, sems):
    copies = [pltpu.make_async_copy(a, b, sems.at[i]) for i, (a, b) in enumerate(pairs)]
    for copy in copies:
        copy.start()
    return copies


def wait(copies):
    for copy in copies:
        copy.wait()


def own_kernel(
    history_hbm, gain_hbm, w_ref, gate_hbm, both_hbm, query_hbm, keys_t_hbm, tail_hbm,
    history_ref, gain_ref, gate_ref, both_ref, query_ref, keys_t_ref, sems, out_sems,
):
    rows = query_ref.shape[0]
    part = 2 * BLK
    parts = [pl.ds(p * part, part) for p in range(rows // part)]
    gain_copy, *copies = fetch(
        [(gain_hbm, gain_ref)] + [(history_hbm.at[at], history_ref.at[at]) for at in parts], sems
    )
    gain_copy.wait()
    gain = gain_ref[...].reshape(1, -1)
    for p, (at, copy) in enumerate(zip(parts, copies)):
        copy.wait()
        here = normed(history_ref[at, :], gain)
        query_ref[at, :] = project(here, w_ref[2]).astype(jnp.bfloat16)
        keys = project(here, w_ref[3])
        keys_t_ref[:, at] = keys.T.astype(jnp.bfloat16)
        both_ref[at, :] = keys.astype(jnp.bfloat16)
        both_ref[pl.ds(rows + p * part, part), :] = project(here, w_ref[1]).astype(jnp.bfloat16)
        gate_ref[at, :] = project(here, w_ref[0]).astype(jnp.bfloat16)
    wait(
        fetch(
            [
                (query_ref, query_hbm), (both_ref, both_hbm), (keys_t_ref, keys_t_hbm), (gate_ref, gate_hbm),
                (both_ref.at[pl.ds(rows - BLK, BLK)], tail_hbm.at[0]),
                (both_ref.at[pl.ds(2 * rows - BLK, BLK)], tail_hbm.at[1]),
            ],
            out_sems,
        )
    )


def own_attend_kernel(
    told_ref, query_hbm, keys_t_hbm, both_hbm, sums_hbm, query_ref, keys_t_ref, values_ref, sums_ref, live_ref, sems
):
    rows, cols = query_ref.shape
    blocks = rows // BLK
    copies = fetch(
        [
            (query_hbm, query_ref), (keys_t_hbm, keys_t_ref),
            (both_hbm.at[pl.ds(rows, rows)], values_ref),
        ],
        sems,
    )
    mark(live_ref, told_ref, lax.axis_index("seq") * blocks, blocks, 0)
    wait(copies)
    behind = lax.broadcasted_iota(jnp.int32, (BLK, BLK), 1) <= lax.broadcasted_iota(
        jnp.int32, (BLK, BLK), 0
    )
    for p in range(blocks // 2):
        q_rows = pl.ds(p * 2 * BLK, 2 * BLK)
        seen = pl.ds(0, (2 * p + 2) * BLK)
        for h in range(cols // DH):
            at = pl.ds(h * DH, DH)
            scores = jnp.dot(
                query_ref[q_rows, at], keys_t_ref[at, seen], preferred_element_type=jnp.float32
            )
            weights = []
            for g in range(2 * p + 2):
                column = []
                for i in range(2):
                    b = 2 * p + i
                    if g > b:
                        column.append(jnp.zeros((BLK, BLK), jnp.float32))
                        continue
                    some = tile(
                        scores[i * BLK : (i + 1) * BLK, g * BLK : (g + 1) * BLK], live_ref[b * 8 + g]
                    )
                    column.append(jnp.where(behind, some, 0.0) if g == b else some)
                weights.append(jnp.concatenate(column, axis=0).astype(jnp.bfloat16))
            sums_ref[q_rows, at] = jnp.dot(
                jnp.concatenate(weights, axis=1),
                values_ref[seen, at],
                preferred_element_type=jnp.float32,
            )
    wait(fetch([(sums_ref, sums_hbm)], sems))


def centred(part):
    return part - jnp.mean(part, axis=-1, keepdims=True)


def send_off(sums_ref, send_ref):
    for h in range(send_ref.shape[1] // DH):
        at = pl.ds(h * DH, DH)
        send_ref[:, at] = centred(sums_ref[:, at]).astype(jnp.bfloat16)


def chunk_keys(pieces, w_ref, keys_ref, keys_t_ref, values_ref):
    share = pieces[0].shape[0]
    for m, piece in enumerate(pieces):
        at = pl.ds(pl.multiple_of((lax.axis_index("head") ^ m) * share, share), share)
        keys_ref[at, :] = project(piece[...], w_ref[3])
        values_ref[at, :] = project(piece[...], w_ref[1]).astype(jnp.bfloat16)
    keys_t_ref[...] = keys_ref[...].T.astype(jnp.bfloat16)


def make_chunk_kernel(back, n_head):
    def kernel(told_ref, told_x_ref, *refs):
        pieces, refs = refs[:n_head], refs[n_head:]
        w_ref, query_hbm, query_x_hbm, own_t_hbm, own_both_hbm, before_hbm, sums_hbm, sums_x_hbm = refs[:8]
        query_ref, query_x_ref, own_t_ref, own_values_ref, sums_ref, sums_x_ref = refs[8:14]
        keys_ref, keys_t_ref, values_ref, live_ref, sems, out_sems = refs[14:]
        blocks = query_ref.shape[0] // BLK
        here = lax.axis_index("seq")
        source = here - 2 * back
        copies = fetch(
            [
                (query_x_hbm, query_x_ref), (own_t_hbm, own_t_ref),
                (own_both_hbm.at[pl.ds(blocks * BLK, blocks * BLK)], own_values_ref),
                (before_hbm, sums_ref), (query_hbm, query_ref),
            ],
            sems,
        )
        sums_x_ref[...] = jnp.zeros_like(sums_x_ref)
        mark(live_ref, told_x_ref, here * blocks, blocks, 0)

        @pl.when(source >= 0)
        def _():
            chunk_keys(pieces, w_ref, keys_ref, keys_t_ref, values_ref)

        wait(copies)
        attend_all(query_x_ref, sums_x_ref, own_t_ref, own_values_ref, live_ref, 0, blocks)

        @pl.when(source >= 0)
        def _():
            mark(live_ref, told_ref, source * blocks, blocks, 0)
            mark(live_ref, told_x_ref, source * blocks, blocks, blocks)
            attend_all(query_ref, sums_ref, keys_t_ref, values_ref, live_ref, 0, blocks)
            attend_all(query_x_ref, sums_x_ref, keys_t_ref, values_ref, live_ref, blocks, blocks)

        wait(fetch([(sums_ref, sums_hbm), (sums_x_ref, sums_x_hbm)], out_sems))

    return kernel


def make_last_kernel(back, n_head):
    def kernel(told_x_ref, *refs):
        pieces, refs = refs[:n_head], refs[n_head:]
        w_ref, query_x_hbm, before_hbm, send_ref, keys_t_ref, values_ref = refs[:6]
        query_x_ref, sums_ref, keys_ref, live_ref, sems = refs[6:]
        blocks = query_x_ref.shape[0] // BLK
        source = lax.axis_index("seq") - 2 * back
        copies = fetch([(query_x_hbm, query_x_ref), (before_hbm, sums_ref)], sems)

        @pl.when(source >= 0)
        def _():
            chunk_keys(pieces, w_ref, keys_ref, keys_t_ref, values_ref)
            mark(live_ref, told_x_ref, source * blocks, blocks, 0)

        wait(copies)

        @pl.when(source >= 0)
        def _():
            attend_all(query_x_ref, sums_ref, keys_t_ref, values_ref, live_ref, 0, blocks)

        send_off(sums_ref, send_ref)

    return kernel


def make_own_last_kernel(back):
    def kernel(
        told_ref, query_hbm, keys_t_ref, values_ref, before_hbm, gate_hbm, gain_ref,
        sums_ref, scale_ref, query_ref, gate_ref, live_ref, sems,
    ):
        blocks = query_ref.shape[0] // BLK
        source = lax.axis_index("seq") - 2 * back
        copies = fetch([(query_hbm, query_ref), (before_hbm, sums_ref), (gate_hbm, gate_ref)], sems)
        mark(live_ref, told_ref, source * blocks, blocks, 0)
        wait(copies)

        @pl.when(source >= 0)
        def _():
            attend_all(query_ref, sums_ref, keys_t_ref, values_ref, live_ref, 0, blocks)

        scale_ref[...] = gain_ref[...].reshape(1, -1).astype(jnp.float32) * gate_ref[...].astype(
            jnp.float32
        )

    return kernel


def far_kernel(
    told_ref, query_hbm, tail_ref, far_ref, unused, sums_ref, query_ref, far_t_ref, live_ref, sems
):
    rows, cols = query_ref.shape
    blocks = rows // BLK
    here = lax.axis_index("seq")
    far = here - FAR
    farthest = here - FAR - 1

    @pl.when(far >= 0)
    def _():
        copies = fetch([(query_hbm, query_ref)], sems)
        mark(live_ref, told_ref, far * blocks, blocks, 0)

        @pl.when(here % 2 == 0)
        def _():
            far_t_ref[...] = far_ref[0:rows, :].astype(jnp.float32).T.astype(jnp.bfloat16)

        wait(copies)

        @pl.when(here % 2 == 0)
        def _():
            attend_all(query_ref, sums_ref, far_t_ref, far_ref.at[pl.ds(rows, rows)], live_ref, 0, blocks)

    @pl.when(farthest >= 0)
    def _():
        mark(live_ref, told_ref, farthest * blocks + blocks - 1, 1, 0)
        for h in range(cols // DH):
            at = pl.ds(h * DH, DH)
            scores = lax.dot_general(
                query_ref[0:BLK, at], tail_ref[0, :, at], NT, preferred_element_type=jnp.float32
            )
            weights = tile(scores, live_ref[0]).astype(jnp.bfloat16)
            sums_ref[0:BLK, at] += jnp.dot(
                weights, tail_ref[1, :, at], preferred_element_type=jnp.float32
            )

    for h in range(cols // DH):
        at = pl.ds(h * DH, DH)
        sums_ref[:, at] = centred(sums_ref[:, at])


def finish_kernel(sums_ref, near_ref, scale_ref, out_ref):
    for h in range(sums_ref.shape[1] // DH):
        at = pl.ds(h * DH, DH)
        part = sums_ref[:, at] + near_ref[:, at].astype(jnp.float32)
        off = centred(part)
        spread_sq = jnp.mean(jnp.square(off), axis=-1, keepdims=True)
        out_ref[:, at] = (off * lax.rsqrt(spread_sq + EPS) * scale_ref[:, at]).astype(jnp.bfloat16)


def mix(total, pieces, w_ref):
    cols = pieces[0].shape[1]
    for m, piece in enumerate(pieces):
        w = w_ref[m * cols : (m + 1) * cols, :]
        total = total + jnp.dot(piece[...], w, preferred_element_type=jnp.float32)
    return total


def near_out_kernel(*refs):
    n = (len(refs) - 7) // 3
    pieces, w_hbm, refs = refs[:n], refs[n : 3 * n], refs[3 * n :]
    history_hbm, out_ref, w_far_ref, w_near_ref, history_ref, sems, w_sems = refs
    cols = out_ref.shape[1]
    rows = w_hbm[0].shape[0]
    at = pl.ds(pl.multiple_of(lax.axis_index("head") * cols, cols), cols)
    copies = fetch([(history_hbm.at[:, at], history_ref)], sems)
    w_copies = fetch(
        [
            (w.at[:, at], (w_near_ref if m < n else w_far_ref).at[pl.ds(m % n * rows, rows)])
            for m, w in enumerate(w_hbm)
        ],
        w_sems,
    )
    wait(copies)
    wait(w_copies)
    out_ref[...] = mix(history_ref[...].astype(jnp.float32), pieces, w_near_ref)


def far_out_kernel(*refs):
    *pieces, w_ref, near_ref, out_ref = refs
    out_ref[...] = mix(near_ref[...], pieces, w_ref).astype(jnp.bfloat16)


def crossed(array, axis, bit):
    return lax.ppermute(array, axis, [(i, i ^ bit) for i in range(lax.axis_size(axis))])


def spread(piece, bit):
    pieces = {0: piece}
    while bit:
        pieces.update({m + bit: crossed(p, "head", bit) for m, p in list(pieces.items())})
        bit //= 2
    return [pieces[m] for m in sorted(pieces)]


def body(history, ln_gain, w_in, out_gain, w_out, block_lists, counts):
    tok_rows, width = history.shape
    blocks = counts.shape[0]
    cols = w_in.shape[2]
    n_seq, n_head = lax.axis_size("seq"), lax.axis_size("head")
    assert 2 * (PLANES + 1) * blocks - (WIN - 1) == blocks - 1
    barrier = lax.optimization_barrier

    shape = lambda like, *dims: jax.ShapeDtypeStruct(dims, like)
    bf16, f32 = jnp.bfloat16, jnp.float32
    wide = pl.BlockSpec(memory_space=pltpu.VMEM)
    flat = pl.BlockSpec(memory_space=pltpu.SMEM)
    far_off = pl.BlockSpec(memory_space=pltpu.HBM)
    n_live = 2 * blocks * 8
    upright, lying = (tok_rows, cols), (cols, tok_rows)
    sems = lambda n: pltpu.SemaphoreType.DMA((n,))
    live = pltpu.SMEM((n_live,), f32)

    share_rows = tok_rows // n_head
    steps = share_rows // 48
    share = pl.pallas_call(
        norm_kernel,
        in_specs=[far_off] * 2,
        out_specs=wide,
        out_shape=shape(bf16, share_rows, width),
        scratch_shapes=[
            pltpu.VMEM((share_rows, width), bf16),
            pltpu.VMEM((width,), bf16),
            sems(steps + 1),
        ],
        cost_estimate=cost(2),
        compiler_params=params(60),
    )(history, ln_gain)
    gain, block_lists, counts, w_out, share = barrier((ln_gain, block_lists, counts, w_out, share))
    told = jnp.concatenate([block_lists, counts[:, None]], axis=1)
    upward = [(i, i + 2) for i in range(n_seq - 2)]
    share_1 = lax.ppermute(share, "seq", upward)

    gate, both, query, keys_t, tail = pl.pallas_call(
        own_kernel,
        in_specs=[far_off, far_off, wide],
        out_specs=[far_off] * 5,
        out_shape=[
            shape(bf16, *upright), shape(bf16, 2 * tok_rows, cols), shape(bf16, *upright),
            shape(bf16, *lying), shape(bf16, 2, BLK, cols),
        ],
        scratch_shapes=[
            pltpu.VMEM((tok_rows, width), bf16), pltpu.VMEM((width,), bf16), pltpu.VMEM(upright, bf16),
            pltpu.VMEM((2 * tok_rows, cols), bf16), pltpu.VMEM(upright, bf16), pltpu.VMEM(lying, bf16),
            sems(1 + tok_rows // (2 * BLK)), sems(6),
        ],
        compiler_params=params(60),
        cost_estimate=cost(4),
    )(history, gain, w_in)

    w_cross = crossed(w_out, "head", n_head // 2)
    query_x = crossed(query, "seq", 1)
    share_1, query, w_cross = barrier((share_1, query, w_cross))
    share_2 = lax.ppermute(share_1, "seq", upward[2:])
    cross_1 = crossed(share_1, "head", n_head // 2)
    told_x = crossed(told, "seq", 1)
    told, told_x, tail = barrier((told, told_x, tail))
    tail = lax.ppermute(tail, "seq", [(i, i + FAR + 1) for i in range(n_seq - FAR - 1)])
    own_sums = pl.pallas_call(
        own_attend_kernel,
        in_specs=[flat] + [far_off] * 3,
        out_specs=far_off,
        out_shape=shape(f32, *upright),
        scratch_shapes=[pltpu.VMEM(upright, bf16), pltpu.VMEM(lying, bf16), pltpu.VMEM(upright, bf16)]
        + [pltpu.VMEM(upright, f32), live, sems(3)],
        compiler_params=params(),
        cost_estimate=cost(4),
    )(told, query, keys_t, both)
    share_2, cross_1, own_sums, query_x = barrier((share_2, cross_1, own_sums, query_x))
    chunk_1 = spread(share_1, n_head // 4) + spread(cross_1, n_head // 4)
    cross_2 = crossed(share_2, "head", n_head // 2)
    near_2 = spread(share_2, n_head // 4)

    both, query_x, share_2 = barrier((both, query_x, share_2))
    far = lax.ppermute(both, "seq", [(i, i + FAR) for i in range(1, n_seq - FAR, 2)])

    sums, sums_x = pl.pallas_call(
        make_chunk_kernel(1, n_head),
        in_specs=[flat] * 2 + [wide] * (n_head + 1) + [far_off] * 5,
        out_specs=[far_off] * 2,
        out_shape=[shape(f32, *upright)] * 2,
        scratch_shapes=[
            pltpu.VMEM(dims, kind)
            for dims, kind in (
                (upright, bf16), (upright, bf16), (lying, bf16), (upright, bf16), (upright, f32),
                (upright, f32), (upright, f32), (lying, bf16), (upright, bf16),
            )
        ]
        + [live, sems(5), sems(2)],
        compiler_params=params(16),
        cost_estimate=cost(0.05),
    )(told, told_x, *chunk_1, w_in, query, query_x, keys_t, both, own_sums)

    cross_2, sums_x = barrier((cross_2, sums_x))
    send, keys_t, values = pl.pallas_call(
        make_last_kernel(PLANES, n_head),
        in_specs=[flat] + [wide] * (n_head + 1) + [far_off] * 2,
        out_specs=[wide] * 3,
        out_shape=[shape(bf16, *upright), shape(bf16, *lying), shape(bf16, *upright)],
        scratch_shapes=[
            pltpu.VMEM(upright, bf16), pltpu.VMEM(upright, f32), pltpu.VMEM(upright, f32), live, sems(2)
        ],
        compiler_params=params(),
        cost_estimate=cost(0.05),
    )(told_x, *near_2, *spread(cross_2, n_head // 4), w_in, query_x, sums_x)
    near = crossed(send, "seq", 1)
    send, w_out, w_cross = barrier((send, w_out, w_cross))
    w_all = spread(w_out, n_head // 4) + spread(w_cross, n_head // 4)
    mine, scale = pl.pallas_call(
        make_own_last_kernel(PLANES),
        in_specs=[flat, far_off, wide, wide, far_off, far_off, wide],
        out_specs=[wide] * 2,
        out_shape=[shape(f32, *upright)] * 2,
        scratch_shapes=[pltpu.VMEM(upright, bf16)] * 2 + [live, sems(3)],
        compiler_params=params(),
        cost_estimate=cost(0.05),
    )(told, query, keys_t, values, sums, gate, out_gain)
    far, tail, mine = barrier((far, tail, mine))
    mine = pl.pallas_call(
        far_kernel,
        in_specs=[flat, far_off, wide, wide, wide],
        out_specs=wide,
        out_shape=shape(f32, *upright),
        input_output_aliases={4: 0},
        scratch_shapes=[
            pltpu.VMEM(upright, bf16), pltpu.VMEM(lying, bf16), live, sems(1),
        ],
        compiler_params=params(),
        cost_estimate=cost(9),
    )(told, query, tail, far, mine)
    near, mine, w_all = barrier((near, mine, tuple(w_all)))
    gated = pl.pallas_call(
        finish_kernel,
        in_specs=[wide] * 3,
        out_specs=wide,
        out_shape=shape(bf16, *upright),
        compiler_params=params(),
        cost_estimate=cost(1),
    )(mine, near, scale)

    out_cols = width // n_head
    cross_gated = crossed(gated, "head", n_head // 2)
    near_gated = spread(gated, n_head // 4)
    half = n_head // 2
    mixed, w_far = pl.pallas_call(
        near_out_kernel,
        in_specs=[wide] * half + [far_off] * (n_head + 1),
        out_specs=[wide] * 2,
        out_shape=[shape(f32, tok_rows, out_cols), shape(bf16, half * cols, out_cols)],
        scratch_shapes=[
            pltpu.VMEM((half * cols, out_cols), bf16), pltpu.VMEM((tok_rows, out_cols), bf16),
            sems(1), sems(n_head),
        ],
        compiler_params=params(),
        cost_estimate=cost(2),
    )(*near_gated, *w_all, history)
    cross_gated, mixed = barrier((cross_gated, mixed))
    return pl.pallas_call(
        far_out_kernel,
        in_specs=[wide] * (half + 2),
        out_specs=wide,
        out_shape=shape(bf16, tok_rows, out_cols),
        compiler_params=params(),
        cost_estimate=cost(2),
    )(*spread(cross_gated, n_head // 4), w_far, mixed)


def solution(mesh):
    placed = (
        P("seq", None),
        P(),
        P(None, None, "head"),
        P("head"),
        P("head", None),
        P("seq", None),
        P("seq"),
    )
    return jax.shard_map(
        body, mesh=mesh, in_specs=placed, out_specs=P("seq", "head"), check_vma=False
    )
```

```python
import jax
import jax.numpy as jnp
from jax import lax
from jax.experimental import pallas as pl
from jax.experimental.pallas import tpu as pltpu
from jax.sharding import PartitionSpec as P

DH = 128
BLK = 128
WIN = 32
MAXK = 16
EPS = 1e-05
PLANES = 2
FAR = 2 * PLANES + 1
SCALE = 0.5 * DH ** (-0.5)

NT = (((1,), (1,)), ((), ()))


def params(mib=12):
    return pltpu.CompilerParams(vmem_limit_bytes=mib << 20)


def cost(us):
    return pl.CostEstimate(flops=int(us * 1e9 * 0.3), bytes_accessed=int(us * 3e6 * 0.3), transcendentals=0)


def silu(v):
    half = 0.5 * v
    return half * jnp.tanh(half) + half


def project(rows, w):
    return silu(jnp.dot(rows, w, preferred_element_type=jnp.float32))


def normed(rows, gain):
    floats = rows.astype(jnp.float32)
    centre = jnp.mean(floats, axis=-1, keepdims=True)
    off = floats - centre
    spread_sq = jnp.mean(jnp.square(off), axis=-1, keepdims=True)
    return (off * lax.rsqrt(spread_sq + EPS) * gain.astype(jnp.float32)).astype(jnp.bfloat16)


def norm_kernel(history_ref, gain_ref, out_ref, rows_ref, gain_rows_ref, sems):
    share = out_ref.shape[0]
    steps = sems.shape[0] - 1
    step = share // steps
    first = lax.axis_index("head") * share
    gain_copy = pltpu.make_async_copy(gain_ref, gain_rows_ref, sems.at[steps])
    gain_copy.start()
    copies = []
    for i in range(steps):
        at = pl.ds(pl.multiple_of(first + i * step, step), step)
        copies.append(
            pltpu.make_async_copy(history_ref.at[at], rows_ref.at[pl.ds(i * step, step)], sems.at[i])
        )
        copies[i].start()
    gain_copy.wait()
    gain = gain_rows_ref[...].reshape(1, -1)
    for i in range(steps):
        copies[i].wait()
        at = pl.ds(i * step, step)
        out_ref[at, :] = normed(rows_ref[at, :], gain)


def mark(live_ref, told_ref, base, key_blocks, first):
    for b in range(told_ref.shape[0]):
        for g in range(key_blocks):
            live_ref[(first + b) * 8 + g] = 0.0

        def entry(t, unused):
            g = told_ref[b, t] - base
            live_ref[(first + b) * 8 + jnp.where((g >= 0) & (g < key_blocks), g, 7)] = SCALE
            return unused

        lax.fori_loop(0, told_ref[b, MAXK], entry, 0)


def tile(scores, factor):
    half = scores * factor
    return half * jnp.tanh(half) + half


def attend_dense(query_ref, rows, sums_ref, keys_t_ref, values_ref, factors):
    n, blocks = len(factors), len(factors[0])
    for h in range(query_ref.shape[1] // DH):
        cols = pl.ds(h * DH, DH)
        scores = jnp.dot(
            query_ref[rows, cols], keys_t_ref[cols, :], preferred_element_type=jnp.float32
        )
        weights = [
            jnp.concatenate(
                [
                    tile(scores[i * BLK : (i + 1) * BLK, g * BLK : (g + 1) * BLK], factors[i][g])
                    for i in range(n)
                ],
                axis=0,
            ).astype(jnp.bfloat16)
            for g in range(blocks)
        ]
        sums_ref[rows, cols] += jnp.dot(
            jnp.concatenate(weights, axis=1), values_ref[:, cols], preferred_element_type=jnp.float32
        )


def attend_all(query_ref, sums_ref, keys_t_ref, values_ref, live_ref, live_first, key_blocks):
    n = 2

    def some(p, unused):
        factors = [
            [live_ref[(live_first + n * p + i) * 8 + g] for g in range(key_blocks)] for i in range(n)
        ]

        @pl.when(sum(sum(f) for f in factors) > 0.0)
        def _():
            rows = pl.ds(pl.multiple_of(p * n * BLK, n * BLK), n * BLK)
            attend_dense(query_ref, rows, sums_ref, keys_t_ref, values_ref, factors)

        return unused

    lax.fori_loop(0, query_ref.shape[0] // (n * BLK), some, 0)


def fetch(pairs, sems):
    copies = [pltpu.make_async_copy(a, b, sems.at[i]) for i, (a, b) in enumerate(pairs)]
    for copy in copies:
        copy.start()
    return copies


def wait(copies):
    for copy in copies:
        copy.wait()


def own_kernel(
    history_hbm, gain_hbm, w_ref, gate_hbm, both_hbm, query_hbm, keys_t_hbm, tail_hbm,
    history_ref, gain_ref, gate_ref, both_ref, query_ref, keys_t_ref, sems, out_sems,
):
    rows = query_ref.shape[0]
    part = 2 * BLK
    parts = [pl.ds(p * part, part) for p in range(rows // part)]
    gain_copy, *copies = fetch(
        [(gain_hbm, gain_ref)] + [(history_hbm.at[at], history_ref.at[at]) for at in parts], sems
    )
    gain_copy.wait()
    gain = gain_ref[...].reshape(1, -1)
    for p, (at, copy) in enumerate(zip(parts, copies)):
        copy.wait()
        here = normed(history_ref[at, :], gain)
        query_ref[at, :] = project(here, w_ref[2]).astype(jnp.bfloat16)
        keys = project(here, w_ref[3])
        keys_t_ref[:, at] = keys.T.astype(jnp.bfloat16)
        both_ref[at, :] = keys.astype(jnp.bfloat16)
        both_ref[pl.ds(rows + p * part, part), :] = project(here, w_ref[1]).astype(jnp.bfloat16)
        gate_ref[at, :] = project(here, w_ref[0]).astype(jnp.bfloat16)
    wait(
        fetch(
            [
                (query_ref, query_hbm), (both_ref, both_hbm), (keys_t_ref, keys_t_hbm), (gate_ref, gate_hbm),
                (both_ref.at[pl.ds(rows - BLK, BLK)], tail_hbm.at[0]),
                (both_ref.at[pl.ds(2 * rows - BLK, BLK)], tail_hbm.at[1]),
            ],
            out_sems,
        )
    )


def own_attend_kernel(
    told_ref, query_hbm, keys_t_hbm, both_hbm, sums_hbm, query_ref, keys_t_ref, values_ref, sums_ref, live_ref, sems
):
    rows, cols = query_ref.shape
    blocks = rows // BLK
    copies = fetch(
        [
            (query_hbm, query_ref), (keys_t_hbm, keys_t_ref),
            (both_hbm.at[pl.ds(rows, rows)], values_ref),
        ],
        sems,
    )
    mark(live_ref, told_ref, lax.axis_index("seq") * blocks, blocks, 0)
    wait(copies)
    behind = lax.broadcasted_iota(jnp.int32, (BLK, BLK), 1) <= lax.broadcasted_iota(
        jnp.int32, (BLK, BLK), 0
    )
    for p in range(blocks // 2):
        q_rows = pl.ds(p * 2 * BLK, 2 * BLK)
        seen = pl.ds(0, (2 * p + 2) * BLK)
        for h in range(cols // DH):
            at = pl.ds(h * DH, DH)
            scores = jnp.dot(
                query_ref[q_rows, at], keys_t_ref[at, seen], preferred_element_type=jnp.float32
            )
            weights = []
            for g in range(2 * p + 2):
                column = []
                for i in range(2):
                    b = 2 * p + i
                    if g > b:
                        column.append(jnp.zeros((BLK, BLK), jnp.float32))
                        continue
                    some = tile(
                        scores[i * BLK : (i + 1) * BLK, g * BLK : (g + 1) * BLK], live_ref[b * 8 + g]
                    )
                    column.append(jnp.where(behind, some, 0.0) if g == b else some)
                weights.append(jnp.concatenate(column, axis=0).astype(jnp.bfloat16))
            sums_ref[q_rows, at] = jnp.dot(
                jnp.concatenate(weights, axis=1),
                values_ref[seen, at],
                preferred_element_type=jnp.float32,
            )
    wait(fetch([(sums_ref, sums_hbm)], sems))


def centred(part):
    return part - jnp.mean(part, axis=-1, keepdims=True)


def send_off(sums_ref, send_ref):
    for h in range(send_ref.shape[1] // DH):
        at = pl.ds(h * DH, DH)
        send_ref[:, at] = centred(sums_ref[:, at]).astype(jnp.bfloat16)


def chunk_keys(pieces, w_ref, keys_ref, keys_t_ref, values_ref):
    share = pieces[0].shape[0]
    for m, piece in enumerate(pieces):
        at = pl.ds(pl.multiple_of((lax.axis_index("head") ^ m) * share, share), share)
        keys_ref[at, :] = project(piece[...], w_ref[3])
        values_ref[at, :] = project(piece[...], w_ref[1]).astype(jnp.bfloat16)
    keys_t_ref[...] = keys_ref[...].T.astype(jnp.bfloat16)


def make_chunk_kernel(back, n_head):
    def kernel(told_ref, told_x_ref, *refs):
        pieces, refs = refs[:n_head], refs[n_head:]
        w_ref, query_hbm, query_x_hbm, own_t_hbm, own_both_hbm, before_hbm, sums_hbm, sums_x_hbm = refs[:8]
        query_ref, query_x_ref, own_t_ref, own_values_ref, sums_ref, sums_x_ref = refs[8:14]
        keys_ref, keys_t_ref, values_ref, live_ref, sems, out_sems = refs[14:]
        blocks = query_ref.shape[0] // BLK
        here = lax.axis_index("seq")
        source = here - 2 * back
        copies = fetch(
            [
                (query_x_hbm, query_x_ref), (own_t_hbm, own_t_ref),
                (own_both_hbm.at[pl.ds(blocks * BLK, blocks * BLK)], own_values_ref),
                (before_hbm, sums_ref), (query_hbm, query_ref),
            ],
            sems,
        )
        sums_x_ref[...] = jnp.zeros_like(sums_x_ref)
        mark(live_ref, told_x_ref, here * blocks, blocks, 0)

        @pl.when(source >= 0)
        def _():
            chunk_keys(pieces, w_ref, keys_ref, keys_t_ref, values_ref)

        wait(copies)
        attend_all(query_x_ref, sums_x_ref, own_t_ref, own_values_ref, live_ref, 0, blocks)

        @pl.when(source >= 0)
        def _():
            mark(live_ref, told_ref, source * blocks, blocks, 0)
            mark(live_ref, told_x_ref, source * blocks, blocks, blocks)
            attend_all(query_ref, sums_ref, keys_t_ref, values_ref, live_ref, 0, blocks)
            attend_all(query_x_ref, sums_x_ref, keys_t_ref, values_ref, live_ref, blocks, blocks)

        wait(fetch([(sums_ref, sums_hbm), (sums_x_ref, sums_x_hbm)], out_sems))

    return kernel


def make_last_kernel(back, n_head):
    def kernel(told_x_ref, *refs):
        pieces, refs = refs[:n_head], refs[n_head:]
        w_ref, query_x_hbm, before_hbm, send_ref, keys_t_ref, values_ref = refs[:6]
        query_x_ref, sums_ref, keys_ref, live_ref, sems = refs[6:]
        blocks = query_x_ref.shape[0] // BLK
        source = lax.axis_index("seq") - 2 * back
        copies = fetch([(query_x_hbm, query_x_ref), (before_hbm, sums_ref)], sems)

        @pl.when(source >= 0)
        def _():
            chunk_keys(pieces, w_ref, keys_ref, keys_t_ref, values_ref)
            mark(live_ref, told_x_ref, source * blocks, blocks, 0)

        wait(copies)

        @pl.when(source >= 0)
        def _():
            attend_all(query_x_ref, sums_ref, keys_t_ref, values_ref, live_ref, 0, blocks)

        send_off(sums_ref, send_ref)

    return kernel


def make_own_last_kernel(back):
    def kernel(
        told_ref, query_hbm, keys_t_ref, values_ref, before_hbm, gate_hbm, gain_ref,
        sums_ref, scale_ref, query_ref, gate_ref, live_ref, sems,
    ):
        blocks = query_ref.shape[0] // BLK
        source = lax.axis_index("seq") - 2 * back
        copies = fetch([(query_hbm, query_ref), (before_hbm, sums_ref), (gate_hbm, gate_ref)], sems)
        mark(live_ref, told_ref, source * blocks, blocks, 0)
        wait(copies)

        @pl.when(source >= 0)
        def _():
            attend_all(query_ref, sums_ref, keys_t_ref, values_ref, live_ref, 0, blocks)

        scale_ref[...] = gain_ref[...].reshape(1, -1).astype(jnp.float32) * gate_ref[...].astype(
            jnp.float32
        )

    return kernel


def far_kernel(
    told_ref, query_hbm, tail_ref, far_hbm, unused, sums_ref, query_ref, far_ref, far_t_ref, live_ref, sems, far_sems
):
    rows, cols = query_ref.shape
    blocks = rows // BLK
    here = lax.axis_index("seq")
    far = here - FAR
    farthest = here - FAR - 1

    @pl.when(far >= 0)
    def _():
        copies = fetch([(query_hbm, query_ref)], sems)
        far_copies = fetch([(far_hbm, far_ref)], far_sems)
        mark(live_ref, told_ref, far * blocks, blocks, 0)
        wait(copies)
        wait(far_copies)

        @pl.when(here % 2 == 0)
        def _():
            far_t_ref[...] = far_ref[0:rows, :].astype(jnp.float32).T.astype(jnp.bfloat16)
            attend_all(query_ref, sums_ref, far_t_ref, far_ref.at[pl.ds(rows, rows)], live_ref, 0, blocks)

    @pl.when(farthest >= 0)
    def _():
        mark(live_ref, told_ref, farthest * blocks + blocks - 1, 1, 0)
        for h in range(cols // DH):
            at = pl.ds(h * DH, DH)
            scores = lax.dot_general(
                query_ref[0:BLK, at], tail_ref[0, :, at], NT, preferred_element_type=jnp.float32
            )
            weights = tile(scores, live_ref[0]).astype(jnp.bfloat16)
            sums_ref[0:BLK, at] += jnp.dot(
                weights, tail_ref[1, :, at], preferred_element_type=jnp.float32
            )

    for h in range(cols // DH):
        at = pl.ds(h * DH, DH)
        sums_ref[:, at] = centred(sums_ref[:, at])


def finish_kernel(sums_ref, near_ref, scale_ref, out_ref):
    for h in range(sums_ref.shape[1] // DH):
        at = pl.ds(h * DH, DH)
        part = sums_ref[:, at] + near_ref[:, at].astype(jnp.float32)
        off = centred(part)
        spread_sq = jnp.mean(jnp.square(off), axis=-1, keepdims=True)
        out_ref[:, at] = (off * lax.rsqrt(spread_sq + EPS) * scale_ref[:, at]).astype(jnp.bfloat16)


def mix(total, pieces, w_ref):
    cols = pieces[0].shape[1]
    for m, piece in enumerate(pieces):
        w = w_ref[m * cols : (m + 1) * cols, :]
        total = total + jnp.dot(piece[...], w, preferred_element_type=jnp.float32)
    return total


def near_out_kernel(*refs):
    n = (len(refs) - 7) // 3
    pieces, w_hbm, refs = refs[:n], refs[n : 3 * n], refs[3 * n :]
    history_hbm, out_ref, w_far_ref, w_near_ref, history_ref, sems, w_sems = refs
    cols = out_ref.shape[1]
    rows = w_hbm[0].shape[0]
    at = pl.ds(pl.multiple_of(lax.axis_index("head") * cols, cols), cols)
    copies = fetch([(history_hbm.at[:, at], history_ref)], sems)
    w_copies = fetch(
        [
            (w.at[:, at], (w_near_ref if m < n else w_far_ref).at[pl.ds(m % n * rows, rows)])
            for m, w in enumerate(w_hbm)
        ],
        w_sems,
    )
    wait(copies)
    wait(w_copies)
    out_ref[...] = mix(history_ref[...].astype(jnp.float32), pieces, w_near_ref)


def far_out_kernel(*refs):
    *pieces, w_ref, near_ref, out_ref = refs
    out_ref[...] = mix(near_ref[...], pieces, w_ref).astype(jnp.bfloat16)


def crossed(array, axis, bit):
    return lax.ppermute(array, axis, [(i, i ^ bit) for i in range(lax.axis_size(axis))])


def spread(piece, bit):
    pieces = {0: piece}
    while bit:
        pieces.update({m + bit: crossed(p, "head", bit) for m, p in list(pieces.items())})
        bit //= 2
    return [pieces[m] for m in sorted(pieces)]


def body(history, ln_gain, w_in, out_gain, w_out, block_lists, counts):
    tok_rows, width = history.shape
    blocks = counts.shape[0]
    cols = w_in.shape[2]
    n_seq, n_head = lax.axis_size("seq"), lax.axis_size("head")
    assert 2 * (PLANES + 1) * blocks - (WIN - 1) == blocks - 1
    barrier = lax.optimization_barrier

    shape = lambda like, *dims: jax.ShapeDtypeStruct(dims, like)
    bf16, f32 = jnp.bfloat16, jnp.float32
    wide = pl.BlockSpec(memory_space=pltpu.VMEM)
    flat = pl.BlockSpec(memory_space=pltpu.SMEM)
    far_off = pl.BlockSpec(memory_space=pltpu.HBM)
    n_live = 2 * blocks * 8
    upright, lying = (tok_rows, cols), (cols, tok_rows)
    sems = lambda n: pltpu.SemaphoreType.DMA((n,))
    live = pltpu.SMEM((n_live,), f32)

    share_rows = tok_rows // n_head
    steps = share_rows // 48
    share = pl.pallas_call(
        norm_kernel,
        in_specs=[far_off] * 2,
        out_specs=wide,
        out_shape=shape(bf16, share_rows, width),
        scratch_shapes=[
            pltpu.VMEM((share_rows, width), bf16),
            pltpu.VMEM((width,), bf16),
            sems(steps + 1),
        ],
        cost_estimate=cost(2),
        compiler_params=params(60),
    )(history, ln_gain)
    gain, block_lists, counts, w_out, share = barrier((ln_gain, block_lists, counts, w_out, share))
    told = jnp.concatenate([block_lists, counts[:, None]], axis=1)
    upward = [(i, i + 2) for i in range(n_seq - 2)]
    share_1 = lax.ppermute(share, "seq", upward)

    gate, both, query, keys_t, tail = pl.pallas_call(
        own_kernel,
        in_specs=[far_off, far_off, wide],
        out_specs=[far_off] * 5,
        out_shape=[
            shape(bf16, *upright), shape(bf16, 2 * tok_rows, cols), shape(bf16, *upright),
            shape(bf16, *lying), shape(bf16, 2, BLK, cols),
        ],
        scratch_shapes=[
            pltpu.VMEM((tok_rows, width), bf16), pltpu.VMEM((width,), bf16), pltpu.VMEM(upright, bf16),
            pltpu.VMEM((2 * tok_rows, cols), bf16), pltpu.VMEM(upright, bf16), pltpu.VMEM(lying, bf16),
            sems(1 + tok_rows // (2 * BLK)), sems(6),
        ],
        compiler_params=params(60),
        cost_estimate=cost(4),
    )(history, gain, w_in)

    w_cross = crossed(w_out, "head", n_head // 2)
    query_x = crossed(query, "seq", 1)
    share_1, query, w_cross = barrier((share_1, query, w_cross))
    share_2 = lax.ppermute(share_1, "seq", upward[2:])
    cross_1 = crossed(share_1, "head", n_head // 2)
    told_x = crossed(told, "seq", 1)
    told, told_x, tail, w_out, w_cross = barrier((told, told_x, tail, w_out, w_cross))
    w_all = spread(w_out, n_head // 4) + spread(w_cross, n_head // 4)
    tail = lax.ppermute(tail, "seq", [(i, i + FAR + 1) for i in range(n_seq - FAR - 1)])
    own_sums = pl.pallas_call(
        own_attend_kernel,
        in_specs=[flat] + [far_off] * 3,
        out_specs=far_off,
        out_shape=shape(f32, *upright),
        scratch_shapes=[pltpu.VMEM(upright, bf16), pltpu.VMEM(lying, bf16), pltpu.VMEM(upright, bf16)]
        + [pltpu.VMEM(upright, f32), live, sems(3)],
        compiler_params=params(),
        cost_estimate=cost(4),
    )(told, query, keys_t, both)
    share_2, cross_1, own_sums, query_x = barrier((share_2, cross_1, own_sums, query_x))
    chunk_1 = spread(share_1, n_head // 4) + spread(cross_1, n_head // 4)
    cross_2 = crossed(share_2, "head", n_head // 2)
    near_2 = spread(share_2, n_head // 4)

    both, query_x, share_2 = barrier((both, query_x, share_2))
    far = lax.ppermute(both, "seq", [(i, i + FAR) for i in range(1, n_seq - FAR, 2)])

    sums, sums_x = pl.pallas_call(
        make_chunk_kernel(1, n_head),
        in_specs=[flat] * 2 + [wide] * (n_head + 1) + [far_off] * 5,
        out_specs=[far_off] * 2,
        out_shape=[shape(f32, *upright)] * 2,
        scratch_shapes=[
            pltpu.VMEM(dims, kind)
            for dims, kind in (
                (upright, bf16), (upright, bf16), (lying, bf16), (upright, bf16), (upright, f32),
                (upright, f32), (upright, f32), (lying, bf16), (upright, bf16),
            )
        ]
        + [live, sems(5), sems(2)],
        compiler_params=params(16),
        cost_estimate=cost(0.05),
    )(told, told_x, *chunk_1, w_in, query, query_x, keys_t, both, own_sums)

    cross_2, sums_x, w_all = barrier((cross_2, sums_x, tuple(w_all)))
    send, keys_t, values = pl.pallas_call(
        make_last_kernel(PLANES, n_head),
        in_specs=[flat] + [wide] * (n_head + 1) + [far_off] * 2,
        out_specs=[wide] * 3,
        out_shape=[shape(bf16, *upright), shape(bf16, *lying), shape(bf16, *upright)],
        scratch_shapes=[
            pltpu.VMEM(upright, bf16), pltpu.VMEM(upright, f32), pltpu.VMEM(upright, f32), live, sems(2)
        ],
        compiler_params=params(),
        cost_estimate=cost(0.05),
    )(told_x, *near_2, *spread(cross_2, n_head // 4), w_in, query_x, sums_x)
    near = crossed(send, "seq", 1)
    mine, scale = pl.pallas_call(
        make_own_last_kernel(PLANES),
        in_specs=[flat, far_off, wide, wide, far_off, far_off, wide],
        out_specs=[wide] * 2,
        out_shape=[shape(f32, *upright)] * 2,
        scratch_shapes=[pltpu.VMEM(upright, bf16)] * 2 + [live, sems(3)],
        compiler_params=params(),
        cost_estimate=cost(0.05),
    )(told, query, keys_t, values, sums, gate, out_gain)
    far, tail, mine = barrier((far, tail, mine))
    mine = pl.pallas_call(
        far_kernel,
        in_specs=[flat, far_off, wide, far_off, wide],
        out_specs=wide,
        out_shape=shape(f32, *upright),
        input_output_aliases={4: 0},
        scratch_shapes=[
            pltpu.VMEM(upright, bf16), pltpu.VMEM((2 * tok_rows, cols), bf16), pltpu.VMEM(lying, bf16), live,
            sems(1), sems(1),
        ],
        compiler_params=params(),
        cost_estimate=cost(9),
    )(told, query, tail, far, mine)
    near, mine = barrier((near, mine))
    gated = pl.pallas_call(
        finish_kernel,
        in_specs=[wide] * 3,
        out_specs=wide,
        out_shape=shape(bf16, *upright),
        compiler_params=params(),
        cost_estimate=cost(1),
    )(mine, near, scale)

    out_cols = width // n_head
    cross_gated = crossed(gated, "head", n_head // 2)
    near_gated = spread(gated, n_head // 4)
    half = n_head // 2
    mixed, w_far = pl.pallas_call(
        near_out_kernel,
        in_specs=[wide] * half + [far_off] * (n_head + 1),
        out_specs=[wide] * 2,
        out_shape=[shape(f32, tok_rows, out_cols), shape(bf16, half * cols, out_cols)],
        scratch_shapes=[
            pltpu.VMEM((half * cols, out_cols), bf16), pltpu.VMEM((tok_rows, out_cols), bf16),
            sems(1), sems(n_head),
        ],
        compiler_params=params(),
        cost_estimate=cost(2),
    )(*near_gated, *w_all, history)
    cross_gated, mixed = barrier((cross_gated, mixed))
    return pl.pallas_call(
        far_out_kernel,
        in_specs=[wide] * (half + 2),
        out_specs=wide,
        out_shape=shape(bf16, tok_rows, out_cols),
        compiler_params=params(),
        cost_estimate=cost(2),
    )(*spread(cross_gated, n_head // 4), w_far, mixed)


def solution(mesh):
    placed = (
        P("seq", None),
        P(),
        P(None, None, "head"),
        P("head"),
        P("head", None),
        P("seq", None),
        P("seq"),
    )
    return jax.shard_map(
        body, mesh=mesh, in_specs=placed, out_specs=P("seq", "head"), check_vma=False
    )
```
